32 devices in a mesh: wide: 8 (over y, x, core), narrow: 4 (over z).
Axes of the slice: x: 2, y: 2, z: 4, core: 2. Of those that a mesh axis runs over, the one named last changes fastest.
Arguments:
- tokens: bfloat16 [2, 6304, 768], P(None, ('wide', 'narrow')), may hold values from -6 to 6
- page_mask: int32 [2, 6304], P(None, ('wide', 'narrow')), may hold values 0 or 1
- buckets: int32 [197, 197], replicated, may hold values from 0 to 731
- mask_token: float32 [768], replicated, may hold values from -6 to 6
- first_gain: float32 [768], replicated, may hold values from 0.5 to 1.5
- first_shift: float32 [768], replicated, may hold values from -3 to 3
- qkv_weight: bfloat16 [768, 3, 768], P(None, None, 'narrow'), may hold values from -0.21875 to 0.21875
- query_bias: float32 [768], P('narrow'), may hold values from -3 to 3
- value_bias: float32 [768], P('narrow'), may hold values from -3 to 3
- position_bias: float32 [12, 732], P('narrow'), may hold values from -4 to 4
- out_weight: bfloat16 [768, 768], P('narrow'), may hold values from -0.875 to 0.875
- out_bias: float32 [768], replicated, may hold values from -3 to 3
- attn_scale: float32 [768], replicated, may hold values from 0.5 to 2
- second_gain: float32 [768], replicated, may hold values from 0.5 to 1.5
- second_shift: float32 [768], replicated, may hold values from -3 to 3
- in_weight: bfloat16 [768, 3072], P(None, 'narrow'), may hold values from -0.21875 to 0.21875
- in_bias: float32 [3072], P('narrow'), may hold values from -3 to 3
- down_weight: bfloat16 [3072, 768], P('narrow'), may hold values from -0.109375 to 0.109375
- down_bias: float32 [768], replicated, may hold values from -3 to 3
- mlp_scale: float32 [768], replicated, may hold values from 0.5 to 2
- out_grad: bfloat16 [2, 6304, 768], P(None, ('wide', 'narrow')), may hold values from -6 to 6
Outputs:
- layer_out: bfloat16 [2, 6304, 768], P(None, ('wide', 'narrow'))
- tokens_grad: bfloat16 [2, 6304, 768], P(None, ('wide', 'narrow'))
- mask_token_grad: float32 [768], replicated
- first_gain_grad: float32 [768], replicated
- first_shift_grad: float32 [768], replicated
- qkv_weight_grad: float32 [768, 3, 768], P(None, None, 'narrow')
- query_bias_grad: float32 [768], P('narrow')
- value_bias_grad: float32 [768], P('narrow')
- position_bias_grad: float32 [12, 732], P('narrow')
- out_weight_grad: float32 [768, 768], P('narrow')
- out_bias_grad: float32 [768], replicated
- attn_scale_grad: float32 [768], replicated
- second_gain_grad: float32 [768], replicated
- second_shift_grad: float32 [768], replicated
- in_weight_grad: float32 [768, 3072], P(None, 'narrow')
- in_bias_grad: float32 [3072], P('narrow')
- down_weight_grad: float32 [3072, 768], P('narrow')
- down_bias_grad: float32 [768], replicated
- mlp_scale_grad: float32 [768], replicated
The draws below stay inside these ranges and needn't reach their ends.
All inputs are finite; a program needn't handle non-finite values. No bound on the sum of `page_mask` on one device may be relied on, other than what follows from the above.
Results may differ from the reference program's by a relative error of at most 0.015.
Values may be sent and summed in bfloat16 or wider, within the bound.
No kernel may reach another device: no remote copies, remote signals or barrier semaphores. Data moves between devices by JAX's collectives and lax.ppermute only.
A program may use at most 128 MiB of HBM per device.

```python
import math
import jax
import jax.numpy as jnp
from jax import lax

D = 768
HEADS = 12
FF = 3072
SEQ = 197
BUCKETS = 732
MICRO = 2
PAGES_MB = 4
MB_ROWS = 6304
N_WIDE = 8


def with_ends(values, stream_key, smallest, high):
    dims = values.shape
    place = [jax.random.randint(jax.random.fold_in(stream_key, axis), (), 0, dims[axis]) for axis in range(len(dims))]
    values = values.at[tuple(place)].set(smallest)
    longest = dims.index(max(dims))
    place[longest] = (place[longest] + 1) % dims[longest]
    return values.at[tuple(place)].set(high)


def block_scale(key, extent, split, least, largest):
    level = 1.0
    for dim, shards_of in split:
        draws = jax.random.uniform(jax.random.fold_in(jax.random.fold_in(key, 6), dim), (shards_of,), jnp.float32, least / len(split), largest / len(split))
        level = level * jnp.repeat(jnp.exp(draws), extent[dim] // shards_of).reshape((-1,) + (1,) * (len(extent) - 1 - dim))
    return level


def normal_values(own_key, shape, deviation, reach, shards=(), held_as=jnp.bfloat16):
    level = block_scale(own_key, shape, shards, -0.22, 0.18) if shards else 1.0
    entries = jax.random.normal(own_key, shape, jnp.float32) * deviation * level
    return jnp.minimum(jnp.maximum(entries, -reach), reach).astype(held_as)


def setup_inputs(seed: int = 0) -> dict:
    keys = jax.random.split(jax.random.key(seed), 22)
    return {
        "tokens": normal_values(keys[0], (MICRO, MB_ROWS, D), 1.0, 6.0, ((1, 32),)),
        "page_mask": with_ends((jax.random.randint(keys[1], (MICRO, MB_ROWS), 0, 5) < 2).astype(jnp.int32), jax.random.fold_in(keys[1], 1), 0, 1),
        "buckets": with_ends(jax.random.randint(keys[2], (SEQ, SEQ), 0, BUCKETS), jax.random.fold_in(keys[2], 1), 0, BUCKETS - 1).astype(jnp.int32),
        "mask_token": normal_values(keys[3], (D,), 1.0, 6.0, (), jnp.float32),
        "first_gain": jnp.clip(jax.random.uniform(keys[4], (D,), jnp.float32, 0.5, 1.5), 0.5, 1.5),
        "first_shift": normal_values(keys[5], (D,), 0.5, 3.0, (), jnp.float32),
        "qkv_weight": normal_values(keys[6], (D, 3, D), D ** -0.5, 0.21875, ((2, 4),)),
        "query_bias": normal_values(keys[7], (D,), 0.5, 3.0, ((0, 4),), jnp.float32),
        "value_bias": normal_values(keys[8], (D,), 0.5, 3.0, ((0, 4),), jnp.float32),
        "position_bias": normal_values(keys[9], (HEADS, BUCKETS), 1.0, 4.0, ((0, 4),), jnp.float32),
        "out_weight": normal_values(keys[10], (D, D), (D // 16) ** -0.5, 0.875, ((0, 4),)),
        "out_bias": normal_values(keys[11], (D,), 0.5, 3.0, (), jnp.float32),
        "attn_scale": jnp.clip(jnp.exp(jax.random.uniform(keys[12], (D,), jnp.float32, math.log(0.5), math.log(2.0))), 0.5, 2.0),
        "second_gain": jnp.clip(jax.random.uniform(keys[13], (D,), jnp.float32, 0.5, 1.5), 0.5, 1.5),
        "second_shift": normal_values(keys[14], (D,), 0.5, 3.0, (), jnp.float32),
        "in_weight": normal_values(keys[15], (D, FF), D ** -0.5, 0.21875, ((1, 4),)),
        "in_bias": normal_values(keys[16], (FF,), 0.5, 3.0, ((0, 4),), jnp.float32),
        "down_weight": normal_values(keys[17], (FF, D), FF ** -0.5, 0.109375, ((0, 4),)),
        "down_bias": normal_values(keys[18], (D,), 0.5, 3.0, (), jnp.float32),
        "mlp_scale": jnp.clip(jnp.exp(jax.random.uniform(keys[19], (D,), jnp.float32, math.log(0.5), math.log(2.0))), 0.5, 2.0),
        "out_grad": normal_values(keys[20], (MICRO, MB_ROWS, D), 1.0, 6.0, ((1, 32),)),
    }


@jax.custom_vjp
def low(v):
    return lax.optimization_barrier(v.astype(jnp.bfloat16)).astype(jnp.float32)

@jax.custom_vjp
def low_back(v):
    return v

def low_keep(v):
    return (low(v), None)

def low_pass(kept, grad):
    return (grad,)

def back_keep(v):
    return (v, None)

def back_low(kept, grad):
    return (low(grad),)
low.defvjp(low_keep, low_pass)
low_back.defvjp(back_keep, back_low)
EPSILON = 1e-06

def precise_dot(left, right):
    return jnp.dot(left, right, precision=lax.Precision.HIGHEST)

def layer_norm(values, gain, shift):
    center = values - lax.optimization_barrier(jnp.mean(values, axis=-1, keepdims=True))
    spread = lax.optimization_barrier(jnp.mean(center * center, axis=-1, keepdims=True))
    return center * lax.rsqrt(spread + EPSILON) * gain + shift

def one_group(params, rows_in, masked_rows, buckets):
    mask_token, first_gain, first_shift, qkv_weight, query_bias, value_bias, position_bias, out_weight, out_bias, attn_scale, second_gain, second_shift, in_weight, in_bias, down_weight, down_bias, mlp_scale = params
    page_count = rows_in.shape[0] // SEQ
    head_size = D // HEADS
    head_shape = (page_count, SEQ, HEADS, head_size)
    masked_in = jnp.where(masked_rows[:, None] > 0, mask_token[None, :], rows_in)
    first_norm = low(layer_norm(masked_in, first_gain, first_shift))
    queries = low(low_back(precise_dot(first_norm, qkv_weight[:, 0, :]) + query_bias))
    keys_all = low(low_back(precise_dot(first_norm, qkv_weight[:, 1, :])))
    values_all = low(low_back(precise_dot(first_norm, qkv_weight[:, 2, :]) + value_bias))
    scores = jnp.einsum('pqhe,pkhe->phqk', queries.reshape(head_shape), keys_all.reshape(head_shape), precision=lax.Precision.HIGHEST) * head_size ** (-0.5) + position_bias[:, buckets][None]
    scores = low_back(scores)
    probs = low(jax.nn.softmax(scores, axis=-1))
    mixed_rows = jnp.einsum('phqk,pkhe->pqhe', probs, values_all.reshape(head_shape), precision=lax.Precision.HIGHEST).reshape(page_count * SEQ, D)
    mixed_rows = low(low_back(mixed_rows))
    attn_out = low_back(precise_dot(mixed_rows, out_weight)) + out_bias
    middle = masked_in + attn_scale * attn_out
    second_norm = low(layer_norm(middle, second_gain, second_shift))
    hidden_pre = low_back(precise_dot(second_norm, in_weight) + in_bias)
    hidden = low(jax.nn.gelu(hidden_pre, approximate=False))
    mlp_out = low_back(precise_dot(hidden, down_weight)) + down_bias
    return middle + mlp_scale * mlp_out

def reference(tokens, page_mask, buckets, mask_token, first_gain, first_shift, qkv_weight, query_bias, value_bias, position_bias, out_weight, out_bias, attn_scale, second_gain, second_shift, in_weight, in_bias, down_weight, down_bias, mlp_scale, out_grad):
    groups = MICRO * N_WIDE
    group_rows = PAGES_MB * SEQ
    positions = jnp.arange(group_rows, dtype=jnp.int32) % SEQ
    masked_rows = (page_mask.reshape(groups, group_rows) * (positions != 0).astype(jnp.int32)[None, :]).astype(jnp.float32)
    rows_in = tokens.astype(jnp.float32).reshape(groups, group_rows, D)
    params = (mask_token, first_gain, first_shift, qkv_weight.astype(jnp.float32), query_bias, value_bias, position_bias, out_weight.astype(jnp.float32), out_bias, attn_scale, second_gain, second_shift, in_weight.astype(jnp.float32), in_bias, down_weight.astype(jnp.float32), down_bias, mlp_scale)

    def forward(params, rows_in):

        def one_item(group_item):
            return one_group(params, group_item[0], group_item[1], buckets)
        return lax.map(jax.checkpoint(one_item), (rows_in, masked_rows))
    layer_out, pull_back = jax.vjp(forward, params, rows_in)
    param_grads, input_grad = pull_back(out_grad.astype(jnp.float32).reshape(groups, group_rows, D))
    mask_token_grad, first_gain_grad, first_shift_grad, qkv_weight_grad, query_bias_grad, value_bias_grad, position_bias_grad, out_weight_grad, out_bias_grad, attn_scale_grad, second_gain_grad, second_shift_grad, in_weight_grad, in_bias_grad, down_weight_grad, down_bias_grad, mlp_scale_grad = param_grads
    whole_shape = (MICRO, N_WIDE * group_rows, D)
    return (layer_out.reshape(whole_shape).astype(jnp.bfloat16), input_grad.reshape(whole_shape).astype(jnp.bfloat16), mask_token_grad, first_gain_grad, first_shift_grad, qkv_weight_grad, query_bias_grad, value_bias_grad, position_bias_grad, out_weight_grad, out_bias_grad, attn_scale_grad, second_gain_grad, second_shift_grad, in_weight_grad, in_bias_grad, down_weight_grad, down_bias_grad, mlp_scale_grad)
```

```python
import functools

import jax
import jax.numpy as jnp
from jax import lax
from jax.experimental import pallas as pl
from jax.experimental.pallas import tpu as pltpu
from jax.sharding import PartitionSpec as P


SEQ = 197
PAD = 208
LANES = 256
EPSILON = 1e-06
ROOT_HALF = 0.7071067811865476
DENSITY = 0.3989422804014327
CORE, SIDE, DEEP = 1, 2, 4
PIECES = 8
LOW = 32
NEGATIVE = -1e30
VMEM_LIMIT = 56 * 1024 * 1024
F32 = jnp.float32
BF16 = jnp.bfloat16

NN = (((1,), (0,)), ((), ()))
NT = (((1,), (1,)), ((), ()))
TN = (((0,), (0,)), ((), ()))


def mul(left, right, dims=NN):
    return lax.dot_general(left, right, dims, preferred_element_type=F32)


def vmem():
    return pl.BlockSpec(memory_space=pltpu.VMEM)


def anywhere():
    return pl.BlockSpec(memory_space=pl.ANY)


def scalars():
    return pl.BlockSpec(memory_space=pltpu.SMEM)


def call(kernel, name, outs, in_specs, out_specs=None, scratch=(), flops=0, nbytes=0):
    if out_specs is None:
        out_specs = [vmem()] * len(outs)
    return pl.pallas_call(
        kernel,
        out_shape=[jax.ShapeDtypeStruct(shape, dtype) for shape, dtype in outs],
        in_specs=in_specs,
        out_specs=out_specs,
        scratch_shapes=list(scratch),
        compiler_params=pltpu.CompilerParams(vmem_limit_bytes=VMEM_LIMIT),
        cost_estimate=pl.CostEstimate(flops=flops, bytes_accessed=nbytes, transcendentals=0),
        name=name,
    )


def norm_parts(values):
    center = values - jnp.mean(values, axis=-1, keepdims=True)
    spread = jnp.mean(center * center, axis=-1, keepdims=True)
    inverse = lax.rsqrt(spread + EPSILON)
    return center * inverse, inverse


def norm_back(grad, normed, inverse, gain):
    scaled = grad * gain
    inner = jnp.mean(scaled, axis=-1, keepdims=True)
    cross = jnp.mean(scaled * normed, axis=-1, keepdims=True)
    return inverse * (scaled - inner - normed * cross)


def col(values):
    return jnp.sum(values, axis=0, keepdims=True)


def first_kernel(tok_ref, mask_ref, vec_ref, out_ref):
    width = tok_ref.shape[1]
    masked = jnp.where(mask_ref[...] > 0.0, vec_ref[0:1, :], tok_ref[...].astype(F32))
    normed, _ = norm_parts(masked)
    out = normed * vec_ref[1:2, :] + vec_ref[2:3, :]
    rows = lax.broadcasted_iota(jnp.int32, (tok_ref.shape[0], 1), 0)
    real = lax.rem(rows, PAD) < SEQ
    out_ref[...] = jnp.where(real, out, 0.0).astype(BF16)


def bias_kernel(buckets_ref, table_ref, out_ref):
    heads, parts, _ = table_ref.shape
    for half in range(2):
        lanes = pl.ds(half * 128, 128)
        index = buckets_ref[:, lanes]
        low = lax.bitwise_and(index, 127)
        high = lax.shift_right_logical(index, 7)
        column = lax.broadcasted_iota(jnp.int32, index.shape, 1) + half * 128
        for head in range(heads):
            total = jnp.full(index.shape, NEGATIVE, F32)
            for part in range(parts):
                row = jnp.broadcast_to(table_ref[head, part : part + 1, :], index.shape)
                found = jnp.take_along_axis(row, low, axis=1, mode="promise_in_bounds")
                total = jnp.where(high == part, found, total)
            out_ref[head, :, lanes] = jnp.where(column < SEQ, total, NEGATIVE)


def copies_in(w_ref, pieces, slot, target, sem):
    rows = target.shape[0] // PIECES
    half = rows // 2
    place = w_ref[0]
    made = []
    for piece, (first, count, ref) in zip(
        (0, 1, 2, 3, 4, 5, 6, 6, 7, 7),
        [(0, rows, r) for r in pieces[:6]]
        + [(0, half, pieces[6]), (half, half, pieces[7]), (0, half, pieces[8]), (half, half, pieces[9])],
        strict=True,
    ):
        start = pl.multiple_of(lax.bitwise_xor(place, piece) * rows, rows) + first
        made.append(
            pltpu.make_async_copy(
                ref.at[slot], target.at[pl.ds(pl.multiple_of(start, 16), count), :], sem
            )
        )
    return made


def load_weights(w_ref, refs, slot, target, sem):
    if len(refs) == 1:
        return [pltpu.make_async_copy(refs[0], target, sem)]
    return copies_in(w_ref, refs, slot, target, sem)


def go(copies):
    for c in copies:
        c.start()


def finish(copies):
    for c in copies:
        c.wait()


def attend_kernel(n_weights, slot, first, *refs):
    w_ref = refs[0]
    weights = refs[1 : 1 + n_weights]
    rest = refs[1 + n_weights :]
    x_ref, shift_ref, bias_ref = rest[:3]
    rest = rest[3:]
    if not first:
        acc_in = rest[0]
        rest = rest[1:]
    acc_ref, qkv_ref, probs_ref, mixed_ref, mat, sem = rest
    copies = load_weights(w_ref, weights, slot, mat, sem)
    go(copies)
    finish(copies)
    width = mat.shape[0]
    local = width // 4
    heads = bias_ref.shape[0]
    size = local // heads
    qkv = mul(x_ref[...], mat[: 3 * local, :], NT) + shift_ref[...]
    queries = (qkv[:, :local].astype(BF16).astype(F32) * size ** (-0.5)).astype(BF16)
    keys = qkv[:, local : 2 * local].astype(BF16)
    values = qkv[:, 2 * local :].astype(BF16)
    qkv_ref[0] = queries
    qkv_ref[1] = keys
    qkv_ref[2] = values
    lane = lax.broadcasted_iota(jnp.int32, (PAD, local), 1)
    pages = x_ref.shape[0] // PAD
    zero = jnp.zeros((PAD, local), BF16)
    for page in range(pages):
        rows = slice(page * PAD, (page + 1) * PAD)
        q, k, v = queries[rows], keys[rows], values[rows]
        mixed = jnp.zeros((PAD, local), F32)
        for head in range(heads):
            own = (lane >= head * size) & (lane < (head + 1) * size)
            scores = mul(jnp.where(own, q, zero), k, NT) + bias_ref[head][:, :PAD]
            top = jnp.max(scores, axis=1, keepdims=True)
            power = jnp.exp(scores - top)
            total = jnp.sum(power, axis=1, keepdims=True)
            probs = (power * (1.0 / total)).astype(BF16)
            probs_ref[page * heads + head] = probs
            mixed = mixed + mul(probs, jnp.where(own, v, zero))
        mixed_ref[rows, :] = mixed.astype(BF16)
    out = mul(mixed_ref[...], mat[3 * local :, :])
    acc_ref[...] = out if first else acc_in[...] + out


def middle_kernel(acc_ref, tok_ref, mask_ref, grad_ref, vec_ref, mid_ref, x_ref, mg_ref):
    masked = jnp.where(mask_ref[...] > 0.0, vec_ref[0:1, :], tok_ref[...].astype(F32))
    middle = masked + vec_ref[2:3, :] * (acc_ref[...] + vec_ref[1:2, :])
    mid_ref[...] = middle
    normed, _ = norm_parts(middle)
    x_ref[...] = (normed * vec_ref[3:4, :] + vec_ref[4:5, :]).astype(BF16)
    mg_ref[...] = (grad_ref[...].astype(F32) * vec_ref[5:6, :]).astype(BF16)


def copies_out(w_ref, mats, keep, send, sem):
    place = w_ref[0]
    made = []
    for number, mat in enumerate(mats):
        rows = mat.shape[0] // PIECES
        for piece in range(PIECES):
            start = pl.multiple_of(lax.bitwise_xor(place, piece) * rows, rows)
            target = send if piece & CORE else keep
            made.append(
                pltpu.make_async_copy(
                    mat.at[pl.ds(start, rows), :], target.at[piece >> 1, number], sem
                )
            )
    return made


def mlp_kernel(n_weights, slot, first, *refs):
    w_ref = refs[0]
    in_refs = refs[1 : 1 + n_weights]
    down_refs = refs[1 + n_weights : 1 + 2 * n_weights]
    rest = refs[1 + 2 * n_weights :]
    x_ref, mg_ref, shift_ref = rest[:3]
    rest = rest[3:]
    if not first:
        out_in, grad_in = rest[:2]
        rest = rest[2:]
    out_ref, grad_ref, col_ref, keep, send, in_mat, down_mat, in_grad, down_grad, sem, osem = rest
    copies = load_weights(w_ref, in_refs, slot, in_mat, sem.at[0]) + load_weights(
        w_ref, down_refs, slot, down_mat, sem.at[1]
    )
    go(copies)
    finish(copies)
    width = in_mat.shape[0]
    x = x_ref[...]
    mg = mg_ref[...]
    out = None
    back = None
    for start in range(0, width, 256):
        units = slice(start, start + 256)
        weight_in = in_mat[:, units]
        weight_down = down_mat[units, :]
        pre = mul(x, weight_in) + shift_ref[:, units]
        phi = 0.5 * (1.0 + lax.erf(pre * ROOT_HALF))
        hidden = (pre * phi).astype(BF16)
        slope = phi + pre * (DENSITY * jnp.exp(-0.5 * pre * pre))
        part = mul(hidden, weight_down)
        out = part if out is None else out + part
        hidden_grad = mul(mg, weight_down, NT)
        pre_grad = hidden_grad * slope
        low = pre_grad.astype(BF16)
        col_ref[:, units] = col(low.astype(F32))
        part = mul(low, weight_in, NT)
        back = part if back is None else back + part
        down_grad[units, :] = mul(hidden, mg, TN).astype(BF16)
        in_grad[:, units] = mul(x, low, TN).astype(BF16)
    out_ref[...] = out if first else out_in[...] + out
    grad_ref[...] = back if first else grad_in[...] + back
    copies = copies_out(w_ref, [in_grad, down_grad], keep, send, osem)
    go(copies)
    finish(copies)


def turn_kernel(mid_ref, out_ref, back_ref, grad_ref, acc_ref, vec_ref, layer_ref, mgrad_ref, ag_ref, sums_ref):
    middle = mid_ref[...]
    grad = grad_ref[...].astype(F32)
    mlp_out = out_ref[...] + vec_ref[1:2, :]
    layer_ref[...] = (middle + vec_ref[2:3, :] * mlp_out).astype(BF16)
    normed, inverse = norm_parts(middle)
    second = back_ref[...]
    middle_grad = grad + norm_back(second, normed, inverse, vec_ref[0:1, :])
    mgrad_ref[...] = middle_grad
    scaled = middle_grad * vec_ref[3:4, :]
    ag_ref[...] = scaled.astype(BF16)
    sums_ref[0:1, :] = col(scaled)
    sums_ref[1:2, :] = col(middle_grad * (acc_ref[...] + vec_ref[4:5, :]))
    sums_ref[2:3, :] = col(second * normed)
    sums_ref[3:4, :] = col(second)
    sums_ref[4:5, :] = col(grad * vec_ref[2:3, :])
    sums_ref[5:6, :] = col(grad * mlp_out)
    sums_ref[6:8, :] = jnp.zeros_like(sums_ref[6:8, :])


def attend_back_kernel(n_weights, slot, first, *refs):
    w_ref = refs[0]
    weights = refs[1 : 1 + n_weights]
    rest = refs[1 + n_weights :]
    x_ref, ag_ref, qkv_ref, probs_ref, mixed_ref = rest[:5]
    rest = rest[5:]
    if not first:
        grad_in = rest[0]
        rest = rest[1:]
    grad_ref, col_ref, grid_ref, keep, send, mat, mat_grad, dqkv, sem, osem = rest
    copies = load_weights(w_ref, weights, slot, mat, sem)
    go(copies)
    finish(copies)
    width = mat.shape[0]
    local = width // 4
    heads = grid_ref.shape[0]
    size = local // heads
    ag = ag_ref[...]
    mixed_grad = mul(ag, mat[3 * local :, :], NT).astype(BF16)
    mat_grad[3 * local :, :] = mul(mixed_ref[...], ag, TN).astype(BF16)
    lane = lax.broadcasted_iota(jnp.int32, (PAD, local), 1)
    pages = x_ref.shape[0] // PAD
    zero = jnp.zeros((PAD, local), BF16)
    for page in range(pages):
        rows = slice(page * PAD, (page + 1) * PAD)
        q, v, dm = qkv_ref[0, rows, :], qkv_ref[2, rows, :], mixed_grad[rows]
        k = (qkv_ref[1, rows, :].astype(F32) * size ** (-0.5)).astype(BF16)
        dq = jnp.zeros((PAD, local), F32)
        dk = jnp.zeros((PAD, local), F32)
        dv = jnp.zeros((PAD, local), F32)
        for head in range(heads):
            own = (lane >= head * size) & (lane < (head + 1) * size)
            dmh = jnp.where(own, dm, zero)
            probs_low = probs_ref[page * heads + head]
            probs = probs_low.astype(F32)
            weighed = probs * mul(dmh, v, NT)
            score = weighed - probs * jnp.sum(weighed, axis=1, keepdims=True)
            low = score.astype(BF16)
            if page == 0:
                grid_ref[head] = low.astype(F32)
            else:
                grid_ref[head] = grid_ref[head] + low.astype(F32)
            dq = dq + mul(low, jnp.where(own, k, zero))
            dk = dk + mul(low, jnp.where(own, q, zero), TN)
            dv = dv + mul(probs_low, dmh, TN)
        dqkv[rows, :] = jnp.concatenate([dq, dk, dv], axis=1).astype(BF16)
    grads = dqkv[...]
    col_ref[...] = col(grads.astype(F32))
    mat_grad[: 3 * local, :] = mul(grads, x_ref[...], TN).astype(BF16)
    back = mul(grads, mat[: 3 * local, :])
    grad_ref[...] = back if first else grad_in[...] + back
    copies = copies_out(w_ref, [mat_grad], keep, send, osem)
    go(copies)
    finish(copies)


def last_kernel(tok_ref, mask_ref, mgrad_ref, first_ref, vec_ref, grad_ref, sums_ref):
    mask = mask_ref[...] > 0.0
    masked = jnp.where(mask, vec_ref[0:1, :], tok_ref[...].astype(F32))
    normed, inverse = norm_parts(masked)
    first = first_ref[...]
    in_grad = mgrad_ref[...] + norm_back(first, normed, inverse, vec_ref[1:2, :])
    grad_ref[...] = jnp.where(mask, 0.0, in_grad).astype(BF16)
    sums_ref[0:1, :] = col(jnp.where(mask, in_grad, 0.0))
    sums_ref[1:2, :] = col(first * normed)
    sums_ref[2:3, :] = col(first)
    sums_ref[3:8, :] = jnp.zeros_like(sums_ref[3:8, :])


def table_kernel(grid_count, *refs):
    buckets_ref = refs[0]
    grids = refs[1 : 1 + grid_count]
    out_ref = refs[1 + grid_count]
    heads = grids[0].shape[0]
    highs = out_ref.shape[0] // (grid_count * heads)
    out_ref[...] = jnp.zeros_like(out_ref)

    def step(block, _):
        base = pl.multiple_of(block * 8, 8)
        index = buckets_ref[pl.ds(base, 8), :][:, :PAD]
        loads = [[g[h, pl.ds(base, 8), :] for h in range(heads)] for g in grids]
        total = None
        for row in range(8):
            one = index[row : row + 1]
            low = lax.bitwise_and(one, LOW - 1)
            high = lax.shift_right_logical(one, 5)
            right = (
                jnp.broadcast_to(low, (LOW, PAD)) == lax.broadcasted_iota(jnp.int32, (LOW, PAD), 0)
            ).astype(F32).astype(BF16)
            match = jnp.broadcast_to(high, (highs, PAD)) == lax.broadcasted_iota(
                jnp.int32, (highs, PAD), 0
            )
            left = jnp.concatenate(
                [
                    jnp.where(match, jnp.broadcast_to(loads[g][h][row : row + 1], (highs, PAD)), 0.0)
                    for g in range(grid_count)
                    for h in range(heads)
                ],
                axis=0,
            ).astype(BF16)
            part = mul(left, right, NT)
            total = part if total is None else total + part
        out_ref[...] += total
        return 0

    lax.fori_loop(0, PAD // 8, step, 0)


def assemble(w_ref, pieces, number, place_in):
    for piece, ref in enumerate(pieces):
        rows = place_in.shape[0] // PIECES
        start = pl.multiple_of(lax.bitwise_xor(w_ref[0], piece) * rows, rows)
        place_in[pl.ds(start, rows), :] = ref[number].astype(F32)


def mlp_final_kernel(w_ref, *refs):
    pieces, (in_ref, down_ref) = refs[:PIECES], refs[PIECES:]
    assemble(w_ref, pieces, 0, in_ref)
    assemble(w_ref, pieces, 1, down_ref)


def attend_final_kernel(w_ref, *refs):
    pieces, (qkv_ref, out_ref, whole) = refs[:PIECES], refs[PIECES:]
    assemble(w_ref, pieces, 0, whole)
    cut = qkv_ref.shape[0]
    qkv_ref[...] = whole[:cut, :]
    out_ref[...] = whole[cut:, :]


def across(values, bit):
    count = lax.axis_size("wide")
    return lax.ppermute(values, "wide", [(i, i ^ bit) for i in range(count)])


def along(values, step):
    count = lax.axis_size("narrow")
    return lax.ppermute(values, "narrow", [(i, (i + step) % count) for i in range(count)])


def gather_shards(piece, count):
    half = piece.shape[0] // 2
    zero = jnp.stack([along(piece, -step) for step in range(1, count)])
    side, deep = across(zero, SIDE), across(zero, DEEP)
    far_a = across(side[:, :half], DEEP)
    far_b = across(deep[:, half:], SIDE)
    found = [zero, side, deep, far_a, far_b]
    other = [across(a, CORE) for a in found]
    return [found[0], other[0], found[1], other[1], found[2], other[2], found[3], found[4], other[3], other[4]]


def add_low(left, right):
    return (left.astype(F32) + right.astype(F32)).astype(BF16)


def reduce_plane(keep, send, side_first):
    other = across(send, CORE)
    if side_first:
        stay = add_low(jnp.stack([keep[0], keep[2]]), jnp.stack([other[0], other[2]]))
        leave = add_low(jnp.stack([keep[1], keep[3]]), jnp.stack([other[1], other[3]]))
        bits = (SIDE, DEEP)
    else:
        stay = add_low(keep[:2], other[:2])
        leave = add_low(keep[2:], other[2:])
        bits = (DEEP, SIDE)
    other = across(leave, bits[0])
    stay_one = add_low(stay[0], other[0])
    leave_one = add_low(stay[1], other[1])
    return add_low(stay_one, across(leave_one, bits[1]))


def rest_of_wide(values):
    bit = PIECES
    while bit < lax.axis_size("wide"):
        values = (values.astype(F32) + across(values, bit).astype(F32)).astype(values.dtype)
        bit *= 2
    return values


def gather_wide(values):
    half = values.shape[1] // 2
    side, deep = across(values, SIDE), across(values, DEEP)
    far = jnp.concatenate(
        [across(side[:, :half], DEEP), across(deep[:, half:], SIDE)], axis=1
    )
    found = [values, side, deep, far]
    other = [across(a, CORE) for a in found]
    return [a for pair in zip(found, other, strict=True) for a in pair]


def body(
    tokens,
    page_mask,
    buckets,
    mask_token,
    first_gain,
    first_shift,
    qkv_weight,
    query_bias,
    value_bias,
    position_bias,
    out_weight,
    out_bias,
    attn_scale,
    second_gain,
    second_shift,
    in_weight,
    in_bias,
    down_weight,
    down_bias,
    mlp_scale,
    out_grad,
):
    pages, seq, width = tokens.shape
    count = lax.axis_size("narrow")
    local = qkv_weight.shape[2]
    heads, bucket_count = position_bias.shape
    rows = pages * PAD
    piece_rows = width // PIECES
    place = lax.bitwise_and(lax.axis_index("wide").astype(jnp.int32), PIECES - 1)
    place_ref = place.reshape(1)

    attn_own = jnp.concatenate(
        [qkv_weight.transpose(1, 2, 0).reshape(3 * local, width), out_weight], axis=0
    )
    own = [attn_own, in_weight, down_weight]
    gathered = [
        gather_shards(lax.dynamic_slice(mat, (place * piece_rows, 0), (piece_rows, width)), count)
        for mat in own
    ]

    tables = jnp.pad(position_bias, ((0, 0), (0, width - bucket_count)))
    small = jnp.concatenate(
        [query_bias, value_bias, in_bias, tables.reshape(-1)]
    ).reshape(-1, 128)
    smalls = [small] + [along(small, -step) for step in range(1, count)]
    qkv_shifts, in_shifts, table_parts = [], [], []
    for one in smalls:
        flat = one.reshape(-1)
        qkv_shifts.append(
            jnp.concatenate([flat[:local], jnp.zeros((local,), F32), flat[local : 2 * local]])[None]
        )
        in_shifts.append(flat[2 * local : 2 * local + width][None])
        table_parts.append(flat[2 * local + width :].reshape(heads, width // 128, 128))

    fill = ((0, 0), (0, PAD - seq), (0, 0))
    tok = jnp.pad(tokens, fill).reshape(rows, width)
    grad = jnp.pad(out_grad, fill).reshape(rows, width)
    flags = (page_mask > 0) & (jnp.arange(seq, dtype=jnp.int32) % SEQ != 0)
    mask = jnp.pad(flags.astype(F32), ((0, 0), (0, PAD - seq))).reshape(rows, 1)
    index = jnp.pad(buckets, ((0, PAD - seq), (0, LANES - seq)))
    wide_shape = (rows, width)

    x_one = call(first_kernel, "first", [(wide_shape, BF16)], [vmem()] * 3)(
        tok, mask, jnp.stack([mask_token, first_gain, first_shift])
    )[0]
    biases = [
        call(bias_kernel, f"bias{d}", [((heads, PAD, LANES), F32)], [vmem()] * 2)(index, t)[0]
        for d, t in enumerate(table_parts)
    ]

    acc = None
    kept = []
    for d in range(count):
        weights = [attn_own] if d == 0 else gathered[0]
        first = acc is None
        more = [] if first else [acc]
        acc, qkv, probs, mixed = call(
            functools.partial(attend_kernel, len(weights), d - 1, first),
            f"attend{d}",
            [
                (wide_shape, F32),
                ((3, rows, local), BF16),
                ((pages * heads, PAD, PAD), BF16),
                ((rows, local), BF16),
            ],
            [scalars()] + [anywhere()] * len(weights) + [vmem()] * (3 + len(more)),
            scratch=[pltpu.VMEM((width, width), BF16), pltpu.SemaphoreType.DMA],
            flops=2 * rows * width * width + pages * heads * PAD * PAD * 1024,
            nbytes=2 * width * width,
        )(place_ref, *weights, x_one, qkv_shifts[d], biases[d], *more)
        kept.append((qkv, probs, mixed))

    middle, x_two, mlp_grad = call(
        middle_kernel, "middle", [(wide_shape, F32), (wide_shape, BF16), (wide_shape, BF16)], [vmem()] * 5
    )(
        acc,
        tok,
        mask,
        grad,
        jnp.stack([mask_token, out_bias, attn_scale, second_gain, second_shift, mlp_scale]),
    )

    out_sum = back_sum = None
    in_cols, mlp_pieces = [], []
    for d in range(count):
        in_ws = [in_weight] if d == 0 else gathered[1]
        down_ws = [down_weight] if d == 0 else gathered[2]
        first = out_sum is None
        more = [] if first else [out_sum, back_sum]
        out_sum, back_sum, in_col, keep, send = call(
            functools.partial(mlp_kernel, len(in_ws), d - 1, first),
            f"mlp{d}",
            [
                (wide_shape, F32),
                (wide_shape, F32),
                ((1, width), F32),
                ((4, 2, piece_rows, width), BF16),
                ((4, 2, piece_rows, width), BF16),
            ],
            [scalars()] + [anywhere()] * (2 * len(in_ws)) + [vmem()] * (3 + len(more)),
            out_specs=[vmem()] * 3 + [anywhere()] * 2,
            scratch=[pltpu.VMEM((width, width), BF16)] * 4
            + [pltpu.SemaphoreType.DMA((2,)), pltpu.SemaphoreType.DMA],
            flops=12 * rows * width * width,
            nbytes=2 * width * width,
        )(place_ref, *in_ws, *down_ws, x_two, mlp_grad, in_shifts[d], *more)
        in_cols.append(in_col)
        mlp_pieces.append(reduce_plane(keep, send, d % 2 == 0))

    layer, middle_grad, attn_grad, mid_sums = call(
        turn_kernel,
        "turn",
        [(wide_shape, BF16), (wide_shape, F32), (wide_shape, BF16), ((8, width), F32)],
        [vmem()] * 6,
    )(
        middle,
        out_sum,
        back_sum,
        grad,
        acc,
        jnp.stack([second_gain, down_bias, mlp_scale, attn_scale, out_bias]),
    )

    first_sum = None
    qkv_cols, grids = [None] * count, [None] * count
    attn_pieces = [None] * count
    for d in list(range(1, count)) + [0]:
        weights = [attn_own] if d == 0 else gathered[0]
        first = first_sum is None
        more = [] if first else [first_sum]
        first_sum, qkv_cols[d], grids[d], keep, send = call(
            functools.partial(attend_back_kernel, len(weights), d - 1, first),
            f"attend_back{d}",
            [
                (wide_shape, F32),
                ((1, 3 * local), F32),
                ((heads, PAD, PAD), F32),
                ((4, 1, piece_rows, width), BF16),
                ((4, 1, piece_rows, width), BF16),
            ],
            [scalars()] + [anywhere()] * len(weights) + [vmem()] * (5 + len(more)),
            out_specs=[vmem()] * 3 + [anywhere()] * 2,
            scratch=[
                pltpu.VMEM((width, width), BF16),
                pltpu.VMEM((width, width), BF16),
                pltpu.VMEM((rows, 3 * local), BF16),
                pltpu.SemaphoreType.DMA,
                pltpu.SemaphoreType.DMA,
            ],
            flops=4 * rows * width * width + pages * heads * PAD * PAD * 2048,
            nbytes=2 * width * width,
        )(place_ref, *weights, x_one, attn_grad, *kept[d], *more)
        attn_pieces[d] = reduce_plane(keep, send, d % 2 == 0)

    tok_grad, last_sums = call(
        last_kernel, "last", [(wide_shape, BF16), ((8, width), F32)], [vmem()] * 5
    )(tok, mask, middle_grad, first_sum, jnp.stack([mask_token, first_gain]))

    highs = width // LOW
    table = call(
        functools.partial(table_kernel, count),
        "table",
        [((count * heads * highs, LOW), F32)],
        [vmem()] * (1 + count),
        flops=2 * count * heads * highs * PAD * PAD * 128,
    )(index, *grids)[0]

    shared = jnp.concatenate([last_sums[:3], mid_sums[:6]], axis=0).reshape(-1)
    table_rows = table.reshape(count, heads * width)
    own_parts = [
        jnp.concatenate(
            [
                qkv_cols[d][0, :local],
                qkv_cols[d][0, 2 * local :],
                in_cols[d][0],
                table_rows[d],
            ]
        )
        for d in range(count)
    ]
    flat = jnp.concatenate([shared] + own_parts).reshape(-1, 128)
    for bit in (CORE, SIDE, DEEP):
        flat = flat + across(flat, bit)
    flat = rest_of_wide(flat).reshape(-1)
    size, part = shared.shape[0], own_parts[0].shape[0]
    total = flat[: size + part]
    for step in range(1, count):
        sent = jnp.concatenate([flat[:size], flat[size + step * part : size + (step + 1) * part]])
        total = total + along(sent.reshape(-1, 128), step).reshape(-1)
    sums = total[:size].reshape(9, width)
    part_sums = total[size:]

    def finish_pieces(pieces):
        done = pieces[0].astype(F32)
        for step in range(1, count):
            done = done + along(pieces[step], step).astype(F32)
        return gather_wide(rest_of_wide(done.astype(BF16)))

    in_w_grad, down_w_grad = call(
        mlp_final_kernel,
        "mlp_final",
        [((width, width), F32)] * 2,
        [scalars()] + [vmem()] * PIECES,
    )(place_ref, *finish_pieces(mlp_pieces))
    qkv_w_grad, out_w_grad = call(
        attend_final_kernel,
        "attend_final",
        [((3 * local, width), F32), ((local, width), F32)],
        [scalars()] + [vmem()] * PIECES,
        scratch=[pltpu.VMEM((width, width), F32)],
    )(place_ref, *finish_pieces(attn_pieces))

    return (
        layer.reshape(pages, PAD, width)[:, :seq],
        tok_grad.reshape(pages, PAD, width)[:, :seq],
        sums[0],
        sums[1],
        sums[2],
        qkv_w_grad.reshape(3, local, width).transpose(2, 0, 1),
        part_sums[:local],
        part_sums[local : 2 * local],
        part_sums[2 * local + width :].reshape(heads, width)[:, :bucket_count],
        out_w_grad,
        sums[3],
        sums[4],
        sums[5],
        sums[6],
        in_w_grad,
        part_sums[2 * local : 2 * local + width],
        down_w_grad,
        sums[7],
        sums[8],
    )


def solution(mesh):
    placed = (
        P(None, ("wide", "narrow"), None),
        P(None, ("wide", "narrow")),
        P(),
        P(),
        P(),
        P(),
        P(None, None, "narrow"),
        P("narrow"),
        P("narrow"),
        P("narrow", None),
        P("narrow", None),
        P(),
        P(),
        P(),
        P(),
        P(None, "narrow"),
        P("narrow"),
        P("narrow", None),
        P(),
        P(),
        P(None, ("wide", "narrow"), None),
    )
    return jax.shard_map(
        body,
        mesh=mesh,
        in_specs=placed,
        out_specs=(
            P(None, ("wide", "narrow"), None),
            P(None, ("wide", "narrow"), None),
            P(),
            P(),
            P(),
            P(None, None, "narrow"),
            P("narrow"),
            P("narrow"),
            P("narrow", None),
            P("narrow", None),
            P(),
            P(),
            P(),
            P(),
            P(None, "narrow"),
            P("narrow"),
            P("narrow", None),
            P(),
            P(),
        ),
        check_vma=False,
    )
```

```python
import functools

import jax
import jax.numpy as jnp
from jax import lax
from jax.experimental import pallas as pl
from jax.experimental.pallas import tpu as pltpu
from jax.sharding import PartitionSpec as P


SEQ = 197
PAD = 208
LANES = 256
EPSILON = 1e-06
ROOT_HALF = 0.7071067811865476
DENSITY = 0.3989422804014327
CORE, SIDE, DEEP = 1, 2, 4
PIECES = 8
LOW = 32
NEGATIVE = -1e30
FLOPS = 4 * 10**9
F32 = jnp.float32
BF16 = jnp.bfloat16

NN = (((1,), (0,)), ((), ()))
NT = (((1,), (1,)), ((), ()))
TN = (((0,), (0,)), ((), ()))


def mul(left, right, dims=NN):
    return lax.dot_general(left, right, dims, preferred_element_type=F32)


def vmem():
    return pl.BlockSpec(memory_space=pltpu.VMEM)


def anywhere():
    return pl.BlockSpec(memory_space=pl.ANY)


def scalars():
    return pl.BlockSpec(memory_space=pltpu.SMEM)


def near(values):
    return pltpu.with_memory_space_constraint(values, pltpu.VMEM)


def kept(shape, dtype):
    return pltpu.VMEM(shape, dtype)


def sent(shape, dtype):
    return jax.ShapeDtypeStruct(shape, dtype)


def call(kernel, name, outs, in_specs, out_specs=None, scratch=(), flops=0, limit=24):
    if out_specs is None:
        out_specs = [vmem()] * len(outs)
    return pl.pallas_call(
        kernel,
        out_shape=outs,
        in_specs=in_specs,
        out_specs=out_specs,
        scratch_shapes=list(scratch),
        compiler_params=pltpu.CompilerParams(vmem_limit_bytes=limit * 1024 * 1024),
        cost_estimate=pl.CostEstimate(flops=flops, bytes_accessed=1 << 20, transcendentals=0),
        name=name,
    )


class Jobs:
    def __init__(self, jobs):
        self.jobs = jobs

    def arrays(self):
        return [a for arrays, _ in self.jobs for a in arrays]

    def outs(self):
        return [
            sent((count,) + arrays[0].shape[1:], BF16) for arrays, counts in self.jobs for count in counts
        ]

    def scratch(self):
        made = [pltpu.VMEM((len(arrays),) + arrays[0].shape, BF16) for arrays, _ in self.jobs]
        return made + [pltpu.SemaphoreType.DMA((2 * len(self.jobs),))] if self.jobs else []

    def bind(self, refs_in, refs_out, scratch):
        if not self.jobs:
            return (lambda: None,) * 3
        sems = scratch[-1]
        coming, going, adds = [], [], []
        at_in = at_out = 0
        for number, (arrays, counts) in enumerate(self.jobs):
            held = scratch[number]
            for k in range(len(arrays)):
                coming.append(pltpu.make_async_copy(refs_in[at_in + k], held.at[k], sems.at[2 * number]))
            at_in += len(arrays)
            first = 0
            for count in counts:
                going.append(
                    pltpu.make_async_copy(
                        held.at[0, pl.ds(first, count)], refs_out[at_out], sems.at[2 * number + 1]
                    )
                )
                first += count
                at_out += 1
            adds.append((held, len(arrays)))

        def add():
            finish(coming)
            for held, n in adds:
                for i in range(held.shape[1]):
                    total = held[0, i].astype(F32)
                    for k in range(1, n):
                        total = total + held[k, i].astype(F32)
                    held[0, i] = total.astype(BF16)
            go(going)

        return (lambda: go(coming)), add, (lambda: finish(going))

    def split(self, outs):
        made, at = [], 0
        for _, counts in self.jobs:
            made.append(list(outs[at : at + len(counts)]))
            at += len(counts)
        return made


def norm_parts(values):
    center = values - jnp.mean(values, axis=-1, keepdims=True)
    spread = jnp.mean(center * center, axis=-1, keepdims=True)
    inverse = lax.rsqrt(spread + EPSILON)
    return center * inverse, inverse


def norm_back(grad, normed, inverse, gain):
    scaled = grad * gain
    inner = jnp.mean(scaled, axis=-1, keepdims=True)
    cross = jnp.mean(scaled * normed, axis=-1, keepdims=True)
    return inverse * (scaled - inner - normed * cross)


def col(values):
    return jnp.sum(values, axis=0, keepdims=True)


def go(copies):
    for c in copies:
        c.start()


def finish(copies):
    for c in copies:
        c.wait()


def first_kernel(tok_ref, mask_ref, token_ref, gain_ref, shift_ref, out_ref):
    masked = jnp.where(mask_ref[...] > 0.0, token_ref[...], tok_ref[...].astype(F32))
    normed, _ = norm_parts(masked)
    out = normed * gain_ref[...] + shift_ref[...]
    rows = lax.broadcasted_iota(jnp.int32, (tok_ref.shape[0], 1), 0)
    real = lax.rem(rows, PAD) < SEQ
    out_ref[...] = jnp.where(real, out, 0.0).astype(BF16)


def bias_kernel(buckets_ref, table_ref, out_ref):
    heads, parts, _ = table_ref.shape
    for half in range(2):
        lanes = pl.ds(half * 128, 128)
        index = buckets_ref[:, lanes]
        low = lax.bitwise_and(index, 127)
        high = lax.shift_right_logical(index, 7)
        column = lax.broadcasted_iota(jnp.int32, index.shape, 1) + half * 128
        for head in range(heads):
            total = jnp.full(index.shape, NEGATIVE, F32)
            for part in range(parts):
                row = jnp.broadcast_to(table_ref[head, part : part + 1, :], index.shape)
                found = jnp.take_along_axis(row, low, axis=1, mode="promise_in_bounds")
                total = jnp.where(high == part, found, total)
            out_ref[head, :, lanes] = jnp.where(column < SEQ, total, NEGATIVE)


def load_weights(w_ref, refs, slot, cut, target, sem):
    if len(refs) == 1:
        return [pltpu.make_async_copy(refs[0], target, sem)]
    rows = target.shape[0] // PIECES
    half = rows // 2
    parts = []
    for core in range(2):
        zero, side, deep, far_a, far_b = refs[5 * core : 5 * core + 5]
        parts += [(core + 2 * k, (cut or 0) * rows, 0, rows, ref) for k, ref in enumerate((zero, side, deep))]
        if cut is None:
            parts += [(core + 6, 0, 0, half, far_a), (core + 6, 0, half, half, far_b)]
        else:
            parts += [(core + 6, 0, 0, rows, (far_a, far_b)[cut])]
    made = []
    for piece, source, offset, count, ref in parts:
        start = pl.multiple_of(lax.bitwise_xor(w_ref[0], piece) * rows, rows)
        start = pl.multiple_of(start + offset, 16)
        made.append(
            pltpu.make_async_copy(
                ref.at[slot, pl.ds(source, count), :], target.at[pl.ds(start, count), :], sem
            )
        )
    return made


def attend_kernel(n_weights, slot, first, *refs):
    w_ref = refs[0]
    weights = refs[1 : 1 + n_weights]
    rest = refs[1 + n_weights :]
    x_ref, shift_ref, bias_ref = rest[:3]
    rest = rest[3:]
    if not first:
        acc_in = rest[0]
        rest = rest[1:]
    acc_ref, qkv_ref, probs_ref, mixed_ref, mat, sem = rest
    copies = load_weights(w_ref, weights, slot, None, mat, sem)
    go(copies)
    finish(copies)
    width = mat.shape[0]
    local = width // 4
    heads = bias_ref.shape[0]
    size = local // heads
    qkv = mul(x_ref[...], mat[: 3 * local, :], NT) + shift_ref[...]
    queries = (qkv[:, :local].astype(BF16).astype(F32) * size ** (-0.5)).astype(BF16)
    keys = qkv[:, local : 2 * local].astype(BF16)
    values = qkv[:, 2 * local :].astype(BF16)
    qkv_ref[0] = queries
    qkv_ref[1] = keys
    qkv_ref[2] = values
    lane = lax.broadcasted_iota(jnp.int32, (PAD, local), 1)
    pages = x_ref.shape[0] // PAD
    zero = jnp.zeros((PAD, local), BF16)
    for page in range(pages):
        rows = slice(page * PAD, (page + 1) * PAD)
        q, k, v = queries[rows], keys[rows], values[rows]
        mixed = jnp.zeros((PAD, local), F32)
        for head in range(heads):
            own = (lane >= head * size) & (lane < (head + 1) * size)
            scores = mul(jnp.where(own, q, zero), k, NT) + bias_ref[head][:, :PAD]
            top = jnp.max(scores, axis=1, keepdims=True)
            power = jnp.exp(scores - top)
            total = jnp.sum(power, axis=1, keepdims=True)
            probs = (power * (1.0 / total)).astype(BF16)
            probs_ref[page * heads + head] = probs
            mixed = mixed + mul(probs, jnp.where(own, v, zero))
        mixed_ref[rows, :] = mixed.astype(BF16)
    out = mul(mixed_ref[...], mat[3 * local :, :])
    acc_ref[...] = out if first else acc_in[...] + out


def middle_kernel(
    acc_ref, tok_ref, mask_ref, grad_ref, token_ref, bias_ref, scale_ref, gain_ref, shift_ref, mlp_ref, mid_ref, x_ref, mg_ref
):
    masked = jnp.where(mask_ref[...] > 0.0, token_ref[...], tok_ref[...].astype(F32))
    middle = masked + scale_ref[...] * (acc_ref[...] + bias_ref[...])
    mid_ref[...] = middle
    normed, _ = norm_parts(middle)
    x_ref[...] = (normed * gain_ref[...] + shift_ref[...]).astype(BF16)
    mg_ref[...] = (grad_ref[...].astype(F32) * mlp_ref[...]).astype(BF16)


def copies_out(w_ref, mats, order, keep, send, sem):
    place = w_ref[0]
    made = []
    for number, mat in enumerate(mats):
        rows = mat.shape[0] // PIECES
        for piece in range(PIECES):
            start = pl.multiple_of(lax.bitwise_xor(place, piece) * rows, rows)
            target = send if piece & CORE else keep
            made.append(
                pltpu.make_async_copy(
                    mat.at[pl.ds(start, rows), :], target.at[order[piece >> 1], number], sem
                )
            )
    return made


def mlp_kernel(n_weights, slot, first, order, jobs, *refs):
    w_ref = refs[0]
    in_refs = refs[1 : 1 + n_weights]
    down_refs = in_refs
    rest = refs[1 + n_weights :]
    if n_weights == 2:
        in_refs, down_refs = in_refs[:1], in_refs[1:]
    x_ref, mg_ref, shift_ref = rest[:3]
    rest = rest[3:]
    if not first:
        out_in, grad_in = rest[:2]
        rest = rest[2:]
    n_jobs = len(jobs.arrays())
    jobs_in, rest = rest[:n_jobs], rest[n_jobs:]
    out_ref, grad_ref, col_ref, keep, send = rest[:5]
    rest = rest[5:]
    n_jobs = len(jobs.outs())
    jobs_out, rest = rest[:n_jobs], rest[n_jobs:]
    in_mat, down_mat, in_grad, down_grad, sem, osem = rest[:6]
    start_jobs, add_jobs, end_jobs = jobs.bind(jobs_in, jobs_out, rest[6:])
    copies_a = load_weights(w_ref, in_refs, slot, 0, in_mat, sem.at[0])
    copies_b = load_weights(w_ref, down_refs, slot, 1, down_mat, sem.at[1])
    go(copies_a)
    go(copies_b)
    start_jobs()
    finish(copies_a)
    width = in_mat.shape[0]
    x = x_ref[...]
    mg = mg_ref[...]
    out = None
    back = None
    for start in range(0, width, 256):
        units = slice(start, start + 256)
        weight_in = in_mat[:, units]
        pre = mul(x, weight_in) + shift_ref[:, units]
        phi = 0.5 * (1.0 + lax.erf(pre * ROOT_HALF))
        hidden = (pre * phi).astype(BF16)
        slope = phi + pre * (DENSITY * jnp.exp(-0.5 * pre * pre))
        if start == 0:
            finish(copies_b)
        weight_down = down_mat[units, :]
        part = mul(hidden, weight_down)
        out = part if out is None else out + part
        hidden_grad = mul(mg, weight_down, NT)
        pre_grad = hidden_grad * slope
        low = pre_grad.astype(BF16)
        col_ref[:, units] = col(low.astype(F32))
        part = mul(low, weight_in, NT)
        back = part if back is None else back + part
        down_grad[units, :] = mul(hidden, mg, TN).astype(BF16)
        in_grad[:, units] = mul(x, low, TN).astype(BF16)
        if start == 0:
            add_jobs()
    copies = copies_out(w_ref, [in_grad, down_grad], order, keep, send, osem)
    go(copies)
    out_ref[...] = out if first else out_in[...] + out
    grad_ref[...] = back if first else grad_in[...] + back
    finish(copies)
    end_jobs()


def turn_kernel(
    mid_ref, out_ref, back_ref, grad_ref, acc_ref, gain_ref, down_ref, mlp_ref, scale_ref, bias_ref, layer_ref, mgrad_ref, ag_ref, sums_ref
):
    middle = mid_ref[...]
    grad = grad_ref[...].astype(F32)
    mlp_out = out_ref[...] + down_ref[...]
    layer_ref[...] = (middle + mlp_ref[...] * mlp_out).astype(BF16)
    normed, inverse = norm_parts(middle)
    second = back_ref[...]
    middle_grad = grad + norm_back(second, normed, inverse, gain_ref[...])
    mgrad_ref[...] = middle_grad
    scaled = middle_grad * scale_ref[...]
    ag_ref[...] = scaled.astype(BF16)
    sums_ref[0:1, :] = col(scaled)
    sums_ref[1:2, :] = col(middle_grad * (acc_ref[...] + bias_ref[...]))
    sums_ref[2:3, :] = col(second * normed)
    sums_ref[3:4, :] = col(second)
    sums_ref[4:5, :] = col(grad * mlp_ref[...])
    sums_ref[5:6, :] = col(grad * mlp_out)
    sums_ref[6:8, :] = jnp.zeros_like(sums_ref[6:8, :])


def attend_back_kernel(n_weights, slot, first, order, jobs, *refs):
    w_ref = refs[0]
    weights = refs[1 : 1 + n_weights]
    rest = refs[1 + n_weights :]
    x_ref, ag_ref, qkv_ref, probs_ref, mixed_ref = rest[:5]
    rest = rest[5:]
    if not first:
        grad_in = rest[0]
        rest = rest[1:]
    n_jobs = len(jobs.arrays())
    jobs_in, rest = rest[:n_jobs], rest[n_jobs:]
    grad_ref, col_ref, grid_ref, keep, send = rest[:5]
    rest = rest[5:]
    n_jobs = len(jobs.outs())
    jobs_out, rest = rest[:n_jobs], rest[n_jobs:]
    mat, mat_grad, dqkv, sem, osem = rest[:5]
    start_jobs, add_jobs, end_jobs = jobs.bind(jobs_in, jobs_out, rest[5:])
    copies = load_weights(w_ref, weights, slot, None, mat, sem)
    go(copies)
    start_jobs()
    finish(copies)
    width = mat.shape[0]
    local = width // 4
    heads = grid_ref.shape[0]
    size = local // heads
    ag = ag_ref[...]
    mixed_grad = mul(ag, mat[3 * local :, :], NT).astype(BF16)
    mat_grad[3 * local :, :] = mul(mixed_ref[...], ag, TN).astype(BF16)
    add_jobs()
    lane = lax.broadcasted_iota(jnp.int32, (PAD, local), 1)
    pages = x_ref.shape[0] // PAD
    zero = jnp.zeros((PAD, local), BF16)
    for page in range(pages):
        rows = slice(page * PAD, (page + 1) * PAD)
        q, v, dm = qkv_ref[0, rows, :], qkv_ref[2, rows, :], mixed_grad[rows]
        k = (qkv_ref[1, rows, :].astype(F32) * size ** (-0.5)).astype(BF16)
        dq = jnp.zeros((PAD, local), F32)
        dk = jnp.zeros((PAD, local), F32)
        dv = jnp.zeros((PAD, local), F32)
        for head in range(heads):
            own = (lane >= head * size) & (lane < (head + 1) * size)
            dmh = jnp.where(own, dm, zero)
            probs_low = probs_ref[page * heads + head]
            probs = probs_low.astype(F32)
            weighed = probs * mul(dmh, v, NT)
            score = weighed - probs * jnp.sum(weighed, axis=1, keepdims=True)
            low = score.astype(BF16)
            if page == 0:
                grid_ref[head] = low.astype(F32)
            else:
                grid_ref[head] = grid_ref[head] + low.astype(F32)
            dq = dq + mul(low, jnp.where(own, k, zero))
            dk = dk + mul(low, jnp.where(own, q, zero), TN)
            dv = dv + mul(probs_low, dmh, TN)
        dqkv[rows, :] = jnp.concatenate([dq, dk, dv], axis=1).astype(BF16)
    grads = dqkv[...]
    mat_grad[: 3 * local, :] = mul(grads, x_ref[...], TN).astype(BF16)
    copies = copies_out(w_ref, [mat_grad], order, keep, send, osem)
    go(copies)
    col_ref[...] = col(grads.astype(F32))
    back = mul(grads, mat[: 3 * local, :])
    grad_ref[...] = back if first else grad_in[...] + back
    finish(copies)
    end_jobs()


def last_kernel(tok_ref, mask_ref, mgrad_ref, first_ref, token_ref, gain_ref, grad_ref, sums_ref):
    mask = mask_ref[...] > 0.0
    masked = jnp.where(mask, token_ref[...], tok_ref[...].astype(F32))
    normed, inverse = norm_parts(masked)
    first = first_ref[...]
    in_grad = mgrad_ref[...] + norm_back(first, normed, inverse, gain_ref[...])
    grad_ref[...] = jnp.where(mask, 0.0, in_grad).astype(BF16)
    sums_ref[0:1, :] = col(jnp.where(mask, in_grad, 0.0))
    sums_ref[1:2, :] = col(first * normed)
    sums_ref[2:3, :] = col(first)
    sums_ref[3:8, :] = jnp.zeros_like(sums_ref[3:8, :])


def table_kernel(grid_count, *refs):
    buckets_ref = refs[0]
    grids = refs[1 : 1 + grid_count]
    out_ref = refs[1 + grid_count]
    heads = grids[0].shape[0]
    highs = out_ref.shape[0] // (grid_count * heads)
    out_ref[...] = jnp.zeros_like(out_ref)

    def step(block, _):
        base = pl.multiple_of(block * 8, 8)
        index = buckets_ref[pl.ds(base, 8), :][:, :PAD]
        loads = [[g[h, pl.ds(base, 8), :] for h in range(heads)] for g in grids]
        total = None
        for row in range(8):
            one = index[row : row + 1]
            low = lax.bitwise_and(one, LOW - 1)
            high = lax.shift_right_logical(one, LOW.bit_length() - 1)
            right = (
                jnp.broadcast_to(low, (LOW, PAD)) == lax.broadcasted_iota(jnp.int32, (LOW, PAD), 0)
            ).astype(F32).astype(BF16)
            match = jnp.broadcast_to(high, (highs, PAD)) == lax.broadcasted_iota(
                jnp.int32, (highs, PAD), 0
            )
            left = jnp.concatenate(
                [
                    jnp.where(match, jnp.broadcast_to(loads[g][h][row : row + 1], (highs, PAD)), 0.0)
                    for g in range(grid_count)
                    for h in range(heads)
                ],
                axis=0,
            ).astype(BF16)
            part = mul(left, right, NT)
            total = part if total is None else total + part
        out_ref[...] += total
        return 0

    lax.fori_loop(0, PAD // 8, step, 0)


def sum_kernel(jobs, *refs):
    n_in, n_out = len(jobs.arrays()), len(jobs.outs())
    start, add, end = jobs.bind(refs[:n_in], refs[n_in : n_in + n_out], refs[n_in + n_out :])
    start()
    add()
    end()


def assemble(w_ref, pieces, number, place_in):
    for piece, ref in enumerate(pieces):
        rows = place_in.shape[0] // PIECES
        start = pl.multiple_of(lax.bitwise_xor(w_ref[0], piece) * rows, rows)
        place_in[pl.ds(start, rows), :] = ref[0, number].astype(F32)


def mlp_final_kernel(w_ref, *refs):
    pieces, (in_ref, down_ref) = refs[:PIECES], refs[PIECES:]
    assemble(w_ref, pieces, 0, in_ref)
    assemble(w_ref, pieces, 1, down_ref)


def attend_final_kernel(w_ref, *refs):
    pieces, (qkv_ref, out_ref, whole) = refs[:PIECES], refs[PIECES:]
    assemble(w_ref, pieces, 0, whole)
    cut = qkv_ref.shape[0]
    qkv_ref[...] = whole[:cut, :]
    out_ref[...] = whole[cut:, :]


def across(values, bit):
    count = lax.axis_size("wide")
    return lax.ppermute(values, "wide", [(i, i ^ bit) for i in range(count)])


def along(values, step):
    count = lax.axis_size("narrow")
    return lax.ppermute(values, "narrow", [(i, (i + step) % count) for i in range(count)])


def spread(zero):
    half = zero.shape[1] // 2
    side, deep = across(zero, SIDE), across(zero, DEEP)
    far_a = across(side[:, :half], DEEP)
    far_b = across(deep[:, half:], SIDE)
    found = [zero, side, deep, far_a, far_b]
    return found + [across(a, CORE) for a in found]


def rest_of_wide(values):
    bit = PIECES
    while bit < lax.axis_size("wide"):
        values = (values.astype(F32) + across(values, bit).astype(F32)).astype(values.dtype)
        bit *= 2
    return values


def gather_wide(values):
    found = [values] + [across(values, bit) for bit in (SIDE, DEEP, SIDE | DEEP)]
    other = [across(a, CORE) for a in found]
    return [a for pair in zip(found, other, strict=True) for a in pair]


SIDE_FIRST = (0, 2, 1, 3)
DEEP_FIRST = (0, 1, 2, 3)


def body(
    tokens,
    page_mask,
    buckets,
    mask_token,
    first_gain,
    first_shift,
    qkv_weight,
    query_bias,
    value_bias,
    position_bias,
    out_weight,
    out_bias,
    attn_scale,
    second_gain,
    second_shift,
    in_weight,
    in_bias,
    down_weight,
    down_bias,
    mlp_scale,
    out_grad,
):
    pages, seq, width = tokens.shape
    count = lax.axis_size("narrow")
    local = qkv_weight.shape[2]
    heads, bucket_count = position_bias.shape
    rows = pages * PAD
    piece_rows = width // PIECES
    place = lax.bitwise_and(lax.axis_index("wide").astype(jnp.int32), PIECES - 1)
    place_ref = place.reshape(1)
    wide_shape = (rows, width)

    def vector(values):
        return values.reshape(1, -1)

    def own_piece(mat):
        return lax.dynamic_slice(mat, (place * piece_rows, 0), (piece_rows, width))

    attn_own = jnp.concatenate(
        [qkv_weight.transpose(1, 2, 0).reshape(3 * local, width), out_weight], axis=0
    )
    piece = own_piece(attn_own)
    attn_parts = spread(jnp.stack([along(piece, -step) for step in range(1, count)]))
    piece = jnp.concatenate([own_piece(in_weight), own_piece(down_weight)], axis=0)
    near_shards = spread(jnp.stack([along(piece, -1), along(piece, 1)]))
    far_shards = [
        spread(jnp.stack([along(piece, -step) for step in range(2, count - 1)]))
    ]
    mlp_order = [0, 1, count - 1] + list(range(2, count - 1))
    mlp_parts = {1: (near_shards, 0), count - 1: (near_shards, 1)}
    for step in range(2, count - 1):
        mlp_parts[step] = (far_shards[0], step - 2)

    tables = jnp.pad(position_bias, ((0, 0), (0, width - bucket_count)))
    small = jnp.concatenate([query_bias, value_bias, in_bias, tables.reshape(-1)]).reshape(-1, 128)
    smalls = [small] + [along(small, -step) for step in range(1, count)]
    qkv_shifts, in_shifts, table_parts = [], [], []
    for one in smalls:
        flat = one.reshape(-1)
        qkv_shifts.append(
            vector(jnp.concatenate([flat[:local], jnp.zeros((local,), F32), flat[local : 2 * local]]))
        )
        in_shifts.append(vector(flat[2 * local : 2 * local + width]))
        table_parts.append(flat[2 * local + width :].reshape(heads, width // 128, 128))

    fill = ((0, 0), (0, PAD - seq), (0, 0))
    tok = near(jnp.pad(tokens, fill).reshape(rows, width))
    grad = near(jnp.pad(out_grad, fill).reshape(rows, width))
    flags = (page_mask > 0) & (jnp.arange(seq, dtype=jnp.int32) % SEQ != 0)
    mask = jnp.pad(flags.astype(F32), ((0, 0), (0, PAD - seq))).reshape(rows, 1)
    index = near(jnp.pad(buckets, ((0, PAD - seq), (0, LANES - seq))))

    x_one = near(
        call(first_kernel, "first", [kept(wide_shape, BF16)], [vmem()] * 5)(
            tok, mask, vector(mask_token), vector(first_gain), vector(first_shift)
        )[0]
    )
    biases = [
        near(
            call(bias_kernel, f"bias{d}", [kept((heads, PAD, LANES), F32)], [vmem()] * 2)(index, t)[0]
        )
        for d, t in enumerate(table_parts)
    ]

    acc = None
    held = []
    for d in range(count):
        weights = [attn_own] if d == 0 else attn_parts
        first = acc is None
        more = [] if first else [acc]
        acc, qkv, probs, mixed = (
            near(a)
            for a in call(
                functools.partial(attend_kernel, len(weights), d - 1, first),
                f"attend{d}",
                [
                    kept(wide_shape, F32),
                    kept((3, rows, local), BF16),
                    kept((pages * heads, PAD, PAD), BF16),
                    kept((rows, local), BF16),
                ],
                [scalars()] + [anywhere()] * len(weights) + [vmem()] * (3 + len(more)),
                scratch=[pltpu.VMEM((width, width), BF16), pltpu.SemaphoreType.DMA],
                flops=FLOPS,
            )(place_ref, *weights, x_one, qkv_shifts[d], biases[d], *more)
        )
        held.append((qkv, probs, mixed))

    middle, x_two, mlp_grad = (
        near(a)
        for a in call(
            middle_kernel,
            "middle",
            [kept(wide_shape, F32), kept(wide_shape, BF16), kept(wide_shape, BF16)],
            [vmem()] * 10,
        )(
            acc,
            tok,
            mask,
            grad,
            vector(mask_token),
            vector(out_bias),
            vector(attn_scale),
            vector(second_gain),
            vector(second_shift),
            vector(mlp_scale),
        )
    )

    group = {}

    def core_job(name):
        keep, send = group[name]
        return [keep, across(send, CORE)], (2, 2)

    def hop_job(name):
        (stay, leave), bit = group[name]
        return [stay, across(leave, bit)], (1, 1)

    def end_job(name):
        (stay, leave), bit = group[name]
        return [stay, across(leave, bit)], (1,)

    bits = {}

    def run_jobs(plan):
        makers = {"core": core_job, "hop": hop_job, "end": end_job}
        jobs = Jobs([makers[step](name) for step, name in plan])

        def store(outs):
            for (step, name), made in zip(plan, jobs.split(outs), strict=True):
                if step == "core":
                    group[name] = (made, bits[name][0])
                elif step == "hop":
                    group[name] = (made, bits[name][1])
                else:
                    group[name] = made[0]

        return jobs, store

    def sums_of(plan):
        jobs, store = run_jobs(plan)
        outs = call(
            functools.partial(sum_kernel, jobs),
            "sum_" + "_".join(name for _, name in plan),
            jobs.outs(),
            [anywhere()] * len(jobs.arrays()),
            out_specs=[anywhere()] * len(jobs.outs()),
            scratch=jobs.scratch(),
        )(*jobs.arrays())
        store(outs)

    out_sum = back_sum = None
    in_cols = [None] * count
    mlp_plans = {2: [("core", "m0")], 3: [("core", "m1")]}
    for turn, d in enumerate(mlp_order):
        weights, slot = ([in_weight, down_weight], 0) if d == 0 else mlp_parts[d]
        first = out_sum is None
        more = [] if first else [out_sum, back_sum]
        name = f"m{turn}"
        order = SIDE_FIRST if turn % 2 == 0 else DEEP_FIRST
        bits[name] = (SIDE, DEEP) if turn % 2 == 0 else (DEEP, SIDE)
        jobs, store = run_jobs(mlp_plans.get(turn, []))
        outs = call(
            functools.partial(mlp_kernel, len(weights), slot, first, order, jobs),
            f"mlp{turn}",
            [
                kept(wide_shape, F32),
                kept(wide_shape, F32),
                sent((1, width), F32),
                sent((4, 2, piece_rows, width), BF16),
                sent((4, 2, piece_rows, width), BF16),
            ]
            + jobs.outs(),
            [scalars()]
            + [anywhere()] * len(weights)
            + [vmem()] * (3 + len(more))
            + [anywhere()] * len(jobs.arrays()),
            out_specs=[vmem()] * 3 + [anywhere()] * (2 + len(jobs.outs())),
            scratch=[pltpu.VMEM((width, width), BF16)] * 4
            + [pltpu.SemaphoreType.DMA((2,)), pltpu.SemaphoreType.DMA]
            + jobs.scratch(),
            flops=FLOPS,
        )(place_ref, *weights, x_two, mlp_grad, in_shifts[d], *more, *jobs.arrays())
        out_sum, back_sum, in_cols[d] = near(outs[0]), near(outs[1]), outs[2]
        group[name] = outs[3:5]
        store(outs[5:])

    layer, middle_grad, attn_grad, mid_sums = call(
        turn_kernel,
        "turn",
        [sent(wide_shape, BF16), kept(wide_shape, F32), kept(wide_shape, BF16), kept((8, width), F32)],
        [vmem()] * 10,
    )(
        middle,
        out_sum,
        back_sum,
        grad,
        acc,
        vector(second_gain),
        vector(down_bias),
        vector(mlp_scale),
        vector(attn_scale),
        vector(out_bias),
    )
    middle_grad, attn_grad = near(middle_grad), near(attn_grad)

    first_sum = None
    qkv_cols, grids = [None] * count, [None] * count
    back_order = list(range(1, count)) + [0]
    back_plans = {
        0: [("core", "m2")],
        1: [("hop", "m0"), ("core", "m3")],
        2: [("hop", "m1"), ("core", "a0")],
        3: [("hop", "m2"), ("core", "a1"), ("end", "m0")],
    }
    for turn, d in enumerate(back_order):
        weights = [attn_own] if d == 0 else attn_parts
        first = first_sum is None
        more = [] if first else [first_sum]
        name = f"a{turn}"
        order = SIDE_FIRST if turn % 2 == 0 else DEEP_FIRST
        bits[name] = (SIDE, DEEP) if turn % 2 == 0 else (DEEP, SIDE)
        jobs, store = run_jobs(back_plans.get(turn, []))
        outs = call(
            functools.partial(attend_back_kernel, len(weights), d - 1, first, order, jobs),
            f"attend_back{d}",
            [
                kept(wide_shape, F32),
                sent((1, 3 * local), F32),
                kept((heads, PAD, PAD), F32),
                sent((4, 1, piece_rows, width), BF16),
                sent((4, 1, piece_rows, width), BF16),
            ]
            + jobs.outs(),
            [scalars()]
            + [anywhere()] * len(weights)
            + [vmem()] * (5 + len(more))
            + [anywhere()] * len(jobs.arrays()),
            out_specs=[vmem()] * 3 + [anywhere()] * (2 + len(jobs.outs())),
            scratch=[
                pltpu.VMEM((width, width), BF16),
                pltpu.VMEM((width, width), BF16),
                pltpu.VMEM((rows, 3 * local), BF16),
                pltpu.SemaphoreType.DMA,
                pltpu.SemaphoreType.DMA,
            ]
            + jobs.scratch(),
            flops=FLOPS,
        )(place_ref, *weights, x_one, attn_grad, *held[d], *more, *jobs.arrays())
        first_sum, qkv_cols[d], grids[d] = near(outs[0]), outs[1], near(outs[2])
        group[name] = outs[3:5]
        store(outs[5:])

    sums_of([("core", "a2"), ("core", "a3")])
    sums_of([("hop", "m3"), ("hop", "a0")])
    sums_of([("end", "m1"), ("end", "m2"), ("hop", "a1")])
    sums_of([("hop", "a2"), ("hop", "a3")])
    sums_of([("end", "m3"), ("end", "a0")])
    sums_of([("end", "a1"), ("end", "a2"), ("end", "a3")])

    tok_grad, last_sums = call(
        last_kernel, "last", [sent(wide_shape, BF16), kept((8, width), F32)], [vmem()] * 6
    )(tok, mask, middle_grad, first_sum, vector(mask_token), vector(first_gain))

    highs = width // LOW
    table = call(
        functools.partial(table_kernel, count),
        "table",
        [sent((count * heads * highs, LOW), F32)],
        [vmem()] * (1 + count),
        flops=FLOPS,
    )(index, *grids)[0]

    shared = jnp.concatenate([last_sums[:3], mid_sums[:6]], axis=0).reshape(-1)
    table_rows = table.reshape(count, heads * width)
    own_parts = [
        jnp.concatenate(
            [
                qkv_cols[d][0, :local],
                qkv_cols[d][0, 2 * local :],
                in_cols[d][0],
                table_rows[d],
            ]
        )
        for d in range(count)
    ]
    flat = jnp.concatenate([shared] + own_parts).reshape(-1, 128)
    for bit in (CORE, SIDE, DEEP):
        flat = flat + across(flat, bit)
    flat = rest_of_wide(flat).reshape(-1)
    size, part = shared.shape[0], own_parts[0].shape[0]
    total = flat[: size + part]
    for step in range(1, count):
        sent_part = jnp.concatenate([flat[:size], flat[size + step * part : size + (step + 1) * part]])
        total = total + along(sent_part.reshape(-1, 128), step).reshape(-1)
    sums = total[:size].reshape(9, width)
    part_sums = total[size:]

    def finish_pieces(pieces):
        jobs = Jobs([([pieces[0]] + [along(pieces[step], step) for step in range(1, count)], (1,))])
        done = call(
            functools.partial(sum_kernel, jobs),
            "sum_end",
            jobs.outs(),
            [anywhere()] * len(jobs.arrays()),
            out_specs=[anywhere()],
            scratch=jobs.scratch(),
        )(*jobs.arrays())[0]
        return gather_wide(rest_of_wide(done))

    mlp_pieces = {d: group[f"m{turn}"] for turn, d in enumerate(mlp_order)}
    in_w_grad, down_w_grad = call(
        mlp_final_kernel,
        "mlp_final",
        [sent((width, width), F32)] * 2,
        [scalars()] + [vmem()] * PIECES,
    )(place_ref, *finish_pieces(mlp_pieces))
    attn_pieces = {d: group[f"a{turn}"] for turn, d in enumerate(back_order)}
    qkv_w_grad, out_w_grad = call(
        attend_final_kernel,
        "attend_final",
        [sent((3 * local, width), F32), sent((local, width), F32)],
        [scalars()] + [vmem()] * PIECES,
        scratch=[pltpu.VMEM((width, width), F32)],
    )(place_ref, *finish_pieces(attn_pieces))

    return (
        layer.reshape(pages, PAD, width)[:, :seq],
        tok_grad.reshape(pages, PAD, width)[:, :seq],
        sums[0],
        sums[1],
        sums[2],
        qkv_w_grad.reshape(3, local, width).transpose(2, 0, 1),
        part_sums[:local],
        part_sums[local : 2 * local],
        part_sums[2 * local + width :].reshape(heads, width)[:, :bucket_count],
        out_w_grad,
        sums[3],
        sums[4],
        sums[5],
        sums[6],
        in_w_grad,
        part_sums[2 * local : 2 * local + width],
        down_w_grad,
        sums[7],
        sums[8],
    )


def solution(mesh):
    placed = (
        P(None, ("wide", "narrow"), None),
        P(None, ("wide", "narrow")),
        P(),
        P(),
        P(),
        P(),
        P(None, None, "narrow"),
        P("narrow"),
        P("narrow"),
        P("narrow", None),
        P("narrow", None),
        P(),
        P(),
        P(),
        P(),
        P(None, "narrow"),
        P("narrow"),
        P("narrow", None),
        P(),
        P(),
        P(None, ("wide", "narrow"), None),
    )
    return jax.shard_map(
        body,
        mesh=mesh,
        in_specs=placed,
        out_specs=(
            P(None, ("wide", "narrow"), None),
            P(None, ("wide", "narrow"), None),
            P(),
            P(),
            P(),
            P(None, None, "narrow"),
            P("narrow"),
            P("narrow"),
            P("narrow", None),
            P("narrow", None),
            P(),
            P(),
            P(),
            P(),
            P(None, "narrow"),
            P("narrow"),
            P("narrow", None),
            P(),
            P(),
        ),
        check_vma=False,
    )
```

```python
import functools

import jax
import jax.numpy as jnp
from jax import lax
from jax.experimental import pallas as pl
from jax.experimental.pallas import tpu as pltpu
from jax.sharding import PartitionSpec as P


SEQ = 197
PAD = 208
LANES = 256
EPSILON = 1e-06
ROOT_HALF = 0.7071067811865476
DENSITY = 0.3989422804014327
CORE, SIDE, DEEP = 1, 2, 4
PIECES = 8
LOW = 128
NEGATIVE = -1e30
FLOPS = 4 * 10**9
F32 = jnp.float32
BF16 = jnp.bfloat16

NN = (((1,), (0,)), ((), ()))
NT = (((1,), (1,)), ((), ()))
TN = (((0,), (0,)), ((), ()))


def mul(left, right, dims=NN):
    return lax.dot_general(left, right, dims, preferred_element_type=F32)


def vmem():
    return pl.BlockSpec(memory_space=pltpu.VMEM)


def anywhere():
    return pl.BlockSpec(memory_space=pl.ANY)


def scalars():
    return pl.BlockSpec(memory_space=pltpu.SMEM)


def near(values):
    return pltpu.with_memory_space_constraint(values, pltpu.VMEM)


def kept(shape, dtype):
    return pltpu.VMEM(shape, dtype)


def sent(shape, dtype):
    return jax.ShapeDtypeStruct(shape, dtype)


def call(kernel, name, outs, in_specs, out_specs=None, scratch=(), flops=0, limit=12):
    if out_specs is None:
        out_specs = [vmem()] * len(outs)
    made = pl.pallas_call(
        kernel,
        out_shape=outs,
        in_specs=in_specs,
        out_specs=out_specs,
        scratch_shapes=list(scratch),
        compiler_params=pltpu.CompilerParams(vmem_limit_bytes=limit * 1024 * 1024),
        cost_estimate=pl.CostEstimate(flops=flops, bytes_accessed=1 << 20, transcendentals=0),
        name=name,
    )
    return lambda *arrays: made(
        *[near(a) if spec.memory_space == pltpu.VMEM else a for spec, a in zip(in_specs, arrays, strict=True)]
    )


class Jobs:
    def __init__(self, jobs):
        self.jobs = jobs

    def arrays(self):
        return [a for arrays, _ in self.jobs for a in arrays]

    def outs(self):
        return [
            kept((count,) + arrays[0].shape[1:], BF16) for arrays, counts in self.jobs for count in counts
        ]

    def add(self, refs_in, refs_out):
        at_in = at_out = 0
        for arrays, counts in self.jobs:
            sources = refs_in[at_in : at_in + len(arrays)]
            at_in += len(arrays)
            first = 0
            for count in counts:
                for i in range(count):
                    total = sources[0][first + i].astype(F32)
                    for source in sources[1:]:
                        total = total + source[first + i].astype(F32)
                    refs_out[at_out][i] = total.astype(BF16)
                first += count
                at_out += 1

    def split(self, outs):
        made, at = [], 0
        for _, counts in self.jobs:
            made.append(list(outs[at : at + len(counts)]))
            at += len(counts)
        return made


def norm_parts(values):
    center = values - jnp.mean(values, axis=-1, keepdims=True)
    spread = jnp.mean(center * center, axis=-1, keepdims=True)
    inverse = lax.rsqrt(spread + EPSILON)
    return center * inverse, inverse


def norm_back(grad, normed, inverse, gain):
    scaled = grad * gain
    inner = jnp.mean(scaled, axis=-1, keepdims=True)
    cross = jnp.mean(scaled * normed, axis=-1, keepdims=True)
    return inverse * (scaled - inner - normed * cross)


def col(values):
    return jnp.sum(values, axis=0, keepdims=True)


SHIFTS = 4
TABLES = 10
SMALL = 32


def first_kernel(tok_ref, mask_ref, token_ref, gain_ref, shift_ref, out_ref):
    masked = jnp.where(mask_ref[...] > 0.0, token_ref[...], tok_ref[...].astype(F32))
    normed, _ = norm_parts(masked)
    out = normed * gain_ref[...] + shift_ref[...]
    rows = lax.broadcasted_iota(jnp.int32, (tok_ref.shape[0], 1), 0)
    real = lax.rem(rows, PAD) < SEQ
    out_ref[...] = jnp.where(real, out, 0.0).astype(BF16)


def bias_kernel(buckets_ref, small_ref, out_ref):
    heads = out_ref.shape[0]
    parts = 6
    for half in range(2):
        lanes = pl.ds(half * 128, 128)
        index = buckets_ref[:, lanes]
        low = lax.bitwise_and(index, 127)
        high = lax.shift_right_logical(index, 7)
        column = lax.broadcasted_iota(jnp.int32, index.shape, 1) + half * 128
        for head in range(heads):
            total = jnp.full(index.shape, NEGATIVE, F32)
            for part in range(parts):
                at = TABLES + head * parts + part
                row = jnp.broadcast_to(small_ref[at : at + 1, :], index.shape)
                found = jnp.take_along_axis(row, low, axis=1, mode="promise_in_bounds")
                total = jnp.where(high == part, found, total)
            out_ref[head, :, lanes] = jnp.where(column < SEQ, total, NEGATIVE)


def relay_kernel(n_in, n_more, *refs):
    refs = refs[len(refs) - n_in - n_more - 1 - (n_more > 0) :]
    for i in range(n_in):
        refs[n_in + n_more][i] = refs[i][...]
    if n_more:
        out = refs[-1]
        rows = refs[n_in].shape[0]
        for i in range(n_more):
            out[i * rows : (i + 1) * rows, :] = refs[n_in + i][...]


def put_together(w_ref, pieces, slot, cut, target):
    rows = target.shape[0] // PIECES
    for piece, ref in enumerate(pieces):
        start = pl.multiple_of(lax.bitwise_xor(w_ref[0], piece) * rows, rows)
        target[pl.ds(start, rows), :] = ref[slot, cut : cut + rows, :]


def take_apart(w_ref, mats, order, keep, send):
    for number, mat in enumerate(mats):
        rows = mat.shape[0] // PIECES
        for piece in range(PIECES):
            start = pl.multiple_of(lax.bitwise_xor(w_ref[0], piece) * rows, rows)
            target = send if piece & CORE else keep
            target[order[piece >> 1], number] = mat[pl.ds(start, rows), :]


def attend_kernel(n_weights, slot, first, *refs):
    w_ref = refs[0]
    weights = refs[1 : 1 + n_weights]
    rest = refs[1 + n_weights :]
    x_ref, small_ref, bias_ref = rest[:3]
    rest = rest[3:]
    if not first:
        acc_in = rest[0]
        rest = rest[1:]
    acc_ref, qkv_ref, probs_ref, mixed_ref = rest[:4]
    if n_weights == 1:
        mat = weights[0]
    else:
        mat = rest[4]
        put_together(w_ref, weights, slot, 0, mat)
    width = mat.shape[0]
    local = width // 4
    heads = bias_ref.shape[0]
    size = local // heads
    qkv = mul(x_ref[...], mat[: 3 * local, :], NT)
    spare = 2 * 128 - local
    queries = qkv[:, :local] + jnp.concatenate([small_ref[0:1, :], small_ref[1:2, : 128 - spare]], axis=1)
    queries = (queries.astype(BF16).astype(F32) * size ** (-0.5)).astype(BF16)
    keys = qkv[:, local : 2 * local].astype(BF16)
    values = qkv[:, 2 * local :] + jnp.concatenate([small_ref[2:3, :], small_ref[3:4, : 128 - spare]], axis=1)
    values = values.astype(BF16)
    qkv_ref[0] = queries
    qkv_ref[1] = keys
    qkv_ref[2] = values
    lane = lax.broadcasted_iota(jnp.int32, (PAD, local), 1)
    pages = x_ref.shape[0] // PAD
    zero = jnp.zeros((PAD, local), BF16)
    for page in range(pages):
        rows = slice(page * PAD, (page + 1) * PAD)
        q, k, v = queries[rows], keys[rows], values[rows]
        mixed = jnp.zeros((PAD, local), F32)
        for head in range(heads):
            own = (lane >= head * size) & (lane < (head + 1) * size)
            scores = mul(jnp.where(own, q, zero), k, NT) + bias_ref[head][:, :PAD]
            top = jnp.max(scores, axis=1, keepdims=True)
            power = jnp.exp(scores - top)
            total = jnp.sum(power, axis=1, keepdims=True)
            probs = (power * (1.0 / total)).astype(BF16)
            probs_ref[page * heads + head] = probs
            mixed = mixed + mul(probs, jnp.where(own, v, zero))
        mixed_ref[rows, :] = mixed.astype(BF16)
    out = mul(mixed_ref[...], mat[3 * local :, :])
    acc_ref[...] = out if first else acc_in[...] + out


def middle_kernel(
    acc_ref, tok_ref, mask_ref, grad_ref, token_ref, bias_ref, scale_ref, gain_ref, shift_ref, mlp_ref, mid_ref, x_ref, mg_ref
):
    masked = jnp.where(mask_ref[...] > 0.0, token_ref[...], tok_ref[...].astype(F32))
    middle = masked + scale_ref[...] * (acc_ref[...] + bias_ref[...])
    mid_ref[...] = middle
    normed, _ = norm_parts(middle)
    x_ref[...] = (normed * gain_ref[...] + shift_ref[...]).astype(BF16)
    mg_ref[...] = (grad_ref[...].astype(F32) * mlp_ref[...]).astype(BF16)


def mlp_kernel(n_weights, slot, first, order, jobs, *refs):
    w_ref = refs[0]
    weights = refs[1 : 1 + n_weights]
    rest = refs[1 + n_weights :]
    x_ref, mg_ref, small_ref = rest[:3]
    rest = rest[3:]
    if not first:
        out_in, grad_in = rest[:2]
        rest = rest[2:]
    n_jobs = len(jobs.arrays())
    jobs_in, rest = rest[:n_jobs], rest[n_jobs:]
    out_ref, grad_ref, col_ref, keep, send = rest[:5]
    rest = rest[5:]
    n_jobs = len(jobs.outs())
    jobs_out, rest = rest[:n_jobs], rest[n_jobs:]
    in_grad, down_grad = rest[:2]
    if n_weights == 2:
        in_mat, down_mat = weights
    else:
        in_mat, down_mat = rest[2:]
        put_together(w_ref, weights, slot, 0, in_mat)
        put_together(w_ref, weights, slot, in_mat.shape[0] // PIECES, down_mat)
    jobs.add(jobs_in, jobs_out)
    width = in_mat.shape[0]
    x = x_ref[...]
    mg = mg_ref[...]
    out = None
    back = None
    for start in range(0, width, 256):
        units = slice(start, start + 256)
        weight_in = in_mat[:, units]
        weight_down = down_mat[units, :]
        at = SHIFTS + start // 128
        pre = mul(x, weight_in) + jnp.concatenate([small_ref[at : at + 1, :], small_ref[at + 1 : at + 2, :]], axis=1)
        phi = 0.5 * (1.0 + lax.erf(pre * ROOT_HALF))
        hidden = (pre * phi).astype(BF16)
        slope = phi + pre * (DENSITY * jnp.exp(-0.5 * pre * pre))
        part = mul(hidden, weight_down)
        out = part if out is None else out + part
        hidden_grad = mul(mg, weight_down, NT)
        pre_grad = hidden_grad * slope
        low = pre_grad.astype(BF16)
        col_ref[:, units] = col(low.astype(F32))
        part = mul(low, weight_in, NT)
        back = part if back is None else back + part
        down_grad[units, :] = mul(hidden, mg, TN).astype(BF16)
        in_grad[:, units] = mul(x, low, TN).astype(BF16)
    out_ref[...] = out if first else out_in[...] + out
    grad_ref[...] = back if first else grad_in[...] + back
    take_apart(w_ref, [in_grad, down_grad], order, keep, send)


def turn_kernel(
    mid_ref, out_ref, back_ref, grad_ref, acc_ref, gain_ref, down_ref, mlp_ref, scale_ref, bias_ref, layer_ref, mgrad_ref, ag_ref, sums_ref
):
    middle = mid_ref[...]
    grad = grad_ref[...].astype(F32)
    mlp_out = out_ref[...] + down_ref[...]
    layer_ref[...] = (middle + mlp_ref[...] * mlp_out).astype(BF16)
    normed, inverse = norm_parts(middle)
    second = back_ref[...]
    middle_grad = grad + norm_back(second, normed, inverse, gain_ref[...])
    mgrad_ref[...] = middle_grad
    scaled = middle_grad * scale_ref[...]
    ag_ref[...] = scaled.astype(BF16)
    sums_ref[0:1, :] = col(scaled)
    sums_ref[1:2, :] = col(middle_grad * (acc_ref[...] + bias_ref[...]))
    sums_ref[2:3, :] = col(second * normed)
    sums_ref[3:4, :] = col(second)
    sums_ref[4:5, :] = col(grad * mlp_ref[...])
    sums_ref[5:6, :] = col(grad * mlp_out)
    sums_ref[6:8, :] = jnp.zeros_like(sums_ref[6:8, :])


def attend_back_kernel(first, order, jobs, *refs):
    w_ref, mat, x_ref, ag_ref, qkv_ref, probs_ref, mixed_ref = refs[:7]
    rest = refs[7:]
    if not first:
        grad_in = rest[0]
        rest = rest[1:]
    n_jobs = len(jobs.arrays())
    jobs_in, rest = rest[:n_jobs], rest[n_jobs:]
    grad_ref, col_ref, grid_ref, keep, send = rest[:5]
    rest = rest[5:]
    n_jobs = len(jobs.outs())
    jobs_out, rest = rest[:n_jobs], rest[n_jobs:]
    mat_grad, dqkv = rest
    jobs.add(jobs_in, jobs_out)
    width = mat.shape[0]
    local = width // 4
    heads = grid_ref.shape[0]
    size = local // heads
    ag = ag_ref[...]
    mixed_grad = mul(ag, mat[3 * local :, :], NT).astype(BF16)
    mat_grad[3 * local :, :] = mul(mixed_ref[...], ag, TN).astype(BF16)
    lane = lax.broadcasted_iota(jnp.int32, (PAD, local), 1)
    pages = x_ref.shape[0] // PAD
    zero = jnp.zeros((PAD, local), BF16)
    for page in range(pages):
        rows = slice(page * PAD, (page + 1) * PAD)
        q, v, dm = qkv_ref[0, rows, :], qkv_ref[2, rows, :], mixed_grad[rows]
        k = (qkv_ref[1, rows, :].astype(F32) * size ** (-0.5)).astype(BF16)
        dq = jnp.zeros((PAD, local), F32)
        dk = jnp.zeros((PAD, local), F32)
        dv = jnp.zeros((PAD, local), F32)
        for head in range(heads):
            own = (lane >= head * size) & (lane < (head + 1) * size)
            dmh = jnp.where(own, dm, zero)
            probs_low = probs_ref[page * heads + head]
            probs = probs_low.astype(F32)
            weighed = probs * mul(dmh, v, NT)
            score = weighed - probs * jnp.sum(weighed, axis=1, keepdims=True)
            low = score.astype(BF16)
            if page == 0:
                grid_ref[head] = low.astype(F32)
            else:
                grid_ref[head] = grid_ref[head] + low.astype(F32)
            dq = dq + mul(low, jnp.where(own, k, zero))
            dk = dk + mul(low, jnp.where(own, q, zero), TN)
            dv = dv + mul(probs_low, dmh, TN)
        dqkv[rows, :] = jnp.concatenate([dq, dk, dv], axis=1).astype(BF16)
    grads = dqkv[...]
    mat_grad[: 3 * local, :] = mul(grads, x_ref[...], TN).astype(BF16)
    col_ref[...] = col(grads.astype(F32))
    back = mul(grads, mat[: 3 * local, :])
    grad_ref[...] = back if first else grad_in[...] + back
    take_apart(w_ref, [mat_grad], order, keep, send)


def last_kernel(tok_ref, mask_ref, mgrad_ref, first_ref, token_ref, gain_ref, grad_ref, sums_ref):
    mask = mask_ref[...] > 0.0
    masked = jnp.where(mask, token_ref[...], tok_ref[...].astype(F32))
    normed, inverse = norm_parts(masked)
    first = first_ref[...]
    in_grad = mgrad_ref[...] + norm_back(first, normed, inverse, gain_ref[...])
    grad_ref[...] = jnp.where(mask, 0.0, in_grad).astype(BF16)
    sums_ref[0:1, :] = col(jnp.where(mask, in_grad, 0.0))
    sums_ref[1:2, :] = col(first * normed)
    sums_ref[2:3, :] = col(first)
    sums_ref[3:8, :] = jnp.zeros_like(sums_ref[3:8, :])


def table_kernel(grid_count, *refs):
    buckets_ref = refs[0]
    grids = refs[1 : 1 + grid_count]
    out_ref = refs[1 + grid_count]
    heads = grids[0].shape[0]
    highs = out_ref.shape[0] // (grid_count * heads)
    out_ref[...] = jnp.zeros_like(out_ref)

    def step(block, _):
        base = pl.multiple_of(block * 8, 8)
        index = buckets_ref[pl.ds(base, 8), :][:, :PAD]
        loads = [[g[h, pl.ds(base, 8), :] for h in range(heads)] for g in grids]
        total = None
        for row in range(8):
            one = index[row : row + 1]
            low = lax.bitwise_and(one, LOW - 1)
            high = lax.shift_right_logical(one, LOW.bit_length() - 1)
            right = (
                jnp.broadcast_to(low, (LOW, PAD)) == lax.broadcasted_iota(jnp.int32, (LOW, PAD), 0)
            ).astype(F32).astype(BF16)
            match = jnp.broadcast_to(high, (highs, PAD)) == lax.broadcasted_iota(
                jnp.int32, (highs, PAD), 0
            )
            left = jnp.concatenate(
                [
                    jnp.where(match, jnp.broadcast_to(loads[g][h][row : row + 1], (highs, PAD)), 0.0)
                    for g in range(grid_count)
                    for h in range(heads)
                ],
                axis=0,
            ).astype(BF16)
            part = mul(left, right, NT)
            total = part if total is None else total + part
        out_ref[...] += total
        return 0

    lax.fori_loop(0, PAD // 8, step, 0)


def sum_kernel(jobs, *refs):
    n_in, n_out = len(jobs.arrays()), len(jobs.outs())
    jobs.add(refs[:n_in], refs[n_in : n_in + n_out])


SHARED = 56
PART = 32


def pack_kernel(count, last_ref, mid_ref, table_ref, *refs):
    qkv_cols, in_cols, out_ref = refs[:count], refs[count : 2 * count], refs[2 * count]
    out_ref[...] = jnp.zeros_like(out_ref)

    def put(at, values):
        for k in range(0, values.shape[1], 128):
            part = values[:, k : k + 128]
            out_ref[at + k // 128 : at + k // 128 + 1, : part.shape[1]] = part

    for i in range(3):
        put(6 * i, last_ref[i : i + 1, :])
    for i in range(6):
        put(18 + 6 * i, mid_ref[i : i + 1, :])
    tables = table_ref.shape[0] // count
    for d in range(count):
        base = SHARED + d * PART
        put(base, qkv_cols[d][...])
        put(base + 6, in_cols[d][...])
        out_ref[base + 12 : base + 12 + tables, :] = table_ref[d * tables : (d + 1) * tables, :]


def parts_kernel(count, left_ref, right_ref, *outs):
    for d in range(count):
        outs[d][:SHARED, :] = left_ref[:SHARED, :] + right_ref[:SHARED, :]
        rows = slice(SHARED + d * PART, SHARED + (d + 1) * PART)
        outs[d][SHARED:, :] = left_ref[rows, :] + right_ref[rows, :]


def assemble(w_ref, pieces, number, place_in):
    for piece, ref in enumerate(pieces):
        rows = place_in.shape[0] // PIECES
        start = pl.multiple_of(lax.bitwise_xor(w_ref[0], piece) * rows, rows)
        place_in[pl.ds(start, rows), :] = ref[0, number].astype(F32)


def mlp_final_kernel(w_ref, *refs):
    pieces, (in_ref, down_ref) = refs[:PIECES], refs[PIECES:]
    assemble(w_ref, pieces, 0, in_ref)
    assemble(w_ref, pieces, 1, down_ref)


def attend_final_kernel(w_ref, *refs):
    pieces, (qkv_ref, out_ref, whole) = refs[:PIECES], refs[PIECES:]
    assemble(w_ref, pieces, 0, whole)
    cut = qkv_ref.shape[0]
    qkv_ref[...] = whole[:cut, :]
    out_ref[...] = whole[cut:, :]


def across(values, bit):
    count = lax.axis_size("wide")
    return lax.ppermute(values, "wide", [(i, i ^ bit) for i in range(count)])


def along(values, step):
    count = lax.axis_size("narrow")
    return lax.ppermute(values, "narrow", [(i, (i + step) % count) for i in range(count)])


def cores(found):
    return [a for one in found for a in (one, across(one, CORE))]


def spread(zero, direct, side_first=True):
    side, deep = across(zero, SIDE), across(zero, DEEP)
    if direct:
        far = across(zero, SIDE | DEEP)
    elif side_first:
        far = across(side, DEEP)
    else:
        far = across(deep, SIDE)
    return cores([zero, side, deep, far])


def rest_of_wide(values):
    bit = PIECES
    while bit < lax.axis_size("wide"):
        values = (values.astype(F32) + across(values, bit).astype(F32)).astype(values.dtype)
        bit *= 2
    return values


SIDE_FIRST = (0, 2, 1, 3)
DEEP_FIRST = (0, 1, 2, 3)


def body(
    tokens,
    page_mask,
    buckets,
    mask_token,
    first_gain,
    first_shift,
    qkv_weight,
    query_bias,
    value_bias,
    position_bias,
    out_weight,
    out_bias,
    attn_scale,
    second_gain,
    second_shift,
    in_weight,
    in_bias,
    down_weight,
    down_bias,
    mlp_scale,
    out_grad,
):
    pages, seq, width = tokens.shape
    count = lax.axis_size("narrow")
    local = qkv_weight.shape[2]
    heads, bucket_count = position_bias.shape
    rows = pages * PAD
    piece_rows = width // PIECES
    place = lax.bitwise_and(lax.axis_index("wide").astype(jnp.int32), PIECES - 1)
    place_ref = place.reshape(1)
    wide_shape = (rows, width)

    def vector(values):
        return values.reshape(1, -1)

    def own_piece(mat):
        return lax.dynamic_slice(mat, (place * piece_rows, 0), (piece_rows, width))

    attn_own = jnp.concatenate(
        [qkv_weight.transpose(1, 2, 0).reshape(3 * local, width), out_weight], axis=0
    )
    piece = own_piece(attn_own)
    attn_came = [along(piece, -step) for step in range(1, count)]

    tables = jnp.pad(position_bias, ((0, 0), (0, width - bucket_count))).reshape(-1)
    fill = jnp.zeros((2 * 128 - local,), F32)
    small = jnp.concatenate(
        [query_bias, fill, value_bias, fill, in_bias, tables, jnp.zeros(((SMALL - 28) * 128,), F32)]
    ).reshape(SMALL, 128)
    smalls = [a for a in [small] + [along(small, -step) for step in range(1, count)]]

    fill = ((0, 0), (0, PAD - seq), (0, 0))
    tok = jnp.pad(tokens, fill).reshape(rows, width)
    grad = jnp.pad(out_grad, fill).reshape(rows, width)
    flags = (page_mask > 0) & (jnp.arange(seq, dtype=jnp.int32) % SEQ != 0)
    mask = jnp.pad(flags.astype(F32), ((0, 0), (0, PAD - seq))).reshape(rows, 1)
    index = jnp.pad(buckets, ((0, PAD - seq), (0, LANES - seq)))

    x_one = (
        call(first_kernel, "first", [kept(wide_shape, BF16)], [vmem()] * 5)(
            tok, mask, vector(mask_token), vector(first_gain), vector(first_shift)
        )[0]
    )

    def relay(name, waits, stack, more):
        outs = [kept((len(stack),) + stack[0].shape, BF16)]
        if more:
            outs.append(kept((len(more) * more[0].shape[0], width), BF16))
        return [
            a
            for a in call(
                functools.partial(relay_kernel, len(stack), len(more)),
                name,
                outs,
                [anywhere()] * len(waits) + [vmem()] * (len(stack) + len(more)),
            )(*waits, *[a for a in stack + more])
        ]

    attn_zero, piece = relay("relay0", [x_one], attn_came, [own_piece(in_weight), own_piece(down_weight)])
    attn_parts = spread(attn_zero, True)
    near_came = [along(piece, -1), along(piece, 1)]

    biases = [
        call(bias_kernel, f"bias{d}", [kept((heads, PAD, LANES), F32)], [vmem()] * 2)(index, one)[0]
        for d, one in enumerate(smalls)
    ]

    acc = None
    held = []
    for d in range(count):
        own = d == 0
        weights = [attn_own] if own else attn_parts
        more = [] if own else [acc]
        outs = [
            a
            for a in call(
                functools.partial(attend_kernel, len(weights), d - 1, own),
                f"attend{d}",
                [
                    kept(wide_shape, F32),
                    kept((3, rows, local), BF16),
                    kept((pages * heads, PAD, PAD), BF16),
                    kept((rows, local), BF16),
                ]
                + ([] if own else [kept((width, width), BF16)]),
                [scalars()] + [vmem()] * (len(weights) + 3 + len(more)),
                flops=FLOPS,
            )(place_ref, *weights, x_one, smalls[d], biases[d], *more)
        ]
        acc = outs[0]
        held.append((weights[0] if own else outs[4], *outs[1:4]))
        if own:
            near_zero, piece = relay("relay1", [acc] + biases[1:], near_came, [piece])
            near_parts = spread(near_zero, False, True)
            far_zero = jnp.stack([along(piece, -step) for step in range(2, count - 1)])
            far_parts = spread(far_zero, False, False)

    mlp_order = [0, 1, count - 1] + list(range(2, count - 1))
    mlp_parts = {1: (near_parts, 0), count - 1: (near_parts, 1)}
    for step in range(2, count - 1):
        mlp_parts[step] = (far_parts, step - 2)

    middle, x_two, mlp_grad = (
        a
        for a in call(
            middle_kernel,
            "middle",
            [kept(wide_shape, F32), kept(wide_shape, BF16), kept(wide_shape, BF16)],
            [vmem()] * 10,
        )(
            acc,
            tok,
            mask,
            grad,
            vector(mask_token),
            vector(out_bias),
            vector(attn_scale),
            vector(second_gain),
            vector(second_shift),
            vector(mlp_scale),
        )
    )

    group, bits = {}, {}

    def core_job(name):
        keep, send = group[name]
        return [keep, across(send, CORE)], (2, 2)

    def hop_job(name):
        (stay, leave), bit = group[name]
        return [stay, across(leave, bit)], (1, 1)

    def end_job(name):
        (stay, leave), bit = group[name]
        return [stay, across(leave, bit)], (1,)

    def run_jobs(plan):
        makers = {"core": core_job, "hop": hop_job, "end": end_job}
        jobs = Jobs([makers[step](name) for step, name in plan])

        def store(outs):
            for (step, name), made in zip(plan, jobs.split(outs), strict=True):
                if step == "core":
                    group[name] = (made, bits[name][0])
                elif step == "hop":
                    group[name] = (made, bits[name][1])
                else:
                    group[name] = made[0]

        return jobs, store

    def sums_of(plan):
        jobs, store = run_jobs(plan)
        outs = call(
            functools.partial(sum_kernel, jobs),
            "sum_" + "_".join(name for _, name in plan),
            jobs.outs(),
            [vmem()] * len(jobs.arrays()),
        )(*jobs.arrays())
        store(outs)

    out_sum = back_sum = None
    in_cols = [None] * count
    mlp_plans = {2: [("core", "m0")], 3: [("core", "m1")]}
    for turn, d in enumerate(mlp_order):
        own = d == 0
        weights, slot = ([in_weight, down_weight], 0) if own else mlp_parts[d]
        more = [] if own else [out_sum, back_sum]
        name = f"m{turn}"
        order = SIDE_FIRST if turn % 2 == 0 else DEEP_FIRST
        bits[name] = (SIDE, DEEP) if turn % 2 == 0 else (DEEP, SIDE)
        jobs, store = run_jobs(mlp_plans.get(turn, []))
        outs = call(
            functools.partial(mlp_kernel, len(weights), slot, own, order, jobs),
            f"mlp{turn}",
            [
                kept(wide_shape, F32),
                kept(wide_shape, F32),
                kept((1, width), F32),
                kept((4, 2, piece_rows, width), BF16),
                kept((4, 2, piece_rows, width), BF16),
            ]
            + jobs.outs(),
            [scalars()] + [vmem()] * (len(weights) + 3 + len(more) + len(jobs.arrays())),
            scratch=[pltpu.VMEM((width, width), BF16)] * (2 if own else 4),
            flops=FLOPS,
        )(place_ref, *weights, x_two, mlp_grad, smalls[d], *more, *jobs.arrays())
        out_sum, back_sum, in_cols[d] = outs[0], outs[1], outs[2]
        group[name] = outs[3:5]
        store(outs[5:])

    layer, middle_grad, attn_grad, mid_sums = call(
        turn_kernel,
        "turn",
        [sent(wide_shape, BF16), kept(wide_shape, F32), kept(wide_shape, BF16), kept((8, width), F32)],
        [vmem()] * 10,
    )(
        middle,
        out_sum,
        back_sum,
        grad,
        acc,
        vector(second_gain),
        vector(down_bias),
        vector(mlp_scale),
        vector(attn_scale),
        vector(out_bias),
    )
    middle_grad, attn_grad, mid_sums = middle_grad, attn_grad, mid_sums

    first_sum = None
    qkv_cols, grids = [None] * count, [None] * count
    back_order = list(range(1, count)) + [0]
    back_plans = {
        0: [("core", "m2")],
        1: [("hop", "m0"), ("core", "m3")],
        2: [("hop", "m1"), ("core", "a0")],
        3: [("hop", "m2"), ("core", "a1"), ("end", "m0")],
    }
    for turn, d in enumerate(back_order):
        first = first_sum is None
        more = [] if first else [first_sum]
        name = f"a{turn}"
        order = SIDE_FIRST if turn % 2 == 0 else DEEP_FIRST
        bits[name] = (SIDE, DEEP) if turn % 2 == 0 else (DEEP, SIDE)
        jobs, store = run_jobs(back_plans.get(turn, []))
        mat, *others = held[d]
        outs = call(
            functools.partial(attend_back_kernel, first, order, jobs),
            f"attend_back{d}",
            [
                kept(wide_shape, F32),
                kept((1, 3 * local), F32),
                kept((heads, PAD, PAD), F32),
                kept((4, 1, piece_rows, width), BF16),
                kept((4, 1, piece_rows, width), BF16),
            ]
            + jobs.outs(),
            [scalars()] + [vmem()] * (6 + len(more) + len(jobs.arrays())),
            scratch=[pltpu.VMEM((width, width), BF16), pltpu.VMEM((rows, 3 * local), BF16)],
            flops=FLOPS,
        )(place_ref, mat, x_one, attn_grad, *others, *more, *jobs.arrays())
        first_sum, qkv_cols[d], grids[d] = outs[0], outs[1], outs[2]
        group[name] = outs[3:5]
        store(outs[5:])

    tok_grad, last_sums = call(
        last_kernel, "last", [sent(wide_shape, BF16), kept((8, width), F32)], [vmem()] * 6
    )(tok, mask, middle_grad, first_sum, vector(mask_token), vector(first_gain))

    sums_of([("core", "a2"), ("core", "a3")])
    sums_of([("hop", "m3"), ("hop", "a0")])
    sums_of([("end", "m1"), ("end", "m2"), ("hop", "a1")])
    sums_of([("hop", "a2"), ("hop", "a3")])
    sums_of([("end", "m3"), ("end", "a0")])
    sums_of([("end", "a1"), ("end", "a2"), ("end", "a3")])

    highs = width // LOW
    table = (
        call(
            functools.partial(table_kernel, count),
            "table",
            [kept((count * heads * highs, LOW), F32)],
            [vmem()] * (1 + count),
            flops=FLOPS,
        )(index, *grids)[0]
    )
    flat = call(
        functools.partial(pack_kernel, count),
        "pack",
        [kept((SHARED + count * PART, 128), F32)],
        [vmem()] * (3 + 2 * count),
    )(last_sums, mid_sums, table, *qkv_cols, *in_cols)[0]

    for bit in (CORE, SIDE):
        flat = flat + across(flat, bit)
    flat = rest_of_wide(flat)
    parts = call(
        functools.partial(parts_kernel, count),
        "parts",
        [kept((SHARED + PART, 128), F32)] * count,
        [vmem()] * 2,
    )(flat, across(flat, DEEP))
    total = parts[0]
    for step in range(1, count):
        total = total + along(parts[step], step)
    sums = total[: 9 * width // 128].reshape(9, width)
    qkv_bias_grads = total[SHARED : SHARED + 6].reshape(-1)

    def finish_pieces(pieces):
        jobs = Jobs([([pieces[0]] + [along(pieces[step], step) for step in range(1, count)], (1,))])
        done = call(
            functools.partial(sum_kernel, jobs),
            "sum_end",
            jobs.outs(),
            [vmem()] * len(jobs.arrays()),
        )(*jobs.arrays())[0]
        return spread(rest_of_wide(done), True)

    mlp_pieces = {d: group[f"m{turn}"] for turn, d in enumerate(mlp_order)}
    in_w_grad, down_w_grad = call(
        mlp_final_kernel,
        "mlp_final",
        [sent((width, width), F32)] * 2,
        [scalars()] + [vmem()] * PIECES,
    )(place_ref, *finish_pieces(mlp_pieces))
    attn_pieces = {d: group[f"a{turn}"] for turn, d in enumerate(back_order)}
    qkv_w_grad, out_w_grad = call(
        attend_final_kernel,
        "attend_final",
        [sent((3 * local, width), F32), sent((local, width), F32)],
        [scalars()] + [vmem()] * PIECES,
        scratch=[pltpu.VMEM((width, width), F32)],
    )(place_ref, *finish_pieces(attn_pieces))

    return (
        layer.reshape(pages, PAD, width)[:, :seq],
        tok_grad.reshape(pages, PAD, width)[:, :seq],
        sums[0],
        sums[1],
        sums[2],
        qkv_w_grad.reshape(3, local, width).transpose(2, 0, 1),
        qkv_bias_grads[:local],
        qkv_bias_grads[2 * local : 3 * local],
        total[SHARED + 12 : SHARED + 30].reshape(heads, width)[:, :bucket_count],
        out_w_grad,
        sums[3],
        sums[4],
        sums[5],
        sums[6],
        in_w_grad,
        total[SHARED + 6 : SHARED + 12].reshape(-1),
        down_w_grad,
        sums[7],
        sums[8],
    )


def solution(mesh):
    placed = (
        P(None, ("wide", "narrow"), None),
        P(None, ("wide", "narrow")),
        P(),
        P(),
        P(),
        P(),
        P(None, None, "narrow"),
        P("narrow"),
        P("narrow"),
        P("narrow", None),
        P("narrow", None),
        P(),
        P(),
        P(),
        P(),
        P(None, "narrow"),
        P("narrow"),
        P("narrow", None),
        P(),
        P(),
        P(None, ("wide", "narrow"), None),
    )
    return jax.shard_map(
        body,
        mesh=mesh,
        in_specs=placed,
        out_specs=(
            P(None, ("wide", "narrow"), None),
            P(None, ("wide", "narrow"), None),
            P(),
            P(),
            P(),
            P(None, None, "narrow"),
            P("narrow"),
            P("narrow"),
            P("narrow", None),
            P("narrow", None),
            P(),
            P(),
            P(),
            P(),
            P(None, "narrow"),
            P("narrow"),
            P("narrow", None),
            P(),
            P(),
        ),
        check_vma=False,
    )
```

```python
import functools

import jax
import jax.numpy as jnp
from jax import lax
from jax.experimental import pallas as pl
from jax.experimental.pallas import tpu as pltpu
from jax.sharding import PartitionSpec as P


SEQ = 197
PAD = 208
LANES = 256
EPSILON = 1e-06
ROOT_HALF = 0.7071067811865476
DENSITY = 0.3989422804014327
CORE, SIDE, DEEP = 1, 2, 4
PIECES = 8
LOW = 128
NEGATIVE = -1e30
FLOPS = 2 * 10**10
F32 = jnp.float32
BF16 = jnp.bfloat16

NN = (((1,), (0,)), ((), ()))
NT = (((1,), (1,)), ((), ()))
TN = (((0,), (0,)), ((), ()))


def mul(left, right, dims=NN):
    return lax.dot_general(left, right, dims, preferred_element_type=F32)


def vmem():
    return pl.BlockSpec(memory_space=pltpu.VMEM)


def anywhere():
    return pl.BlockSpec(memory_space=pl.ANY)


def scalars():
    return pl.BlockSpec(memory_space=pltpu.SMEM)


def near(values):
    return pltpu.with_memory_space_constraint(values, pltpu.VMEM)


def kept(shape, dtype):
    return pltpu.VMEM(shape, dtype)


def sent(shape, dtype):
    return jax.ShapeDtypeStruct(shape, dtype)


def call(kernel, name, outs, in_specs, out_specs=None, scratch=(), flops=FLOPS, limit=12, aliases=None):
    made = pl.pallas_call(
        kernel,
        out_shape=outs,
        in_specs=in_specs,
        out_specs=out_specs or [vmem()] * len(outs),
        scratch_shapes=list(scratch),
        input_output_aliases=aliases or {},
        compiler_params=pltpu.CompilerParams(vmem_limit_bytes=limit * 1024 * 1024),
        cost_estimate=pl.CostEstimate(flops=flops, bytes_accessed=0, transcendentals=0),
        name=name,
    )
    return lambda *arrays: made(
        *[near(a) if spec.memory_space == pltpu.VMEM else a for spec, a in zip(in_specs, arrays, strict=True)]
    )


class Line:
    def __init__(self):
        self.token = None

    def run(self, kernel, name, outs, arrays, scalar=None, waits=(), scratch=(), flops=FLOPS, limit=12):
        before = list(waits) + ([] if self.token is None else [self.token])
        start, n_in = (0 if scalar is None else 1), len(arrays)

        def whole(*refs):
            inputs = refs[: start + n_in]
            rest = refs[start + n_in + len(before) :]
            rest[len(outs)][...] = jnp.zeros((8, 128), F32)
            kernel(*inputs, *rest[: len(outs)], *rest[len(outs) + 1 :])

        made = call(
            whole,
            name,
            outs + [kept((8, 128), F32)],
            [scalars()] * start + [vmem()] * n_in + [anywhere()] * len(before),
            scratch=scratch,
            flops=flops,
            limit=limit,
        )(*([] if scalar is None else [scalar]), *arrays, *before)
        self.token = made[-1]
        return made[:-1]

    def gate(self, *arrays, waits=()):
        n = len(arrays)
        made = call(
            lambda *refs: None,
            "gate",
            [kept(a.shape, a.dtype) for a in arrays],
            [anywhere()] * (n + 1 + len(waits)),
            out_specs=[anywhere()] * n,
            aliases={i: i for i in range(n)},
            flops=0,
        )(*[near(a) for a in arrays], self.token, *waits)
        return made[0] if n == 1 else made


class Jobs:
    def __init__(self, jobs):
        self.jobs = jobs

    def arrays(self):
        return [a for arrays, _, _ in self.jobs for a in arrays]

    def outs(self):
        made = []
        for arrays, counts, parts in self.jobs:
            _, mats, *rest = arrays[0].shape
            made += [kept((count, mats // parts, *rest), BF16) for count in counts for _ in range(parts)]
        return made

    def add(self, refs_in, refs_out):
        at_in = at_out = 0
        for arrays, counts, parts in self.jobs:
            sources = refs_in[at_in : at_in + len(arrays)]
            at_in += len(arrays)
            mats = arrays[0].shape[1] // parts
            first = 0
            for count in counts:
                for part in range(parts):
                    for i in range(count):
                        for j in range(mats):
                            at = (first + i, part * mats + j)
                            total = sources[0][at].astype(F32)
                            for source in sources[1:]:
                                total = total + source[at].astype(F32)
                            refs_out[at_out][i, j] = total.astype(BF16)
                    at_out += 1
                first += count

    def split(self, outs):
        made, at = [], 0
        for _, counts, parts in self.jobs:
            made.append(list(outs[at : at + len(counts) * parts]))
            at += len(counts) * parts
        return made


def final_call(kernel, name, outs, scalar, arrays, token, scratch=()):
    n_in = 1 + len(arrays)
    return call(
        lambda *refs: kernel(*refs[:n_in], *refs[n_in + 1 :]),
        name,
        outs,
        [scalars()] + [vmem()] * len(arrays) + [anywhere()],
        scratch=scratch,
    )(scalar, *arrays, token)


def norm_parts(values):
    center = values - jnp.mean(values, axis=-1, keepdims=True)
    spread = jnp.mean(center * center, axis=-1, keepdims=True)
    inverse = lax.rsqrt(spread + EPSILON)
    return center * inverse, inverse


def norm_back(grad, normed, inverse, gain):
    scaled = grad * gain
    inner = jnp.mean(scaled, axis=-1, keepdims=True)
    cross = jnp.mean(scaled * normed, axis=-1, keepdims=True)
    return inverse * (scaled - inner - normed * cross)


def col(values):
    return jnp.sum(values, axis=0, keepdims=True)


SMALL = 8
VECTORS = 5


TOKEN, FIRST_GAIN, FIRST_SHIFT, OUT_BIAS, ATTN_SCALE, SECOND_GAIN, SECOND_SHIFT, MLP_SCALE, DOWN_BIAS = range(9)


def row(ref, number):
    return ref[number : number + 1, :]


def first_kernel(tok_ref, mask_ref, vec_ref, out_ref):
    masked = jnp.where(mask_ref[...] > 0.0, row(vec_ref, TOKEN), tok_ref[...].astype(F32))
    normed, _ = norm_parts(masked)
    out = normed * row(vec_ref, FIRST_GAIN) + row(vec_ref, FIRST_SHIFT)
    rows = lax.broadcasted_iota(jnp.int32, (tok_ref.shape[0], 1), 0)
    real = lax.rem(rows, PAD) < SEQ
    out_ref[...] = jnp.where(real, out, 0.0).astype(BF16)


def bias_kernel(buckets_ref, small_ref, out_ref):
    heads = out_ref.shape[0]
    parts = small_ref.shape[1] // 128
    for half in range(2):
        lanes = pl.ds(half * 128, 128)
        index = buckets_ref[:, lanes]
        low = lax.bitwise_and(index, 127)
        high = lax.shift_right_logical(index, 7)
        column = lax.broadcasted_iota(jnp.int32, index.shape, 1) + half * 128
        for head in range(heads):
            total = jnp.full(index.shape, NEGATIVE, F32)
            for part in range(parts):
                values = small_ref[2 + head : 3 + head, part * 128 : (part + 1) * 128]
                values = jnp.broadcast_to(values, index.shape)
                found = jnp.take_along_axis(values, low, axis=1, mode="promise_in_bounds")
                total = jnp.where(high == part, found, total)
            out_ref[head, :, lanes] = jnp.where(column < SEQ, total, NEGATIVE)


def stack_kernel(*refs):
    for i, ref in enumerate(refs[:-1]):
        refs[-1][i] = ref[...]


def start_kernel(w_ref, small_ref, qkv_ref, out_ref, piece_ref, own_ref, sem):
    place = w_ref[0]
    rows = piece_ref.shape[0] - 2 * SMALL
    cut = qkv_ref.shape[0] // rows

    def bring(ref, number):
        copy = pltpu.make_async_copy(
            ref.at[pl.ds(pl.multiple_of(number * rows, rows), rows), :], own_ref, sem
        )
        copy.start()
        copy.wait()

    @pl.when(place < cut)
    def _():
        bring(qkv_ref, place)

    @pl.when(place >= cut)
    def _():
        bring(out_ref, place - cut)

    piece_ref[:rows, :] = own_ref[...]
    small = small_ref[:VECTORS, :]
    upper = small.astype(BF16).astype(F32)
    middle = (small - upper).astype(BF16).astype(F32)
    lower = small - upper - middle
    terms = jnp.concatenate([upper, middle, lower, jnp.zeros((1, small.shape[1]), F32)], axis=0)
    piece_ref[rows:, :] = terms.astype(BF16)


def arrive_kernel(count, *refs):
    came, zero_ref, smalls = refs[:count], refs[count], refs[count + 1 :]
    rows = zero_ref.shape[1]
    for i, ref in enumerate(came):
        zero_ref[i] = ref[:rows, :]
        terms = ref[rows:, :].astype(F32)
        smalls[i][...] = jnp.zeros_like(smalls[i])
        smalls[i][:VECTORS, :] = (
            terms[:VECTORS] + terms[VECTORS : 2 * VECTORS] + terms[2 * VECTORS : 3 * VECTORS]
        )


def cut_kernel(w_ref, in_ref, down_ref, four_ref, *own_refs):
    rows = four_ref.shape[1] // 2
    for k in range(four_ref.shape[0]):
        start = pl.multiple_of(lax.bitwise_xor(w_ref[0], 2 * k) * rows, rows)
        for i, ref in enumerate((in_ref, down_ref)):
            part = ref[pl.ds(start, rows), :]
            four_ref[k, i * rows : (i + 1) * rows, :] = part
            for own_ref in own_refs if k == 0 else ():
                own_ref[i * rows : (i + 1) * rows, :] = part


def put_together(w_ref, pair, slot, cut, target):
    rows = target.shape[0] // PIECES
    for piece in range(PIECES):
        start = pl.multiple_of(lax.bitwise_xor(w_ref[0], piece) * rows, rows)
        target[pl.ds(start, rows), :] = pair[piece & CORE][piece >> 1, slot, cut : cut + rows, :]


def take_apart(w_ref, mats, order, keep, send):
    for number, mat in enumerate(mats):
        rows = mat.shape[0] // PIECES
        for piece in range(PIECES):
            start = pl.multiple_of(lax.bitwise_xor(w_ref[0], piece) * rows, rows)
            target = send if piece & CORE else keep
            target[order[piece >> 1], number] = mat[pl.ds(start, rows), :]


def attend_kernel(slot, first, *refs):
    w_ref = refs[0]
    weights = refs[1:3]
    rest = refs[3:]
    x_ref, small_ref, bias_ref = rest[:3]
    rest = rest[3:]
    if not first:
        acc_in = rest[0]
        rest = rest[1:]
    acc_ref, qkv_ref, probs_ref, mixed_ref = rest[:4]
    if first:
        qkv_mat, out_mat = weights
        width = qkv_mat.shape[1]
        local = width // 4
    else:
        mat = rest[4]
        put_together(w_ref, weights, slot, 0, mat)
        width = mat.shape[0]
        local = width // 4
        qkv_mat, out_mat = mat.at[: 3 * local, :], mat.at[3 * local :, :]
    heads = bias_ref.shape[0]
    size = local // heads
    qkv = mul(x_ref[...], qkv_mat[...], NT)
    queries = qkv[:, :local] + small_ref[0:1, :local]
    queries = (queries.astype(BF16).astype(F32) * size ** (-0.5)).astype(BF16)
    keys = qkv[:, local : 2 * local].astype(BF16)
    values = qkv[:, 2 * local :] + small_ref[0:1, LANES : LANES + local]
    values = values.astype(BF16)
    qkv_ref[0] = queries
    qkv_ref[1] = keys
    qkv_ref[2] = values
    lane = lax.broadcasted_iota(jnp.int32, (PAD, local), 1)
    pages = x_ref.shape[0] // PAD
    zero = jnp.zeros((PAD, local), BF16)
    for page in range(pages):
        rows = slice(page * PAD, (page + 1) * PAD)
        q, k, v = queries[rows], keys[rows], values[rows]
        mixed = jnp.zeros((PAD, local), F32)
        for head in range(heads):
            own = (lane >= head * size) & (lane < (head + 1) * size)
            scores = mul(jnp.where(own, q, zero), k, NT) + bias_ref[head][:, :PAD]
            top = jnp.max(scores, axis=1, keepdims=True)
            power = jnp.exp(scores - top)
            total = jnp.sum(power, axis=1, keepdims=True)
            probs = (power * (1.0 / total)).astype(BF16)
            probs_ref[page * heads + head] = probs
            mixed = mixed + mul(probs, jnp.where(own, v, zero))
        mixed_ref[rows, :] = mixed.astype(BF16)
    out = mul(mixed_ref[...], out_mat[...])
    acc_ref[...] = out if first else acc_in[...] + out


def middle_kernel(acc_ref, tok_ref, mask_ref, grad_ref, vec_ref, mid_ref, x_ref, mg_ref):
    masked = jnp.where(mask_ref[...] > 0.0, row(vec_ref, TOKEN), tok_ref[...].astype(F32))
    middle = masked + row(vec_ref, ATTN_SCALE) * (acc_ref[...] + row(vec_ref, OUT_BIAS))
    mid_ref[...] = middle
    normed, _ = norm_parts(middle)
    x_ref[...] = (normed * row(vec_ref, SECOND_GAIN) + row(vec_ref, SECOND_SHIFT)).astype(BF16)
    mg_ref[...] = (grad_ref[...].astype(F32) * row(vec_ref, MLP_SCALE)).astype(BF16)


def mlp_kernel(first, order, jobs, *refs):
    w_ref = refs[0]
    weights = refs[1:3]
    rest = refs[3:]
    x_ref, mg_ref, small_ref = rest[:3]
    rest = rest[3:]
    if not first:
        out_in, grad_in = rest[:2]
        rest = rest[2:]
    n_jobs = len(jobs.arrays())
    jobs_in, rest = rest[:n_jobs], rest[n_jobs:]
    out_ref, grad_ref, col_ref, keep, send = rest[:5]
    rest = rest[5:]
    n_jobs = len(jobs.outs())
    jobs_out, rest = rest[:n_jobs], rest[n_jobs:]
    in_grad, down_grad = rest[:2]
    if first:
        in_mat, down_mat = weights
    else:
        in_mat, down_mat = rest[2:]
        put_together(w_ref, weights, 0, 0, in_mat)
        put_together(w_ref, weights, 0, in_mat.shape[0] // PIECES, down_mat)
    jobs.add(jobs_in, jobs_out)
    width = in_mat.shape[0]
    x = x_ref[...]
    mg = mg_ref[...]
    out = None
    back = None
    for start in range(0, width, 256):
        units = slice(start, start + 256)
        weight_in = in_mat[:, units]
        weight_down = down_mat[units, :]
        pre = mul(x, weight_in) + small_ref[1:2, units]
        phi = 0.5 * (1.0 + lax.erf(pre * ROOT_HALF))
        hidden = (pre * phi).astype(BF16)
        slope = phi + pre * (DENSITY * jnp.exp(-0.5 * pre * pre))
        part = mul(hidden, weight_down)
        out = part if out is None else out + part
        hidden_grad = mul(mg, weight_down, NT)
        pre_grad = hidden_grad * slope
        low = pre_grad.astype(BF16)
        col_ref[:, units] = col(low.astype(F32))
        part = mul(low, weight_in, NT)
        back = part if back is None else back + part
        down_grad[units, :] = mul(hidden, mg, TN).astype(BF16)
        in_grad[:, units] = mul(x, low, TN).astype(BF16)
    out_ref[...] = out if first else out_in[...] + out
    grad_ref[...] = back if first else grad_in[...] + back
    take_apart(w_ref, [in_grad, down_grad], order, keep, send)


def turn_kernel(jobs, *refs):
    mid_ref, out_ref, back_ref, grad_ref, acc_ref, vec_ref = refs[:6]
    refs = refs[6:]
    n_jobs = len(jobs.arrays())
    jobs_in, refs = refs[:n_jobs], refs[n_jobs:]
    layer_ref, mgrad_ref, ag_ref, sums_ref = refs[:4]
    jobs.add(jobs_in, refs[4:])
    middle = mid_ref[...]
    grad = grad_ref[...].astype(F32)
    mlp_out = out_ref[...] + row(vec_ref, DOWN_BIAS)
    layer_ref[...] = (middle + row(vec_ref, MLP_SCALE) * mlp_out).astype(BF16)
    normed, inverse = norm_parts(middle)
    second = back_ref[...]
    middle_grad = grad + norm_back(second, normed, inverse, row(vec_ref, SECOND_GAIN))
    mgrad_ref[...] = middle_grad
    scaled = middle_grad * row(vec_ref, ATTN_SCALE)
    ag_ref[...] = scaled.astype(BF16)
    sums_ref[0:1, :] = col(scaled)
    sums_ref[1:2, :] = col(middle_grad * (acc_ref[...] + row(vec_ref, OUT_BIAS)))
    sums_ref[2:3, :] = col(second * normed)
    sums_ref[3:4, :] = col(second)
    sums_ref[4:5, :] = col(grad * row(vec_ref, MLP_SCALE))
    sums_ref[5:6, :] = col(grad * mlp_out)
    sums_ref[6:8, :] = jnp.zeros_like(sums_ref[6:8, :])


def attend_back_kernel(own, first, order, second, jobs, *refs):
    w_ref = refs[0]
    if own:
        qkv_mat, out_mat = refs[1:3]
        rest = refs[3:]
    else:
        local = refs[1].shape[0] // 4
        qkv_mat, out_mat = refs[1].at[: 3 * local, :], refs[1].at[3 * local :, :]
        rest = refs[2:]
    x_ref, ag_ref, qkv_ref, probs_ref, mixed_ref = rest[:5]
    rest = rest[5:]
    if not first:
        grad_in = rest[0]
        rest = rest[1:]
    if second:
        other_grad = rest[0]
        rest = rest[1:]
    n_jobs = len(jobs.arrays())
    jobs_in, rest = rest[:n_jobs], rest[n_jobs:]
    grad_ref, col_ref, grid_ref = rest[:3]
    if second:
        keep, send = rest[3:5]
        rest = rest[5:]
    else:
        mat_grad = rest[3]
        rest = rest[4:]
    n_jobs = len(jobs.outs())
    jobs_out, rest = rest[:n_jobs], rest[n_jobs:]
    if second:
        mat_grad, dqkv = rest
    else:
        (dqkv,) = rest
    jobs.add(jobs_in, jobs_out)
    local = out_mat.shape[0]
    heads = grid_ref.shape[0]
    size = local // heads
    ag = ag_ref[...]
    mixed_grad = mul(ag, out_mat[...], NT).astype(BF16)
    mat_grad[3 * local :, :] = mul(mixed_ref[...], ag, TN).astype(BF16)
    lane = lax.broadcasted_iota(jnp.int32, (PAD, local), 1)
    pages = x_ref.shape[0] // PAD
    zero = jnp.zeros((PAD, local), BF16)
    for page in range(pages):
        rows = slice(page * PAD, (page + 1) * PAD)
        q, v, dm = qkv_ref[0, rows, :], qkv_ref[2, rows, :], mixed_grad[rows]
        k = (qkv_ref[1, rows, :].astype(F32) * size ** (-0.5)).astype(BF16)
        dq = jnp.zeros((PAD, local), F32)
        dk = jnp.zeros((PAD, local), F32)
        dv = jnp.zeros((PAD, local), F32)
        for head in range(heads):
            own = (lane >= head * size) & (lane < (head + 1) * size)
            dmh = jnp.where(own, dm, zero)
            probs_low = probs_ref[page * heads + head]
            probs = probs_low.astype(F32)
            weighed = probs * mul(dmh, v, NT)
            score = weighed - probs * jnp.sum(weighed, axis=1, keepdims=True)
            low = score.astype(BF16)
            if page == 0:
                grid_ref[head] = low.astype(F32)
            else:
                grid_ref[head] = grid_ref[head] + low.astype(F32)
            dq = dq + mul(low, jnp.where(own, k, zero))
            dk = dk + mul(low, jnp.where(own, q, zero), TN)
            dv = dv + mul(probs_low, dmh, TN)
        dqkv[rows, :] = jnp.concatenate([dq, dk, dv], axis=1).astype(BF16)
    grads = dqkv[...]
    mat_grad[: 3 * local, :] = mul(grads, x_ref[...], TN).astype(BF16)
    col_ref[...] = col(grads.astype(F32))
    back = mul(grads, qkv_mat[...])
    grad_ref[...] = back if first else grad_in[...] + back
    if second:
        take_apart(w_ref, [other_grad, mat_grad], order, keep, send)


def last_kernel(tok_ref, mask_ref, mgrad_ref, first_ref, vec_ref, grad_ref, sums_ref):
    mask = mask_ref[...] > 0.0
    masked = jnp.where(mask, row(vec_ref, TOKEN), tok_ref[...].astype(F32))
    normed, inverse = norm_parts(masked)
    first = first_ref[...]
    in_grad = mgrad_ref[...] + norm_back(first, normed, inverse, row(vec_ref, FIRST_GAIN))
    grad_ref[...] = jnp.where(mask, 0.0, in_grad).astype(BF16)
    sums_ref[0:1, :] = col(jnp.where(mask, in_grad, 0.0))
    sums_ref[1:2, :] = col(first * normed)
    sums_ref[2:3, :] = col(first)
    sums_ref[3:8, :] = jnp.zeros_like(sums_ref[3:8, :])


def table_kernel(grid_count, begin, end, *refs):
    buckets_ref = refs[0]
    grids = refs[1 : 1 + grid_count]
    out_ref = refs[1 + grid_count]
    heads = grids[0].shape[0]
    highs = out_ref.shape[0] // (grid_count * heads)
    out_ref[...] = jnp.zeros_like(out_ref)

    def step(block, _):
        base = pl.multiple_of(block * 8, 8)
        index = buckets_ref[pl.ds(base, 8), :][:, :PAD]
        loads = [[g[h, pl.ds(base, 8), :] for h in range(heads)] for g in grids]
        total = None
        for row in range(8):
            one = index[row : row + 1]
            low = lax.bitwise_and(one, LOW - 1)
            high = lax.shift_right_logical(one, LOW.bit_length() - 1)
            right = (
                jnp.broadcast_to(low, (LOW, PAD)) == lax.broadcasted_iota(jnp.int32, (LOW, PAD), 0)
            ).astype(F32).astype(BF16)
            match = jnp.broadcast_to(high, (highs, PAD)) == lax.broadcasted_iota(
                jnp.int32, (highs, PAD), 0
            )
            left = jnp.concatenate(
                [
                    jnp.where(match, jnp.broadcast_to(loads[g][h][row : row + 1], (highs, PAD)), 0.0)
                    for g in range(grid_count)
                    for h in range(heads)
                ],
                axis=0,
            ).astype(BF16)
            part = mul(left, right, NT)
            total = part if total is None else total + part
        out_ref[...] += total
        return 0

    lax.fori_loop(begin, end, step, 0)


def sum_kernel(jobs, *refs):
    n_in, n_out = len(jobs.arrays()), len(jobs.outs())
    jobs.add(refs[:n_in], refs[n_in : n_in + n_out])


SHARED = 16
PART = 8


def pack_kernel(count, w_ref, last_ref, mid_ref, table_ref, table_more_ref, *refs):
    qkv_cols, in_cols, out_ref = refs[:count], refs[count : 2 * count], refs[2 * count]
    out_ref[...] = jnp.zeros_like(out_ref)
    out_ref[0:3, :] = last_ref[0:3, :]
    out_ref[3:9, :] = mid_ref[0:6, :]
    tables = table_ref.shape[0] // count
    parts = out_ref.shape[1] // LOW
    for d in range(count):
        base = SHARED + d * PART
        out_ref[base : base + 1, : qkv_cols[d].shape[1]] = qkv_cols[d][...]
        out_ref[base + 1 : base + 2, :] = in_cols[d][...]
        for k in range(tables):
            at = d * tables + k
            lanes = slice(k % parts * LOW, (k % parts + 1) * LOW)
            out_ref[base + 2 + k // parts : base + 3 + k // parts, lanes] = row(table_ref, at) + row(table_more_ref, at)
    held = out_ref[SHARED:, :]
    for d in range(count):
        shard = lax.rem(w_ref[1] + d, count)
        out_ref[pl.ds(pl.multiple_of(SHARED + shard * PART, 8), PART), :] = held[d * PART : (d + 1) * PART]


def leave_kernel(count, w_ref, stay_a, came_a, stay_b, came_b, flat_ref, flat_came, *outs):
    rows = stay_a.shape[2]
    pairs = [(stay_b, came_b, 1), (stay_a, came_a, 0), (stay_a, came_a, 1), (stay_b, came_b, 0)]
    for d in range(count):
        stay, came, slot = pairs[d]
        total = stay[0, slot].astype(F32) + came[0, slot].astype(F32)
        shard = lax.rem(w_ref[1] + d, count)
        at = pl.ds(pl.multiple_of(SHARED + shard * PART, 8), PART)
        small = jnp.concatenate(
            [flat_ref[:SHARED, :] + flat_came[:SHARED, :], flat_ref[at, :] + flat_came[at, :]], axis=0
        )
        if d == 0:
            outs[0][:rows, :] = total
            outs[0][rows:, :] = small
        else:
            upper = small.astype(BF16)
            outs[d][:rows, :] = total.astype(BF16)
            outs[d][rows : rows + SHARED + PART, :] = upper
            outs[d][rows + SHARED + PART :, :] = (small - upper.astype(F32)).astype(BF16)


def home_kernel(own_ref, *refs):
    came, done_ref, small_ref = refs[:-2], refs[-2], refs[-1]
    rows = done_ref.shape[2]
    total = own_ref[:rows, :]
    small = own_ref[rows:, :]
    for ref in came:
        total = total + ref[:rows, :].astype(F32)
        terms = ref[rows:, :].astype(F32)
        small = small + (terms[: SHARED + PART] + terms[SHARED + PART :])
    done_ref[0, 0] = total.astype(BF16)
    small_ref[...] = small


def plus_kernel(left_ref, right_ref, out_ref):
    out_ref[...] = left_ref[...] + right_ref[...]


def assemble(w_ref, pair, number, place_in):
    rows = place_in.shape[0] // PIECES
    for piece in range(PIECES):
        start = pl.multiple_of(lax.bitwise_xor(w_ref[0], piece) * rows, rows)
        place_in[pl.ds(start, rows), :] = pair[piece & CORE][piece >> 1, 0, number].astype(F32)


def mlp_final_kernel(w_ref, own_ref, other_ref, in_ref, down_ref):
    assemble(w_ref, (own_ref, other_ref), 0, in_ref)
    assemble(w_ref, (own_ref, other_ref), 1, down_ref)


def attend_final_kernel(w_ref, own_ref, other_ref, qkv_ref, out_ref, whole):
    assemble(w_ref, (own_ref, other_ref), 0, whole)
    cut = qkv_ref.shape[0]
    qkv_ref[...] = whole[:cut, :]
    out_ref[...] = whole[cut:, :]


SIDE_FIRST = (0, 2, 1, 3)
DEEP_FIRST = (0, 1, 2, 3)


def body(
    tokens,
    page_mask,
    buckets,
    mask_token,
    first_gain,
    first_shift,
    qkv_weight,
    query_bias,
    value_bias,
    position_bias,
    out_weight,
    out_bias,
    attn_scale,
    second_gain,
    second_shift,
    in_weight,
    in_bias,
    down_weight,
    down_bias,
    mlp_scale,
    out_grad,
):
    pages, seq, width = tokens.shape
    count = lax.axis_size("narrow")
    local = qkv_weight.shape[2]
    heads, bucket_count = position_bias.shape
    rows = pages * PAD
    piece_rows = width // PIECES
    place = lax.bitwise_and(lax.axis_index("wide").astype(jnp.int32), PIECES - 1)
    place_ref = jnp.stack([place, lax.axis_index("narrow").astype(jnp.int32)])
    wide_shape = (rows, width)
    line = Line()

    def across(values, bit):
        others = lax.axis_size("wide")
        return lax.ppermute(values, "wide", [(i, i ^ bit) for i in range(others)])

    def along(values, step):
        return lax.ppermute(values, "narrow", [(i, (i + step) % count) for i in range(count)])

    def facing(values, bit):
        return lax.ppermute(values, "narrow", [(i, i ^ bit) for i in range(count)])

    def rest_of_wide(values):
        bit = PIECES
        while bit < lax.axis_size("wide"):
            values = (values.astype(F32) + across(values, bit).astype(F32)).astype(values.dtype)
            bit *= 2
        return values

    def plane(values):
        values = line.gate(values)
        return [values] + [across(values, bit) for bit in (SIDE, DEEP, SIDE | DEEP)]

    def stack(name, arrays, waits=()):
        return line.run(
            stack_kernel, name, [kept((len(arrays),) + arrays[0].shape, BF16)], list(arrays), waits=waits
        )[0]

    vecs = jnp.stack(
        [
            mask_token,
            first_gain,
            first_shift,
            out_bias,
            attn_scale,
            second_gain,
            second_shift,
            mlp_scale,
            down_bias,
        ]
    )
    tables = jnp.pad(position_bias, ((0, SMALL - 2 - heads), (0, width - bucket_count)))
    spare = width - LANES - local
    shifts = jnp.pad(query_bias, (0, width - local)) + jnp.pad(value_bias, (LANES, spare))
    small = jnp.concatenate([shifts[None], in_bias[None], tables], axis=0)
    qkv_own = qkv_weight.transpose(1, 2, 0).reshape(3 * local, width)
    piece = call(
        start_kernel,
        "start",
        [kept((piece_rows + 2 * SMALL, width), BF16)],
        [scalars(), vmem(), anywhere(), anywhere()],
        scratch=[pltpu.VMEM((piece_rows, width), BF16), pltpu.SemaphoreType.DMA],
    )(place_ref, small, qkv_own, out_weight)[0]
    attn_came = [along(piece, -step) for step in range(1, count)]
    smalls = [small]

    fill = ((0, 0), (0, PAD - seq), (0, 0))
    tok = jnp.pad(tokens, fill).reshape(rows, width)
    grad = jnp.pad(out_grad, fill).reshape(rows, width)
    flags = (page_mask > 0) & (jnp.arange(seq, dtype=jnp.int32) % SEQ != 0)
    mask = jnp.pad(flags.astype(F32), ((0, 0), (0, PAD - seq))).reshape(rows, 1)
    index = jnp.pad(buckets, ((0, PAD - seq), (0, LANES - seq)))

    four_mlp, *own_mlp = line.run(
        cut_kernel,
        "cut",
        [kept((4, 2 * piece_rows, width), BF16)] + [kept((2 * piece_rows, width), BF16)] * (count - 2),
        [in_weight, down_weight],
        scalar=place_ref,
    )
    x_one = line.run(
        first_kernel,
        "first",
        [kept(wide_shape, BF16)],
        [tok, mask, vecs],
    )[0]
    biases = []

    def make_bias(d, waits=()):
        biases.append(
            line.run(
                bias_kernel, f"bias{d}", [kept((heads, PAD, LANES), F32)], [index, smalls[d]], waits=waits
            )[0]
        )

    make_bias(0)
    zones = {}
    attn_zero, *others = line.run(
        functools.partial(arrive_kernel, count - 1),
        "arrive",
        [kept((count - 1, piece_rows, width), BF16)] + [kept((SMALL, width), F32)] * (count - 1),
        attn_came,
    )
    smalls += others
    attn_came = plane(attn_zero)
    for step in range(1, count - 1):
        zones[step] = along(line.gate(own_mlp[step - 1]), -step)

    held = []

    def attend(d, acc, weights, waits=()):
        own = d == 0
        made = line.run(
            functools.partial(attend_kernel, d - 1, own),
            f"attend{d}",
            [
                kept(wide_shape, F32),
                kept((3, rows, local), BF16),
                kept((pages * heads, PAD, PAD), BF16),
                kept((rows, local), BF16),
            ]
            + ([] if own else [kept((width, width), BF16)]),
            [*weights, x_one, smalls[d], biases[d]] + ([] if own else [acc]),
            scalar=place_ref,
            waits=waits,
        )
        held.append((weights if own else [made[4]], *made[1:4]))
        return made[0]

    acc = attend(0, None, [qkv_own, out_weight])
    for d in range(1, count - 1):
        make_bias(d)
    attn_four = stack("stack_attn", attn_came, [zones[step] for step in range(1, count - 1)])
    attn_other = across(attn_four, CORE)
    planes = {1: plane(zones[1][None])}
    zones[count - 1] = along(line.gate(four_mlp), -(count - 1))
    make_bias(count - 1)
    for d in range(1, count):
        acc = attend(d, acc, [attn_four, attn_other])

    middle, x_two, mlp_grad = line.run(
        middle_kernel,
        "middle",
        [kept(wide_shape, F32), kept(wide_shape, BF16), kept(wide_shape, BF16)],
        [
            acc,
            tok,
            mask,
            grad,
            vecs,
        ],
    )

    group, bits = {}, {}

    def run_jobs(plan):
        jobs = []
        for step, name in plan:
            counts = {"core": (2, 2), "hop": (1, 1), "fan": (1, 1, 1, 1), "end": (1,)}[step]
            jobs.append((group[name], counts, 2 if step == "end" and name[0] == "a" else 1))
        jobs = Jobs(jobs)

        def store(outs):
            for (step, name), made in zip(plan, jobs.split(outs), strict=True):
                group[name] = made
                hops[name] = hops.get(name, 0) + 1

        return jobs, store

    hops = {}

    def send(*names, after=()):
        leaves = [group[name][1] for name in names]
        if after:
            leaves = line.gate(*leaves, waits=[group[name][1] for name in after])
        for name, leave in zip(names, leaves, strict=True):
            group[name] = [group[name][0], across(leave, bits[name][hops[name] - 1])]

    def sums_of(*plan):
        jobs, store = run_jobs(plan)
        outs = line.run(
            functools.partial(sum_kernel, jobs),
            "sum_" + "_".join(step + name for step, name in plan),
            jobs.outs(),
            jobs.arrays(),
        )
        store(outs)

    def pause(*waits):
        line.run(lambda *refs: None, "pause", [], [], waits=waits)

    mlp_sums = []
    in_cols = [None] * count
    mlp_order = []

    def feed(d, weights, *plan):
        own = d == 0
        name = f"m{len(mlp_order)}"
        side_first = len(mlp_order) % 2 == 0
        mlp_order.append(d)
        bits[name] = (SIDE, DEEP) if side_first else (DEEP, SIDE)
        jobs, store = run_jobs(plan)
        outs = line.run(
            functools.partial(mlp_kernel, own, SIDE_FIRST if side_first else DEEP_FIRST, jobs),
            f"mlp{d}",
            [
                kept(wide_shape, F32),
                kept(wide_shape, F32),
                kept((1, width), F32),
                kept((4, 2, piece_rows, width), BF16),
                kept((4, 2, piece_rows, width), BF16),
            ]
            + jobs.outs(),
            [*weights, x_two, mlp_grad, smalls[d], *mlp_sums, *jobs.arrays()],
            scalar=place_ref,
            scratch=[pltpu.VMEM((width, width), BF16)] * (2 if own else 4),
        )
        mlp_sums[:] = outs[:2]
        in_cols[d] = outs[2]
        store(outs[5:])
        group[name] = [outs[3], across(outs[4], CORE)]

    full = {}
    full[1] = stack("stack1", planes[1])
    full[1] = [full[1], across(full[1], CORE)]
    planes[2] = plane(zones[2][None])
    feed(0, [in_weight, down_weight])
    pause(full[1][1])
    feed(1, full[1], ("core", "m0"))
    last_zone = line.gate(zones[count - 1])
    full[2] = stack("stack2", planes[2], [last_zone])
    full[2] = [full[2], across(full[2], CORE)]
    last_zone = last_zone[:, None]
    full[count - 1] = [last_zone, across(last_zone, CORE)]
    send("m0")
    pause()
    feed(2, full[2], ("core", "m1"))
    send("m1")
    feed(count - 1, full[count - 1])

    jobs, store = run_jobs([("core", "m2")])
    layer, middle_grad, attn_grad, mid_sums, *outs = line.run(
        functools.partial(turn_kernel, jobs),
        "turn",
        [kept(wide_shape, BF16), kept(wide_shape, F32), kept(wide_shape, BF16), kept((8, width), F32)]
        + jobs.outs(),
        [
            middle,
            *mlp_sums,
            grad,
            acc,
            vecs,
            *jobs.arrays(),
        ],
    )
    store(outs)

    back_sum = []
    qkv_cols, grids = [None] * count, [None] * count
    back_order = []
    half = []

    def attend_back(d, *plan):
        second = len(half) == 1
        name = f"a{len(back_order) // 2}"
        side_first = name == "a0"
        first = not back_sum
        back_order.append(d)
        bits[name] = (SIDE, DEEP) if side_first else (DEEP, SIDE)
        jobs, store = run_jobs(plan)
        mats, *others = held[d]
        piece_arrays = [kept((4, 2, piece_rows, width), BF16)] * 2
        outs = line.run(
            functools.partial(attend_back_kernel, d == 0, first, SIDE_FIRST if side_first else DEEP_FIRST, second, jobs),
            f"attend_back{d}",
            [kept(wide_shape, F32), kept((1, 3 * local), F32), kept((heads, PAD, PAD), F32)]
            + (piece_arrays if second else [kept((width, width), BF16)])
            + jobs.outs(),
            [*mats, x_one, attn_grad, *others, *back_sum, *half, *jobs.arrays()],
            scalar=place_ref,
            scratch=[pltpu.VMEM((width, width), BF16)] * second + [pltpu.VMEM((rows, 3 * local), BF16)],
        )
        back_sum[:] = outs[:1]
        qkv_cols[d], grids[d] = outs[1:3]
        store(outs[5 if second else 4 :])
        if second:
            group[name] = [outs[3], across(outs[4], CORE)]
            half.clear()
        else:
            half.append(outs[3])

    attend_back(1)
    pause(group["m0"][1], group["m1"][1])
    sums_of(("core", "m3"))
    send("m2", "m3")
    attend_back(2, ("hop", "m0"), ("hop", "m1"))
    attend_back(3)
    attend_back(0)
    send("m0", "m1", after=("m2", "m3"))

    tok_grad, last_sums = line.run(
        last_kernel,
        "last",
        [kept(wide_shape, BF16), kept((8, width), F32)],
        [tok, mask, middle_grad, *back_sum, vecs],
    )

    highs = width // LOW
    blocks = -(-seq // 8)

    def make_table(begin, end):
        return line.run(
            functools.partial(table_kernel, count, begin, end),
            f"table{begin}",
            [kept((count * heads * highs, LOW), F32)],
            [index, *grids],
        )[0]

    def plus(left, right):
        return line.run(plus_kernel, "plus", [kept(left.shape, left.dtype)], [left, right])[0]

    def come_home(name, pieces):
        jobs = Jobs([([pieces[d] for d in range(count)], (1,), 1)])
        done = line.run(functools.partial(sum_kernel, jobs), name, jobs.outs(), jobs.arrays())[0]
        return rest_of_wide(done)

    sums_of(("hop", "m2"), ("hop", "m3"), ("core", "a0"), ("core", "a1"))
    table = make_table(0, blocks // 2)
    send("m2", "m3", after=("m0", "m1"))
    sums_of(("end", "m0"), ("end", "m1"))
    home = {0: group["m0"][0], 1: along(group["m1"][0], 1)}
    more_table = make_table(blocks // 2, blocks)
    flat = line.run(
        functools.partial(pack_kernel, count),
        "pack",
        [kept((SHARED + count * PART, width), F32)],
        [last_sums, mid_sums, table, more_table, *qkv_cols, *in_cols],
        scalar=place_ref,
        waits=[group["m2"][1], group["m3"][1]],
    )[0]
    other = across(flat, CORE)
    send("a0", "a1", after=("m2", "m3"))
    pause(home[1])
    sums_of(("end", "m2"), ("end", "m3"))
    home[2] = along(group["m2"][0], 2)
    home[3] = along(group["m3"][0], 3)
    flat = rest_of_wide(plus(flat, other))
    other = across(flat, SIDE)

    def rows_first(values):
        return values.reshape(pages, PAD, width)[:, :seq].transpose(1, 0, 2)

    layer_out, tokens_out = rows_first(layer), rows_first(tok_grad)
    pause(layer_out, tokens_out)
    sums_of(("hop", "a0"), ("hop", "a1"))
    send("a0", "a1")
    flat = plus(flat, other)
    other = across(flat, DEEP)
    mlp_home = come_home("home_mlp", home)
    high = piece_rows + 2 * (SHARED + PART)
    own_home, *leaving = line.run(
        functools.partial(leave_kernel, count),
        "leave",
        [kept((piece_rows + SHARED + PART, width), F32)] + [kept((high, width), BF16)] * (count - 1),
        [*group["a0"], *group["a1"], flat, other],
        scalar=place_ref,
    )
    came = [along(leaving[d - 1], d) for d in range(1, count)]
    mlp_side, mlp_deep = across(mlp_home, SIDE), across(mlp_home, DEEP)
    pause()
    attn_home, total = line.run(
        home_kernel,
        "home_attn",
        [kept((1, 1, piece_rows, width), BF16), kept((SHARED + PART, width), F32)],
        [own_home, *came],
    )
    attn_home = rest_of_wide(attn_home)
    attn_came = [attn_home] + [across(attn_home, bit) for bit in (SIDE, DEEP, SIDE | DEEP)]
    mlp_side, mlp_deep = line.gate(mlp_side, mlp_deep)
    mlp_far = across(mlp_side, DEEP)
    pause()
    attn_four = stack("stack_attn_home", attn_came)
    attn_other = across(attn_four, CORE)
    mlp_four = stack("stack_mlp", [mlp_home, mlp_side, mlp_deep, mlp_far])
    mlp_other = across(mlp_four, CORE)
    qkv_w_grad, out_w_grad = final_call(
        attend_final_kernel,
        "attend_final",
        [sent((3 * local, width), F32), sent((local, width), F32)],
        place_ref,
        [attn_four, attn_other],
        line.token,
        scratch=[pltpu.VMEM((width, width), F32)],
    )
    in_w_grad, down_w_grad = final_call(
        mlp_final_kernel, "mlp_final", [sent((width, width), F32)] * 2, place_ref, [mlp_four, mlp_other], line.token
    )

    return (
        layer_out.transpose(1, 0, 2),
        tokens_out.transpose(1, 0, 2),
        total[0],
        total[1],
        total[2],
        qkv_w_grad.reshape(3, local, width).transpose(2, 0, 1),
        total[SHARED, :local],
        total[SHARED, 2 * local : 3 * local],
        total[SHARED + 2 : SHARED + 2 + heads, :bucket_count],
        out_w_grad,
        total[3],
        total[4],
        total[5],
        total[6],
        in_w_grad,
        total[SHARED + 1],
        down_w_grad,
        total[7],
        total[8],
    )


def solution(mesh):
    placed = (
        P(None, ("wide", "narrow"), None),
        P(None, ("wide", "narrow")),
        P(),
        P(),
        P(),
        P(),
        P(None, None, "narrow"),
        P("narrow"),
        P("narrow"),
        P("narrow", None),
        P("narrow", None),
        P(),
        P(),
        P(),
        P(),
        P(None, "narrow"),
        P("narrow"),
        P("narrow", None),
        P(),
        P(),
        P(None, ("wide", "narrow"), None),
    )
    return jax.shard_map(
        body,
        mesh=mesh,
        in_specs=placed,
        out_specs=(
            P(None, ("wide", "narrow"), None),
            P(None, ("wide", "narrow"), None),
            P(),
            P(),
            P(),
            P(None, None, "narrow"),
            P("narrow"),
            P("narrow"),
            P("narrow", None),
            P("narrow", None),
            P(),
            P(),
            P(),
            P(),
            P(None, "narrow"),
            P("narrow"),
            P("narrow", None),
            P(),
            P(),
        ),
        check_vma=False,
    )
```

```python
import functools

import jax
import jax.numpy as jnp
from jax import lax
from jax.experimental import pallas as pl
from jax.experimental.pallas import tpu as pltpu
from jax.sharding import PartitionSpec as P


SEQ = 197
PAD = 208
LANES = 256
EPSILON = 1e-06
ROOT_HALF = 0.7071067811865476
DENSITY = 0.3989422804014327
CORE, SIDE, DEEP = 1, 2, 4
PIECES = 8
LOW = 128
NEGATIVE = -1e30
FLOPS = 2 * 10**10
F32 = jnp.float32
BF16 = jnp.bfloat16

NN = (((1,), (0,)), ((), ()))
NT = (((1,), (1,)), ((), ()))
TN = (((0,), (0,)), ((), ()))


def mul(left, right, dims=NN):
    return lax.dot_general(left, right, dims, preferred_element_type=F32)


def vmem():
    return pl.BlockSpec(memory_space=pltpu.VMEM)


def anywhere():
    return pl.BlockSpec(memory_space=pl.ANY)


def scalars():
    return pl.BlockSpec(memory_space=pltpu.SMEM)


def near(values):
    return pltpu.with_memory_space_constraint(values, pltpu.VMEM)


def kept(shape, dtype):
    return pltpu.VMEM(shape, dtype)


def sent(shape, dtype):
    return jax.ShapeDtypeStruct(shape, dtype)


def call(kernel, name, outs, in_specs, out_specs=None, scratch=(), flops=FLOPS, limit=12, aliases=None):
    made = pl.pallas_call(
        kernel,
        out_shape=outs,
        in_specs=in_specs,
        out_specs=out_specs or [vmem()] * len(outs),
        scratch_shapes=list(scratch),
        input_output_aliases=aliases or {},
        compiler_params=pltpu.CompilerParams(vmem_limit_bytes=limit * 1024 * 1024),
        cost_estimate=pl.CostEstimate(flops=flops, bytes_accessed=0, transcendentals=0),
        name=name,
    )
    return lambda *arrays: made(
        *[near(a) if spec.memory_space == pltpu.VMEM else a for spec, a in zip(in_specs, arrays, strict=True)]
    )


class Line:
    def __init__(self):
        self.token = None

    def run(self, kernel, name, outs, arrays, scalar=None, waits=(), scratch=(), flops=FLOPS, limit=12):
        before = list(waits) + ([] if self.token is None else [self.token])
        start, n_in = (0 if scalar is None else 1), len(arrays)

        def whole(*refs):
            inputs = refs[: start + n_in]
            rest = refs[start + n_in + len(before) :]
            rest[len(outs)][...] = jnp.zeros((8, 128), F32)
            kernel(*inputs, *rest[: len(outs)], *rest[len(outs) + 1 :])

        made = call(
            whole,
            name,
            outs + [kept((8, 128), F32)],
            [scalars()] * start + [vmem()] * n_in + [anywhere()] * len(before),
            scratch=scratch,
            flops=flops,
            limit=limit,
        )(*([] if scalar is None else [scalar]), *arrays, *before)
        self.token = made[-1]
        return made[:-1]

    def gate(self, *arrays, waits=(), place=kept):
        n = len(arrays)
        made = call(
            lambda *refs: None,
            "gate",
            [place(a.shape, a.dtype) for a in arrays],
            [anywhere()] * (n + 1 + len(waits)),
            out_specs=[anywhere()] * n,
            aliases={i: i for i in range(n)},
            flops=0,
        )(*[near(a) if place is kept else a for a in arrays], self.token, *waits)
        return made[0] if n == 1 else made


class Jobs:
    def __init__(self, jobs):
        self.jobs = jobs

    def arrays(self):
        return [a for arrays, _, _ in self.jobs for a in arrays]

    def outs(self):
        made = []
        for arrays, counts, parts in self.jobs:
            _, mats, *rest = arrays[0].shape
            made += [kept((count, mats // parts, *rest), BF16) for count in counts for _ in range(parts)]
        return made

    def add(self, refs_in, refs_out):
        at_in = at_out = 0
        for arrays, counts, parts in self.jobs:
            sources = refs_in[at_in : at_in + len(arrays)]
            at_in += len(arrays)
            mats = arrays[0].shape[1] // parts
            first = 0
            for count in counts:
                for part in range(parts):
                    for i in range(count):
                        for j in range(mats):
                            at = (first + i, part * mats + j)
                            total = sources[0][at].astype(F32)
                            for source in sources[1:]:
                                total = total + source[at].astype(F32)
                            refs_out[at_out][i, j] = total.astype(BF16)
                    at_out += 1
                first += count

    def split(self, outs):
        made, at = [], 0
        for _, counts, parts in self.jobs:
            made.append(list(outs[at : at + len(counts) * parts]))
            at += len(counts) * parts
        return made


def final_call(kernel, name, outs, scalar, arrays, token, scratch=()):
    n_in = 1 + len(arrays)
    return call(
        lambda *refs: kernel(*refs[:n_in], *refs[n_in + 1 :]),
        name,
        outs,
        [scalars()] + [vmem()] * len(arrays) + [anywhere()],
        scratch=scratch,
    )(scalar, *arrays, token)


def norm_parts(values):
    center = values - jnp.mean(values, axis=-1, keepdims=True)
    spread = jnp.mean(center * center, axis=-1, keepdims=True)
    inverse = lax.rsqrt(spread + EPSILON)
    return center * inverse, inverse


def norm_back(grad, normed, inverse, gain):
    scaled = grad * gain
    inner = jnp.mean(scaled, axis=-1, keepdims=True)
    cross = jnp.mean(scaled * normed, axis=-1, keepdims=True)
    return inverse * (scaled - inner - normed * cross)


def col(values):
    return jnp.sum(values, axis=0, keepdims=True)


SMALL = 8
VECTORS = 5


TOKEN, FIRST_GAIN, FIRST_SHIFT, OUT_BIAS, ATTN_SCALE, SECOND_GAIN, SECOND_SHIFT, MLP_SCALE, DOWN_BIAS = range(9)


def row(ref, number):
    return ref[number : number + 1, :]


def first_kernel(tok_ref, mask_ref, vec_ref, out_ref):
    masked = jnp.where(mask_ref[...] > 0.0, row(vec_ref, TOKEN), tok_ref[...].astype(F32))
    normed, _ = norm_parts(masked)
    out = normed * row(vec_ref, FIRST_GAIN) + row(vec_ref, FIRST_SHIFT)
    rows = lax.broadcasted_iota(jnp.int32, (tok_ref.shape[0], 1), 0)
    real = lax.rem(rows, PAD) < SEQ
    out_ref[...] = jnp.where(real, out, 0.0).astype(BF16)


def bias_kernel(buckets_ref, small_ref, out_ref):
    heads = out_ref.shape[0]
    parts = small_ref.shape[1] // 128
    for half in range(2):
        lanes = pl.ds(half * 128, 128)
        index = buckets_ref[:, lanes]
        low = lax.bitwise_and(index, 127)
        high = lax.shift_right_logical(index, 7)
        column = lax.broadcasted_iota(jnp.int32, index.shape, 1) + half * 128
        for head in range(heads):
            total = jnp.full(index.shape, NEGATIVE, F32)
            for part in range(parts):
                values = small_ref[2 + head : 3 + head, part * 128 : (part + 1) * 128]
                values = jnp.broadcast_to(values, index.shape)
                found = jnp.take_along_axis(values, low, axis=1, mode="promise_in_bounds")
                total = jnp.where(high == part, found, total)
            out_ref[head, :, lanes] = jnp.where(column < SEQ, total, NEGATIVE)


def stack_kernel(*refs):
    for i, ref in enumerate(refs[:-1]):
        refs[-1][i] = ref[...]


def start_kernel(w_ref, small_ref, qkv_ref, out_ref, piece_ref, own_ref, sem):
    place = w_ref[0]
    rows = piece_ref.shape[0] - 2 * SMALL
    cut = qkv_ref.shape[0] // rows

    def bring(ref, number):
        copy = pltpu.make_async_copy(
            ref.at[pl.ds(pl.multiple_of(number * rows, rows), rows), :], own_ref, sem
        )
        copy.start()
        copy.wait()

    @pl.when(place < cut)
    def _():
        bring(qkv_ref, place)

    @pl.when(place >= cut)
    def _():
        bring(out_ref, place - cut)

    piece_ref[:rows, :] = own_ref[...]
    small = small_ref[:VECTORS, :]
    upper = small.astype(BF16).astype(F32)
    middle = (small - upper).astype(BF16).astype(F32)
    lower = small - upper - middle
    terms = jnp.concatenate([upper, middle, lower, jnp.zeros((1, small.shape[1]), F32)], axis=0)
    piece_ref[rows:, :] = terms.astype(BF16)


def arrive_kernel(count, *refs):
    came, zero_ref, smalls = refs[:count], refs[count], refs[count + 1 :]
    rows = zero_ref.shape[1]
    for i, ref in enumerate(came):
        zero_ref[i] = ref[:rows, :]
        terms = ref[rows:, :].astype(F32)
        smalls[i][...] = jnp.zeros_like(smalls[i])
        smalls[i][:VECTORS, :] = (
            terms[:VECTORS] + terms[VECTORS : 2 * VECTORS] + terms[2 * VECTORS : 3 * VECTORS]
        )


def cut_kernel(w_ref, in_ref, down_ref, four_ref, *own_refs):
    rows = four_ref.shape[1] // 2
    for k in range(four_ref.shape[0]):
        start = pl.multiple_of(lax.bitwise_xor(w_ref[0], 2 * k) * rows, rows)
        for i, ref in enumerate((in_ref, down_ref)):
            part = ref[pl.ds(start, rows), :]
            four_ref[k, i * rows : (i + 1) * rows, :] = part
            for own_ref in own_refs if k == 0 else ():
                own_ref[i * rows : (i + 1) * rows, :] = part


def put_together(w_ref, pair, slot, cut, target):
    rows = target.shape[0] // PIECES
    for piece in range(PIECES):
        start = pl.multiple_of(lax.bitwise_xor(w_ref[0], piece) * rows, rows)
        target[pl.ds(start, rows), :] = pair[piece & CORE][piece >> 1, slot, cut : cut + rows, :]


def take_apart(w_ref, mats, order, keep, send):
    for number, mat in enumerate(mats):
        rows = mat.shape[0] // PIECES
        for piece in range(PIECES):
            start = pl.multiple_of(lax.bitwise_xor(w_ref[0], piece) * rows, rows)
            target = send if piece & CORE else keep
            target[order[piece >> 1], number] = mat[pl.ds(start, rows), :]


def attend_kernel(slot, first, *refs):
    w_ref = refs[0]
    weights = refs[1:3]
    rest = refs[3:]
    x_ref, small_ref, bias_ref = rest[:3]
    rest = rest[3:]
    if not first:
        acc_in = rest[0]
        rest = rest[1:]
    acc_ref, qkv_ref, probs_ref, mixed_ref = rest[:4]
    if first:
        qkv_mat, out_mat = weights
        width = qkv_mat.shape[1]
        local = width // 4
    else:
        mat = rest[4]
        put_together(w_ref, weights, slot, 0, mat)
        width = mat.shape[0]
        local = width // 4
        qkv_mat, out_mat = mat.at[: 3 * local, :], mat.at[3 * local :, :]
    heads = bias_ref.shape[0]
    size = local // heads
    qkv = mul(x_ref[...], qkv_mat[...], NT)
    queries = qkv[:, :local] + small_ref[0:1, :local]
    queries = (queries.astype(BF16).astype(F32) * size ** (-0.5)).astype(BF16)
    keys = qkv[:, local : 2 * local].astype(BF16)
    values = qkv[:, 2 * local :] + small_ref[0:1, LANES : LANES + local]
    values = values.astype(BF16)
    qkv_ref[0] = queries
    qkv_ref[1] = keys
    qkv_ref[2] = values
    lane = lax.broadcasted_iota(jnp.int32, (PAD, local), 1)
    pages = x_ref.shape[0] // PAD
    zero = jnp.zeros((PAD, local), BF16)
    for page in range(pages):
        rows = slice(page * PAD, (page + 1) * PAD)
        q, k, v = queries[rows], keys[rows], values[rows]
        mixed = jnp.zeros((PAD, local), F32)
        for head in range(heads):
            own = (lane >= head * size) & (lane < (head + 1) * size)
            scores = mul(jnp.where(own, q, zero), k, NT) + bias_ref[head][:, :PAD]
            top = jnp.max(scores, axis=1, keepdims=True)
            power = jnp.exp(scores - top)
            total = jnp.sum(power, axis=1, keepdims=True)
            probs = (power * (1.0 / total)).astype(BF16)
            probs_ref[page * heads + head] = probs
            mixed = mixed + mul(probs, jnp.where(own, v, zero))
        mixed_ref[rows, :] = mixed.astype(BF16)
    out = mul(mixed_ref[...], out_mat[...])
    acc_ref[...] = out if first else acc_in[...] + out


def middle_kernel(acc_ref, tok_ref, mask_ref, grad_ref, vec_ref, mid_ref, x_ref, mg_ref):
    masked = jnp.where(mask_ref[...] > 0.0, row(vec_ref, TOKEN), tok_ref[...].astype(F32))
    middle = masked + row(vec_ref, ATTN_SCALE) * (acc_ref[...] + row(vec_ref, OUT_BIAS))
    mid_ref[...] = middle
    normed, _ = norm_parts(middle)
    x_ref[...] = (normed * row(vec_ref, SECOND_GAIN) + row(vec_ref, SECOND_SHIFT)).astype(BF16)
    mg_ref[...] = (grad_ref[...].astype(F32) * row(vec_ref, MLP_SCALE)).astype(BF16)


def mlp_kernel(first, order, jobs, *refs):
    w_ref = refs[0]
    weights = refs[1:3]
    rest = refs[3:]
    x_ref, mg_ref, small_ref = rest[:3]
    rest = rest[3:]
    if not first:
        out_in, grad_in = rest[:2]
        rest = rest[2:]
    n_jobs = len(jobs.arrays())
    jobs_in, rest = rest[:n_jobs], rest[n_jobs:]
    out_ref, grad_ref, col_ref, keep, send = rest[:5]
    rest = rest[5:]
    n_jobs = len(jobs.outs())
    jobs_out, rest = rest[:n_jobs], rest[n_jobs:]
    in_grad, down_grad = rest[:2]
    if first:
        in_mat, down_mat = weights
    else:
        in_mat, down_mat = rest[2:]
        put_together(w_ref, weights, 0, 0, in_mat)
        put_together(w_ref, weights, 0, in_mat.shape[0] // PIECES, down_mat)
    jobs.add(jobs_in, jobs_out)
    width = in_mat.shape[0]
    x = x_ref[...]
    mg = mg_ref[...]
    out = None
    back = None
    for start in range(0, width, 256):
        units = slice(start, start + 256)
        weight_in = in_mat[:, units]
        weight_down = down_mat[units, :]
        pre = mul(x, weight_in) + small_ref[1:2, units]
        phi = 0.5 * (1.0 + lax.erf(pre * ROOT_HALF))
        hidden = (pre * phi).astype(BF16)
        slope = phi + pre * (DENSITY * jnp.exp(-0.5 * pre * pre))
        part = mul(hidden, weight_down)
        out = part if out is None else out + part
        hidden_grad = mul(mg, weight_down, NT)
        pre_grad = hidden_grad * slope
        low = pre_grad.astype(BF16)
        col_ref[:, units] = col(low.astype(F32))
        part = mul(low, weight_in, NT)
        back = part if back is None else back + part
        down_grad[units, :] = mul(hidden, mg, TN).astype(BF16)
        in_grad[:, units] = mul(x, low, TN).astype(BF16)
    out_ref[...] = out if first else out_in[...] + out
    grad_ref[...] = back if first else grad_in[...] + back
    take_apart(w_ref, [in_grad, down_grad], order, keep, send)


def turn_kernel(jobs, *refs):
    mid_ref, out_ref, back_ref, grad_ref, acc_ref, vec_ref = refs[:6]
    refs = refs[6:]
    n_jobs = len(jobs.arrays())
    jobs_in, refs = refs[:n_jobs], refs[n_jobs:]
    layer_ref, mgrad_ref, ag_ref, sums_ref = refs[:4]
    jobs.add(jobs_in, refs[4:])
    middle = mid_ref[...]
    grad = grad_ref[...].astype(F32)
    mlp_out = out_ref[...] + row(vec_ref, DOWN_BIAS)
    layer_ref[...] = (middle + row(vec_ref, MLP_SCALE) * mlp_out).astype(BF16)
    normed, inverse = norm_parts(middle)
    second = back_ref[...]
    middle_grad = grad + norm_back(second, normed, inverse, row(vec_ref, SECOND_GAIN))
    mgrad_ref[...] = middle_grad
    scaled = middle_grad * row(vec_ref, ATTN_SCALE)
    ag_ref[...] = scaled.astype(BF16)
    sums_ref[0:1, :] = col(scaled)
    sums_ref[1:2, :] = col(middle_grad * (acc_ref[...] + row(vec_ref, OUT_BIAS)))
    sums_ref[2:3, :] = col(second * normed)
    sums_ref[3:4, :] = col(second)
    sums_ref[4:5, :] = col(grad * row(vec_ref, MLP_SCALE))
    sums_ref[5:6, :] = col(grad * mlp_out)
    sums_ref[6:8, :] = jnp.zeros_like(sums_ref[6:8, :])


def attend_back_kernel(own, first, order, second, jobs, *refs):
    w_ref = refs[0]
    if own:
        qkv_mat, out_mat = refs[1:3]
        rest = refs[3:]
    else:
        local = refs[1].shape[0] // 4
        qkv_mat, out_mat = refs[1].at[: 3 * local, :], refs[1].at[3 * local :, :]
        rest = refs[2:]
    x_ref, ag_ref, qkv_ref, probs_ref, mixed_ref = rest[:5]
    rest = rest[5:]
    if not first:
        grad_in = rest[0]
        rest = rest[1:]
    if second:
        other_grad = rest[0]
        rest = rest[1:]
    n_jobs = len(jobs.arrays())
    jobs_in, rest = rest[:n_jobs], rest[n_jobs:]
    grad_ref, col_ref, grid_ref = rest[:3]
    if second:
        keep, send = rest[3:5]
        rest = rest[5:]
    else:
        mat_grad = rest[3]
        rest = rest[4:]
    n_jobs = len(jobs.outs())
    jobs_out, rest = rest[:n_jobs], rest[n_jobs:]
    if second:
        mat_grad, dqkv = rest
    else:
        (dqkv,) = rest
    jobs.add(jobs_in, jobs_out)
    local = out_mat.shape[0]
    heads = grid_ref.shape[0]
    size = local // heads
    ag = ag_ref[...]
    mixed_grad = mul(ag, out_mat[...], NT).astype(BF16)
    mat_grad[3 * local :, :] = mul(mixed_ref[...], ag, TN).astype(BF16)
    lane = lax.broadcasted_iota(jnp.int32, (PAD, local), 1)
    pages = x_ref.shape[0] // PAD
    zero = jnp.zeros((PAD, local), BF16)
    for page in range(pages):
        rows = slice(page * PAD, (page + 1) * PAD)
        q, v, dm = qkv_ref[0, rows, :], qkv_ref[2, rows, :], mixed_grad[rows]
        k = (qkv_ref[1, rows, :].astype(F32) * size ** (-0.5)).astype(BF16)
        dq = jnp.zeros((PAD, local), F32)
        dk = jnp.zeros((PAD, local), F32)
        dv = jnp.zeros((PAD, local), F32)
        for head in range(heads):
            own = (lane >= head * size) & (lane < (head + 1) * size)
            dmh = jnp.where(own, dm, zero)
            probs_low = probs_ref[page * heads + head]
            probs = probs_low.astype(F32)
            weighed = probs * mul(dmh, v, NT)
            score = weighed - probs * jnp.sum(weighed, axis=1, keepdims=True)
            low = score.astype(BF16)
            if page == 0:
                grid_ref[head] = low.astype(F32)
            else:
                grid_ref[head] = grid_ref[head] + low.astype(F32)
            dq = dq + mul(low, jnp.where(own, k, zero))
            dk = dk + mul(low, jnp.where(own, q, zero), TN)
            dv = dv + mul(probs_low, dmh, TN)
        dqkv[rows, :] = jnp.concatenate([dq, dk, dv], axis=1).astype(BF16)
    grads = dqkv[...]
    mat_grad[: 3 * local, :] = mul(grads, x_ref[...], TN).astype(BF16)
    col_ref[...] = col(grads.astype(F32))
    back = mul(grads, qkv_mat[...])
    grad_ref[...] = back if first else grad_in[...] + back
    if second:
        take_apart(w_ref, [other_grad, mat_grad], order, keep, send)


def last_kernel(tok_ref, mask_ref, mgrad_ref, first_ref, vec_ref, grad_ref, sums_ref):
    mask = mask_ref[...] > 0.0
    masked = jnp.where(mask, row(vec_ref, TOKEN), tok_ref[...].astype(F32))
    normed, inverse = norm_parts(masked)
    first = first_ref[...]
    in_grad = mgrad_ref[...] + norm_back(first, normed, inverse, row(vec_ref, FIRST_GAIN))
    grad_ref[...] = jnp.where(mask, 0.0, in_grad).astype(BF16)
    sums_ref[0:1, :] = col(jnp.where(mask, in_grad, 0.0))
    sums_ref[1:2, :] = col(first * normed)
    sums_ref[2:3, :] = col(first)
    sums_ref[3:8, :] = jnp.zeros_like(sums_ref[3:8, :])


def table_kernel(grid_count, begin, end, *refs):
    buckets_ref = refs[0]
    grids = refs[1 : 1 + grid_count]
    out_ref = refs[1 + grid_count]
    heads = grids[0].shape[0]
    highs = out_ref.shape[0] // (grid_count * heads)
    out_ref[...] = jnp.zeros_like(out_ref)

    def step(block, _):
        base = pl.multiple_of(block * 8, 8)
        index = buckets_ref[pl.ds(base, 8), :][:, :PAD]
        loads = [[g[h, pl.ds(base, 8), :] for h in range(heads)] for g in grids]
        total = None
        for row in range(8):
            one = index[row : row + 1]
            low = lax.bitwise_and(one, LOW - 1)
            high = lax.shift_right_logical(one, LOW.bit_length() - 1)
            right = (
                jnp.broadcast_to(low, (LOW, PAD)) == lax.broadcasted_iota(jnp.int32, (LOW, PAD), 0)
            ).astype(F32).astype(BF16)
            match = jnp.broadcast_to(high, (highs, PAD)) == lax.broadcasted_iota(
                jnp.int32, (highs, PAD), 0
            )
            left = jnp.concatenate(
                [
                    jnp.where(match, jnp.broadcast_to(loads[g][h][row : row + 1], (highs, PAD)), 0.0)
                    for g in range(grid_count)
                    for h in range(heads)
                ],
                axis=0,
            ).astype(BF16)
            part = mul(left, right, NT)
            total = part if total is None else total + part
        out_ref[...] += total
        return 0

    lax.fori_loop(begin, end, step, 0)


def sum_kernel(jobs, *refs):
    n_in, n_out = len(jobs.arrays()), len(jobs.outs())
    jobs.add(refs[:n_in], refs[n_in : n_in + n_out])


SHARED = 16
PART = 8


def pack_kernel(count, w_ref, last_ref, mid_ref, table_ref, table_more_ref, *refs):
    qkv_cols, in_cols, out_ref = refs[:count], refs[count : 2 * count], refs[2 * count]
    out_ref[...] = jnp.zeros_like(out_ref)
    out_ref[0:3, :] = last_ref[0:3, :]
    out_ref[3:9, :] = mid_ref[0:6, :]
    tables = table_ref.shape[0] // count
    parts = out_ref.shape[1] // LOW
    for d in range(count):
        base = SHARED + d * PART
        out_ref[base : base + 1, : qkv_cols[d].shape[1]] = qkv_cols[d][...]
        out_ref[base + 1 : base + 2, :] = in_cols[d][...]
        for k in range(tables):
            at = d * tables + k
            lanes = slice(k % parts * LOW, (k % parts + 1) * LOW)
            out_ref[base + 2 + k // parts : base + 3 + k // parts, lanes] = row(table_ref, at) + row(table_more_ref, at)
    held = out_ref[SHARED:, :]
    for d in range(count):
        shard = lax.rem(w_ref[1] + d, count)
        out_ref[pl.ds(pl.multiple_of(SHARED + shard * PART, 8), PART), :] = held[d * PART : (d + 1) * PART]


def leave_kernel(count, w_ref, stay_a, came_a, stay_b, came_b, flat_ref, flat_came, *outs):
    rows = stay_a.shape[2]
    pairs = [(stay_b, came_b, 1), (stay_a, came_a, 0), (stay_a, came_a, 1), (stay_b, came_b, 0)]
    for d in range(count):
        stay, came, slot = pairs[d]
        total = stay[0, slot].astype(F32) + came[0, slot].astype(F32)
        shard = lax.rem(w_ref[1] + d, count)
        at = pl.ds(pl.multiple_of(SHARED + shard * PART, 8), PART)
        small = jnp.concatenate(
            [flat_ref[:SHARED, :] + flat_came[:SHARED, :], flat_ref[at, :] + flat_came[at, :]], axis=0
        )
        if d == 0:
            outs[0][:rows, :] = total
            outs[0][rows:, :] = small
        else:
            outs[d][:rows, :] = total.astype(BF16)
            outs[d][rows:, :] = jnp.concatenate(
                [small[:9], small[SHARED : SHARED + 5], jnp.zeros((2, small.shape[1]), F32)], axis=0
            ).astype(BF16)


def home_kernel(own_ref, *refs):
    came, done_ref, small_ref = refs[:-2], refs[-2], refs[-1]
    rows = done_ref.shape[2]
    total = own_ref[:rows, :]
    small = own_ref[rows:, :]
    for ref in came:
        total = total + ref[:rows, :].astype(F32)
        sent_rows = ref[rows:, :].astype(F32)
        small = small + jnp.concatenate(
            [
                sent_rows[:9],
                jnp.zeros((SHARED - 9, small.shape[1]), F32),
                sent_rows[9:14],
                jnp.zeros((PART - 5, small.shape[1]), F32),
            ],
            axis=0,
        )
    done_ref[0, 0] = total.astype(BF16)
    small_ref[...] = small


def plus_kernel(left_ref, right_ref, out_ref):
    out_ref[...] = left_ref[...] + right_ref[...]


def assemble(w_ref, pair, number, place_in):
    rows = place_in.shape[0] // PIECES
    for piece in range(PIECES):
        start = pl.multiple_of(lax.bitwise_xor(w_ref[0], piece) * rows, rows)
        place_in[pl.ds(start, rows), :] = pair[piece & CORE][piece >> 1, 0, number].astype(F32)


def mlp_final_kernel(w_ref, own_ref, other_ref, in_ref, down_ref):
    assemble(w_ref, (own_ref, other_ref), 0, in_ref)
    assemble(w_ref, (own_ref, other_ref), 1, down_ref)


def attend_final_kernel(w_ref, own_ref, other_ref, qkv_ref, out_ref, whole):
    assemble(w_ref, (own_ref, other_ref), 0, whole)
    cut = qkv_ref.shape[0]
    qkv_ref[...] = whole[:cut, :]
    out_ref[...] = whole[cut:, :]


SIDE_FIRST = (0, 2, 1, 3)
DEEP_FIRST = (0, 1, 2, 3)


def body(
    tokens,
    page_mask,
    buckets,
    mask_token,
    first_gain,
    first_shift,
    qkv_weight,
    query_bias,
    value_bias,
    position_bias,
    out_weight,
    out_bias,
    attn_scale,
    second_gain,
    second_shift,
    in_weight,
    in_bias,
    down_weight,
    down_bias,
    mlp_scale,
    out_grad,
):
    pages, seq, width = tokens.shape
    count = lax.axis_size("narrow")
    local = qkv_weight.shape[2]
    heads, bucket_count = position_bias.shape
    rows = pages * PAD
    piece_rows = width // PIECES
    place = lax.bitwise_and(lax.axis_index("wide").astype(jnp.int32), PIECES - 1)
    place_ref = jnp.stack([place, lax.axis_index("narrow").astype(jnp.int32)])
    wide_shape = (rows, width)
    line = Line()

    def across(values, bit):
        others = lax.axis_size("wide")
        return lax.ppermute(values, "wide", [(i, i ^ bit) for i in range(others)])

    def along(values, step):
        return lax.ppermute(values, "narrow", [(i, (i + step) % count) for i in range(count)])

    def facing(values, bit):
        return lax.ppermute(values, "narrow", [(i, i ^ bit) for i in range(count)])

    def rest_of_wide(values):
        bit = PIECES
        while bit < lax.axis_size("wide"):
            values = (values.astype(F32) + across(values, bit).astype(F32)).astype(values.dtype)
            bit *= 2
        return values

    def plane(values):
        values = line.gate(values)
        return [values] + [across(values, bit) for bit in (SIDE, DEEP, SIDE | DEEP)]

    def stack(name, arrays, waits=()):
        return line.run(
            stack_kernel, name, [kept((len(arrays),) + arrays[0].shape, BF16)], list(arrays), waits=waits
        )[0]

    vecs = jnp.stack(
        [
            mask_token,
            first_gain,
            first_shift,
            out_bias,
            attn_scale,
            second_gain,
            second_shift,
            mlp_scale,
            down_bias,
        ]
    )
    tables = jnp.pad(position_bias, ((0, SMALL - 2 - heads), (0, width - bucket_count)))
    spare = width - LANES - local
    shifts = jnp.pad(query_bias, (0, width - local)) + jnp.pad(value_bias, (LANES, spare))
    small = jnp.concatenate([shifts[None], in_bias[None], tables], axis=0)
    qkv_own = qkv_weight.transpose(1, 2, 0).reshape(3 * local, width)
    piece = call(
        start_kernel,
        "start",
        [kept((piece_rows + 2 * SMALL, width), BF16)],
        [scalars(), vmem(), anywhere(), anywhere()],
        scratch=[pltpu.VMEM((piece_rows, width), BF16), pltpu.SemaphoreType.DMA],
    )(place_ref, small, qkv_own, out_weight)[0]
    attn_came = [along(piece, -step) for step in range(1, count)]
    smalls = [small]

    fill = ((0, 0), (0, PAD - seq), (0, 0))
    tok = jnp.pad(tokens, fill).reshape(rows, width)
    grad = jnp.pad(out_grad, fill).reshape(rows, width)
    flags = (page_mask > 0) & (jnp.arange(seq, dtype=jnp.int32) % SEQ != 0)
    mask = jnp.pad(flags.astype(F32), ((0, 0), (0, PAD - seq))).reshape(rows, 1)
    index = jnp.pad(buckets, ((0, PAD - seq), (0, LANES - seq)))

    four_mlp, *own_mlp = line.run(
        cut_kernel,
        "cut",
        [kept((4, 2 * piece_rows, width), BF16)] + [kept((2 * piece_rows, width), BF16)] * (count - 2),
        [in_weight, down_weight],
        scalar=place_ref,
    )
    x_one = line.run(
        first_kernel,
        "first",
        [kept(wide_shape, BF16)],
        [tok, mask, vecs],
    )[0]
    biases = []

    def make_bias(d, waits=()):
        biases.append(
            line.run(
                bias_kernel, f"bias{d}", [kept((heads, PAD, LANES), F32)], [index, smalls[d]], waits=waits
            )[0]
        )

    make_bias(0)
    zones = {}
    attn_zero, *others = line.run(
        functools.partial(arrive_kernel, count - 1),
        "arrive",
        [kept((count - 1, piece_rows, width), BF16)] + [kept((SMALL, width), F32)] * (count - 1),
        attn_came,
    )
    smalls += others
    attn_came = plane(attn_zero)
    for step in range(1, count - 1):
        zones[step] = along(line.gate(own_mlp[step - 1]), -step)

    held = []

    def attend(d, acc, weights, waits=()):
        own = d == 0
        made = line.run(
            functools.partial(attend_kernel, d - 1, own),
            f"attend{d}",
            [
                kept(wide_shape, F32),
                kept((3, rows, local), BF16),
                kept((pages * heads, PAD, PAD), BF16),
                kept((rows, local), BF16),
            ]
            + ([] if own else [kept((width, width), BF16)]),
            [*weights, x_one, smalls[d], biases[d]] + ([] if own else [acc]),
            scalar=place_ref,
            waits=waits,
        )
        held.append((weights if own else [made[4]], *made[1:4]))
        return made[0]

    acc = attend(0, None, [qkv_own, out_weight])
    for d in range(1, count - 1):
        make_bias(d)
    attn_four = stack("stack_attn", attn_came, [zones[step] for step in range(1, count - 1)])
    attn_other = across(attn_four, CORE)
    planes = {1: plane(zones[1][None])}
    zones[count - 1] = along(line.gate(four_mlp), -(count - 1))
    make_bias(count - 1)
    for d in range(1, count):
        acc = attend(d, acc, [attn_four, attn_other])

    middle, x_two, mlp_grad = line.run(
        middle_kernel,
        "middle",
        [kept(wide_shape, F32), kept(wide_shape, BF16), kept(wide_shape, BF16)],
        [
            acc,
            tok,
            mask,
            grad,
            vecs,
        ],
    )

    group, bits = {}, {}

    def run_jobs(plan):
        jobs = []
        for step, name in plan:
            counts = {"core": (2, 2), "hop": (1, 1), "fan": (1, 1, 1, 1), "end": (1,)}[step]
            jobs.append((group[name], counts, 2 if step == "end" and name[0] == "a" else 1))
        jobs = Jobs(jobs)

        def store(outs):
            for (step, name), made in zip(plan, jobs.split(outs), strict=True):
                group[name] = made
                hops[name] = hops.get(name, 0) + 1

        return jobs, store

    hops = {}

    def send(*names, after=()):
        leaves = [group[name][1] for name in names]
        if after:
            leaves = line.gate(*leaves, waits=[group[name][1] for name in after])
        for name, leave in zip(names, leaves, strict=True):
            group[name] = [group[name][0], across(leave, bits[name][hops[name] - 1])]

    def sums_of(*plan):
        jobs, store = run_jobs(plan)
        outs = line.run(
            functools.partial(sum_kernel, jobs),
            "sum_" + "_".join(step + name for step, name in plan),
            jobs.outs(),
            jobs.arrays(),
        )
        store(outs)

    def pause(*waits):
        line.run(lambda *refs: None, "pause", [], [], waits=waits)

    mlp_sums = []
    in_cols = [None] * count
    mlp_order = []

    def feed(d, weights, *plan):
        own = d == 0
        name = f"m{len(mlp_order)}"
        side_first = len(mlp_order) % 2 == 0
        mlp_order.append(d)
        bits[name] = (SIDE, DEEP) if side_first else (DEEP, SIDE)
        jobs, store = run_jobs(plan)
        outs = line.run(
            functools.partial(mlp_kernel, own, SIDE_FIRST if side_first else DEEP_FIRST, jobs),
            f"mlp{d}",
            [
                kept(wide_shape, F32),
                kept(wide_shape, F32),
                kept((1, width), F32),
                kept((4, 2, piece_rows, width), BF16),
                kept((4, 2, piece_rows, width), BF16),
            ]
            + jobs.outs(),
            [*weights, x_two, mlp_grad, smalls[d], *mlp_sums, *jobs.arrays()],
            scalar=place_ref,
            scratch=[pltpu.VMEM((width, width), BF16)] * (2 if own else 4),
        )
        mlp_sums[:] = outs[:2]
        in_cols[d] = outs[2]
        store(outs[5:])
        group[name] = [outs[3], across(outs[4], CORE)]

    full = {}
    full[1] = stack("stack1", planes[1])
    full[1] = [full[1], across(full[1], CORE)]
    planes[2] = plane(zones[2][None])
    feed(0, [in_weight, down_weight])
    pause(full[1][1])
    feed(1, full[1], ("core", "m0"))
    last_zone = line.gate(zones[count - 1])
    full[2] = stack("stack2", planes[2], [last_zone])
    full[2] = [full[2], across(full[2], CORE)]
    last_zone = last_zone[:, None]
    full[count - 1] = [last_zone, across(last_zone, CORE)]
    send("m0")
    sums_of(("core", "m1"))
    send("m1")
    feed(2, full[2])
    feed(count - 1, full[count - 1])

    jobs, store = run_jobs([])
    layer, middle_grad, attn_grad, mid_sums, *outs = line.run(
        functools.partial(turn_kernel, jobs),
        "turn",
        [kept(wide_shape, BF16), kept(wide_shape, F32), kept(wide_shape, BF16), kept((8, width), F32)]
        + jobs.outs(),
        [
            middle,
            *mlp_sums,
            grad,
            acc,
            vecs,
            *jobs.arrays(),
        ],
    )
    store(outs)

    back_sum = []
    qkv_cols, grids = [None] * count, [None] * count
    back_order = []
    half = []

    def attend_back(d, *plan):
        second = len(half) == 1
        name = f"a{len(back_order) // 2}"
        side_first = name == "a0"
        first = not back_sum
        back_order.append(d)
        bits[name] = (SIDE, DEEP) if side_first else (DEEP, SIDE)
        jobs, store = run_jobs(plan)
        mats, *others = held[d]
        piece_arrays = [kept((4, 2, piece_rows, width), BF16)] * 2
        outs = line.run(
            functools.partial(attend_back_kernel, d == 0, first, SIDE_FIRST if side_first else DEEP_FIRST, second, jobs),
            f"attend_back{d}",
            [kept(wide_shape, F32), kept((1, 3 * local), F32), kept((heads, PAD, PAD), F32)]
            + (piece_arrays if second else [kept((width, width), BF16)])
            + jobs.outs(),
            [*mats, x_one, attn_grad, *others, *back_sum, *half, *jobs.arrays()],
            scalar=place_ref,
            scratch=[pltpu.VMEM((width, width), BF16)] * second + [pltpu.VMEM((rows, 3 * local), BF16)],
        )
        back_sum[:] = outs[:1]
        qkv_cols[d], grids[d] = outs[1:3]
        store(outs[5 if second else 4 :])
        if second:
            group[name] = [outs[3], across(outs[4], CORE)]
            half.clear()
        else:
            half.append(outs[3])

    pause(group["m0"][1], group["m1"][1])
    sums_of(("core", "m2"), ("core", "m3"))
    send("m2", "m3")
    attend_back(1, ("hop", "m0"), ("hop", "m1"))
    attend_back(2)
    attend_back(3)
    send("m0", "m1", after=("m2", "m3"))
    attend_back(0, ("hop", "m2"), ("hop", "m3"), ("core", "a0"))

    tok_grad, last_sums = line.run(
        last_kernel,
        "last",
        [kept(wide_shape, BF16), kept((8, width), F32)],
        [tok, mask, middle_grad, *back_sum, vecs],
    )
    send("m2", "m3", after=("m0", "m1"))

    highs = width // LOW
    blocks = -(-seq // 8)

    def make_table(begin, end):
        return line.run(
            functools.partial(table_kernel, count, begin, end),
            f"table{begin}",
            [kept((count * heads * highs, LOW), F32)],
            [index, *grids],
        )[0]

    def plus(left, right):
        return line.run(plus_kernel, "plus", [kept(left.shape, left.dtype)], [left, right])[0]

    def come_home(name, pieces):
        jobs = Jobs([([pieces[d] for d in range(count)], (1,), 1)])
        done = line.run(functools.partial(sum_kernel, jobs), name, jobs.outs(), jobs.arrays())[0]
        return rest_of_wide(done)

    sums_of(("end", "m0"), ("end", "m1"), ("core", "a1"))
    home = {0: group["m0"][0], 1: along(group["m1"][0], 1)}
    table = make_table(0, blocks // 2)
    more_table = make_table(blocks // 2, blocks)
    flat = line.run(
        functools.partial(pack_kernel, count),
        "pack",
        [kept((SHARED + count * PART, width), F32)],
        [last_sums, mid_sums, table, more_table, *qkv_cols, *in_cols],
        scalar=place_ref,
        waits=[group["m2"][1], group["m3"][1]],
    )[0]
    other = across(flat, CORE)
    send("a0", "a1", after=("m2", "m3"))
    pause(home[1])
    sums_of(("end", "m2"), ("end", "m3"))
    home[2] = along(group["m2"][0], 2)
    home[3] = along(group["m3"][0], 3)
    flat = rest_of_wide(plus(flat, other))
    other = across(flat, SIDE)

    def rows_first(values):
        values = line.gate(values)
        return values.reshape(pages, PAD, width)[:, :seq].transpose(1, 0, 2)

    layer_out, tokens_out = line.gate(rows_first(layer), rows_first(tok_grad), place=sent)
    pause(layer_out, tokens_out)
    sums_of(("hop", "a0"), ("hop", "a1"))
    send("a0", "a1")
    flat = plus(flat, other)
    other = across(flat, DEEP)
    mlp_home = come_home("home_mlp", home)
    mlp_side, mlp_deep = across(mlp_home, SIDE), across(mlp_home, DEEP)
    own_home, *leaving = line.run(
        functools.partial(leave_kernel, count),
        "leave",
        [kept((piece_rows + SHARED + PART, width), F32)]
        + [kept((piece_rows + 16, width), BF16)] * (count - 1),
        [*group["a0"], *group["a1"], flat, other],
        scalar=place_ref,
    )
    came = [along(leaving[d - 1], d) for d in range(1, count)]
    pause()
    mlp_side, mlp_deep = line.gate(mlp_side, mlp_deep)
    mlp_far = across(mlp_side, DEEP)
    pause()
    attn_home, total = line.run(
        home_kernel,
        "home_attn",
        [kept((1, 1, piece_rows, width), BF16), kept((SHARED + PART, width), F32)],
        [own_home, *came],
    )
    attn_home = rest_of_wide(attn_home)
    attn_came = [attn_home] + [across(attn_home, bit) for bit in (SIDE, DEEP, SIDE | DEEP)]
    mlp_four = stack("stack_mlp", [mlp_home, mlp_side, mlp_deep, mlp_far])
    mlp_other = across(mlp_four, CORE)
    pause()
    in_w_grad, down_w_grad = line.run(
        mlp_final_kernel,
        "mlp_final",
        [sent((width, width), F32)] * 2,
        [mlp_four, mlp_other],
        scalar=place_ref,
    )
    attn_four = stack("stack_attn_home", attn_came)
    attn_other = across(attn_four, CORE)
    qkv_w_grad, out_w_grad = final_call(
        attend_final_kernel,
        "attend_final",
        [sent((3 * local, width), F32), sent((local, width), F32)],
        place_ref,
        [attn_four, attn_other],
        line.token,
        scratch=[pltpu.VMEM((width, width), F32)],
    )

    return (
        layer_out.transpose(1, 0, 2),
        tokens_out.transpose(1, 0, 2),
        total[0],
        total[1],
        total[2],
        qkv_w_grad.reshape(3, local, width).transpose(2, 0, 1),
        total[SHARED, :local],
        total[SHARED, 2 * local : 3 * local],
        total[SHARED + 2 : SHARED + 2 + heads, :bucket_count],
        out_w_grad,
        total[3],
        total[4],
        total[5],
        total[6],
        in_w_grad,
        total[SHARED + 1],
        down_w_grad,
        total[7],
        total[8],
    )


def solution(mesh):
    placed = (
        P(None, ("wide", "narrow"), None),
        P(None, ("wide", "narrow")),
        P(),
        P(),
        P(),
        P(),
        P(None, None, "narrow"),
        P("narrow"),
        P("narrow"),
        P("narrow", None),
        P("narrow", None),
        P(),
        P(),
        P(),
        P(),
        P(None, "narrow"),
        P("narrow"),
        P("narrow", None),
        P(),
        P(),
        P(None, ("wide", "narrow"), None),
    )
    return jax.shard_map(
        body,
        mesh=mesh,
        in_specs=placed,
        out_specs=(
            P(None, ("wide", "narrow"), None),
            P(None, ("wide", "narrow"), None),
            P(),
            P(),
            P(),
            P(None, None, "narrow"),
            P("narrow"),
            P("narrow"),
            P("narrow", None),
            P("narrow", None),
            P(),
            P(),
            P(),
            P(),
            P(None, "narrow"),
            P("narrow"),
            P("narrow", None),
            P(),
            P(),
        ),
        check_vma=False,
    )
```

```python
import functools

import jax
import jax.numpy as jnp
from jax import lax
from jax.experimental import pallas as pl
from jax.experimental.pallas import tpu as pltpu
from jax.sharding import PartitionSpec as P


SEQ = 197
PAD = 208
LANES = 256
EPSILON = 1e-06
ROOT_HALF = 0.7071067811865476
DENSITY = 0.3989422804014327
CORE, SIDE, DEEP = 1, 2, 4
PIECES = 8
LOW = 128
NEGATIVE = -1e30
FLOPS = 2 * 10**10
F32 = jnp.float32
BF16 = jnp.bfloat16

NN = (((1,), (0,)), ((), ()))
NT = (((1,), (1,)), ((), ()))
TN = (((0,), (0,)), ((), ()))


def mul(left, right, dims=NN):
    return lax.dot_general(left, right, dims, preferred_element_type=F32)


def vmem():
    return pl.BlockSpec(memory_space=pltpu.VMEM)


def anywhere():
    return pl.BlockSpec(memory_space=pl.ANY)


def scalars():
    return pl.BlockSpec(memory_space=pltpu.SMEM)


def near(values):
    return pltpu.with_memory_space_constraint(values, pltpu.VMEM)


def kept(shape, dtype):
    return pltpu.VMEM(shape, dtype)


def sent(shape, dtype):
    return jax.ShapeDtypeStruct(shape, dtype)


def call(kernel, name, outs, in_specs, out_specs=None, scratch=(), flops=FLOPS, limit=12, aliases=None):
    made = pl.pallas_call(
        kernel,
        out_shape=outs,
        in_specs=in_specs,
        out_specs=out_specs or [vmem()] * len(outs),
        scratch_shapes=list(scratch),
        input_output_aliases=aliases or {},
        compiler_params=pltpu.CompilerParams(vmem_limit_bytes=limit * 1024 * 1024),
        cost_estimate=pl.CostEstimate(flops=flops, bytes_accessed=0, transcendentals=0),
        name=name,
    )
    return lambda *arrays: made(
        *[near(a) if spec.memory_space == pltpu.VMEM else a for spec, a in zip(in_specs, arrays, strict=True)]
    )


class Line:
    def __init__(self):
        self.token = None

    def run(self, kernel, name, outs, arrays, scalar=None, waits=(), scratch=(), flops=FLOPS, limit=12):
        before = list(waits) + ([] if self.token is None else [self.token])
        start, n_in = (0 if scalar is None else 1), len(arrays)

        def whole(*refs):
            inputs = refs[: start + n_in]
            rest = refs[start + n_in + len(before) :]
            rest[len(outs)][...] = jnp.zeros((8, 128), F32)
            kernel(*inputs, *rest[: len(outs)], *rest[len(outs) + 1 :])

        made = call(
            whole,
            name,
            outs + [kept((8, 128), F32)],
            [scalars()] * start + [vmem()] * n_in + [anywhere()] * len(before),
            scratch=scratch,
            flops=flops,
            limit=limit,
        )(*([] if scalar is None else [scalar]), *arrays, *before)
        self.token = made[-1]
        return made[:-1]

    def gate(self, *arrays, waits=(), place=kept):
        n = len(arrays)
        made = call(
            lambda *refs: None,
            "gate",
            [place(a.shape, a.dtype) for a in arrays],
            [anywhere()] * (n + 1 + len(waits)),
            out_specs=[anywhere()] * n,
            aliases={i: i for i in range(n)},
            flops=0,
        )(*[near(a) if place is kept else a for a in arrays], self.token, *waits)
        return made[0] if n == 1 else made


class Jobs:
    def __init__(self, jobs):
        self.jobs = jobs

    def arrays(self):
        return [a for arrays, _, _ in self.jobs for a in arrays]

    def outs(self):
        made = []
        for arrays, counts, parts in self.jobs:
            _, mats, *rest = arrays[0].shape
            made += [kept((count, mats // parts, *rest), BF16) for count in counts for _ in range(parts)]
        return made

    def add(self, refs_in, refs_out):
        at_in = at_out = 0
        for arrays, counts, parts in self.jobs:
            sources = refs_in[at_in : at_in + len(arrays)]
            at_in += len(arrays)
            mats = arrays[0].shape[1] // parts
            first = 0
            for count in counts:
                for part in range(parts):
                    for i in range(count):
                        for j in range(mats):
                            at = (first + i, part * mats + j)
                            total = sources[0][at].astype(F32)
                            for source in sources[1:]:
                                total = total + source[at].astype(F32)
                            refs_out[at_out][i, j] = total.astype(BF16)
                    at_out += 1
                first += count

    def split(self, outs):
        made, at = [], 0
        for _, counts, parts in self.jobs:
            made.append(list(outs[at : at + len(counts) * parts]))
            at += len(counts) * parts
        return made


def final_call(kernel, name, outs, scalar, arrays, token, scratch=()):
    n_in = 1 + len(arrays)
    return call(
        lambda *refs: kernel(*refs[:n_in], *refs[n_in + 1 :]),
        name,
        outs,
        [scalars()] + [vmem()] * len(arrays) + [anywhere()],
        scratch=scratch,
    )(scalar, *arrays, token)


def norm_parts(values):
    center = values - jnp.mean(values, axis=-1, keepdims=True)
    spread = jnp.mean(center * center, axis=-1, keepdims=True)
    inverse = lax.rsqrt(spread + EPSILON)
    return center * inverse, inverse


def norm_back(grad, normed, inverse, gain):
    scaled = grad * gain
    inner = jnp.mean(scaled, axis=-1, keepdims=True)
    cross = jnp.mean(scaled * normed, axis=-1, keepdims=True)
    return inverse * (scaled - inner - normed * cross)


def col(values):
    return jnp.sum(values, axis=0, keepdims=True)


SMALL = 8
VECTORS = 5


TOKEN, FIRST_GAIN, FIRST_SHIFT, OUT_BIAS, ATTN_SCALE, SECOND_GAIN, SECOND_SHIFT, MLP_SCALE, DOWN_BIAS = range(9)


def row(ref, number):
    return ref[number : number + 1, :]


def first_kernel(tok_ref, mask_ref, vec_ref, out_ref):
    masked = jnp.where(mask_ref[...] > 0.0, row(vec_ref, TOKEN), tok_ref[...].astype(F32))
    normed, _ = norm_parts(masked)
    out = normed * row(vec_ref, FIRST_GAIN) + row(vec_ref, FIRST_SHIFT)
    rows = lax.broadcasted_iota(jnp.int32, (tok_ref.shape[0], 1), 0)
    real = lax.rem(rows, PAD) < SEQ
    out_ref[...] = jnp.where(real, out, 0.0).astype(BF16)


def bias_kernel(buckets_ref, small_ref, out_ref):
    heads = out_ref.shape[0]
    parts = small_ref.shape[1] // 128
    for half in range(2):
        lanes = pl.ds(half * 128, 128)
        index = buckets_ref[:, lanes]
        low = lax.bitwise_and(index, 127)
        high = lax.shift_right_logical(index, 7)
        column = lax.broadcasted_iota(jnp.int32, index.shape, 1) + half * 128
        for head in range(heads):
            total = jnp.full(index.shape, NEGATIVE, F32)
            for part in range(parts):
                values = small_ref[2 + head : 3 + head, part * 128 : (part + 1) * 128]
                values = jnp.broadcast_to(values, index.shape)
                found = jnp.take_along_axis(values, low, axis=1, mode="promise_in_bounds")
                total = jnp.where(high == part, found, total)
            out_ref[head, :, lanes] = jnp.where(column < SEQ, total, NEGATIVE)


def stack_kernel(*refs):
    for i, ref in enumerate(refs[:-1]):
        refs[-1][i] = ref[...]


def start_kernel(w_ref, small_ref, qkv_ref, out_ref, piece_ref, own_ref, sem):
    place = w_ref[0]
    rows = piece_ref.shape[0] - 2 * SMALL
    cut = qkv_ref.shape[0] // rows

    def bring(ref, number):
        copy = pltpu.make_async_copy(
            ref.at[pl.ds(pl.multiple_of(number * rows, rows), rows), :], own_ref, sem
        )
        copy.start()
        copy.wait()

    @pl.when(place < cut)
    def _():
        bring(qkv_ref, place)

    @pl.when(place >= cut)
    def _():
        bring(out_ref, place - cut)

    piece_ref[:rows, :] = own_ref[...]
    small = small_ref[:VECTORS, :]
    upper = small.astype(BF16).astype(F32)
    middle = (small - upper).astype(BF16).astype(F32)
    lower = small - upper - middle
    terms = jnp.concatenate([upper, middle, lower, jnp.zeros((1, small.shape[1]), F32)], axis=0)
    piece_ref[rows:, :] = terms.astype(BF16)


def arrive_kernel(count, *refs):
    came, zero_ref, smalls = refs[:count], refs[count], refs[count + 1 :]
    rows = zero_ref.shape[1]
    for i, ref in enumerate(came):
        zero_ref[i] = ref[:rows, :]
        terms = ref[rows:, :].astype(F32)
        smalls[i][...] = jnp.zeros_like(smalls[i])
        smalls[i][:VECTORS, :] = (
            terms[:VECTORS] + terms[VECTORS : 2 * VECTORS] + terms[2 * VECTORS : 3 * VECTORS]
        )


def cut_kernel(w_ref, in_ref, down_ref, four_ref, *own_refs):
    rows = four_ref.shape[1] // 2
    for k in range(four_ref.shape[0]):
        start = pl.multiple_of(lax.bitwise_xor(w_ref[0], 2 * k) * rows, rows)
        for i, ref in enumerate((in_ref, down_ref)):
            part = ref[pl.ds(start, rows), :]
            four_ref[k, i * rows : (i + 1) * rows, :] = part
            for own_ref in own_refs if k == 0 else ():
                own_ref[i * rows : (i + 1) * rows, :] = part


def put_together(w_ref, pair, slot, cut, target):
    rows = target.shape[0] // PIECES
    for piece in range(PIECES):
        start = pl.multiple_of(lax.bitwise_xor(w_ref[0], piece) * rows, rows)
        target[pl.ds(start, rows), :] = pair[piece & CORE][piece >> 1, slot, cut : cut + rows, :]


def take_apart(w_ref, mats, order, keep, send):
    for number, mat in enumerate(mats):
        rows = mat.shape[0] // PIECES
        for piece in range(PIECES):
            start = pl.multiple_of(lax.bitwise_xor(w_ref[0], piece) * rows, rows)
            target = send if piece & CORE else keep
            target[order[piece >> 1], number] = mat[pl.ds(start, rows), :]


def attend_kernel(slot, first, *refs):
    w_ref = refs[0]
    weights = refs[1:3]
    rest = refs[3:]
    x_ref, small_ref, bias_ref = rest[:3]
    rest = rest[3:]
    if not first:
        acc_in = rest[0]
        rest = rest[1:]
    acc_ref, qkv_ref, probs_ref, mixed_ref = rest[:4]
    if first:
        qkv_mat, out_mat = weights
        width = qkv_mat.shape[1]
        local = width // 4
    else:
        mat = rest[4]
        put_together(w_ref, weights, slot, 0, mat)
        width = mat.shape[0]
        local = width // 4
        qkv_mat, out_mat = mat.at[: 3 * local, :], mat.at[3 * local :, :]
    heads = bias_ref.shape[0]
    size = local // heads
    qkv = mul(x_ref[...], qkv_mat[...], NT)
    queries = qkv[:, :local] + small_ref[0:1, :local]
    queries = (queries.astype(BF16).astype(F32) * size ** (-0.5)).astype(BF16)
    keys = qkv[:, local : 2 * local].astype(BF16)
    values = qkv[:, 2 * local :] + small_ref[0:1, LANES : LANES + local]
    values = values.astype(BF16)
    qkv_ref[0] = queries
    qkv_ref[1] = keys
    qkv_ref[2] = values
    lane = lax.broadcasted_iota(jnp.int32, (PAD, local), 1)
    pages = x_ref.shape[0] // PAD
    zero = jnp.zeros((PAD, local), BF16)
    for page in range(pages):
        rows = slice(page * PAD, (page + 1) * PAD)
        q, k, v = queries[rows], keys[rows], values[rows]
        mixed = jnp.zeros((PAD, local), F32)
        for head in range(heads):
            own = (lane >= head * size) & (lane < (head + 1) * size)
            scores = mul(jnp.where(own, q, zero), k, NT) + bias_ref[head][:, :PAD]
            top = jnp.max(scores, axis=1, keepdims=True)
            power = jnp.exp(scores - top)
            total = jnp.sum(power, axis=1, keepdims=True)
            probs = (power * (1.0 / total)).astype(BF16)
            probs_ref[page * heads + head] = probs
            mixed = mixed + mul(probs, jnp.where(own, v, zero))
        mixed_ref[rows, :] = mixed.astype(BF16)
    out = mul(mixed_ref[...], out_mat[...])
    acc_ref[...] = out if first else acc_in[...] + out


def middle_kernel(acc_ref, tok_ref, mask_ref, grad_ref, vec_ref, mid_ref, x_ref, mg_ref):
    masked = jnp.where(mask_ref[...] > 0.0, row(vec_ref, TOKEN), tok_ref[...].astype(F32))
    middle = masked + row(vec_ref, ATTN_SCALE) * (acc_ref[...] + row(vec_ref, OUT_BIAS))
    mid_ref[...] = middle
    normed, _ = norm_parts(middle)
    x_ref[...] = (normed * row(vec_ref, SECOND_GAIN) + row(vec_ref, SECOND_SHIFT)).astype(BF16)
    mg_ref[...] = (grad_ref[...].astype(F32) * row(vec_ref, MLP_SCALE)).astype(BF16)


def mlp_kernel(first, order, jobs, *refs):
    w_ref = refs[0]
    weights = refs[1:3]
    rest = refs[3:]
    x_ref, mg_ref, small_ref = rest[:3]
    rest = rest[3:]
    if not first:
        out_in, grad_in = rest[:2]
        rest = rest[2:]
    n_jobs = len(jobs.arrays())
    jobs_in, rest = rest[:n_jobs], rest[n_jobs:]
    out_ref, grad_ref, col_ref, keep, send = rest[:5]
    rest = rest[5:]
    n_jobs = len(jobs.outs())
    jobs_out, rest = rest[:n_jobs], rest[n_jobs:]
    in_grad, down_grad = rest[:2]
    if first:
        in_mat, down_mat = weights
    else:
        in_mat, down_mat = rest[2:]
        put_together(w_ref, weights, 0, 0, in_mat)
        put_together(w_ref, weights, 0, in_mat.shape[0] // PIECES, down_mat)
    jobs.add(jobs_in, jobs_out)
    width = in_mat.shape[0]
    x = x_ref[...]
    mg = mg_ref[...]
    out = None
    back = None
    for start in range(0, width, 256):
        units = slice(start, start + 256)
        weight_in = in_mat[:, units]
        weight_down = down_mat[units, :]
        pre = mul(x, weight_in) + small_ref[1:2, units]
        phi = 0.5 * (1.0 + lax.erf(pre * ROOT_HALF))
        hidden = (pre * phi).astype(BF16)
        slope = phi + pre * (DENSITY * jnp.exp(-0.5 * pre * pre))
        part = mul(hidden, weight_down)
        out = part if out is None else out + part
        hidden_grad = mul(mg, weight_down, NT)
        pre_grad = hidden_grad * slope
        low = pre_grad.astype(BF16)
        col_ref[:, units] = col(low.astype(F32))
        part = mul(low, weight_in, NT)
        back = part if back is None else back + part
        down_grad[units, :] = mul(hidden, mg, TN).astype(BF16)
        in_grad[:, units] = mul(x, low, TN).astype(BF16)
    out_ref[...] = out if first else out_in[...] + out
    grad_ref[...] = back if first else grad_in[...] + back
    take_apart(w_ref, [in_grad, down_grad], order, keep, send)


def turn_kernel(jobs, *refs):
    mid_ref, out_ref, back_ref, grad_ref, acc_ref, vec_ref = refs[:6]
    refs = refs[6:]
    n_jobs = len(jobs.arrays())
    jobs_in, refs = refs[:n_jobs], refs[n_jobs:]
    layer_ref, mgrad_ref, ag_ref, sums_ref = refs[:4]
    jobs.add(jobs_in, refs[4:])
    middle = mid_ref[...]
    grad = grad_ref[...].astype(F32)
    mlp_out = out_ref[...] + row(vec_ref, DOWN_BIAS)
    layer_ref[...] = (middle + row(vec_ref, MLP_SCALE) * mlp_out).astype(BF16)
    normed, inverse = norm_parts(middle)
    second = back_ref[...]
    middle_grad = grad + norm_back(second, normed, inverse, row(vec_ref, SECOND_GAIN))
    mgrad_ref[...] = middle_grad
    scaled = middle_grad * row(vec_ref, ATTN_SCALE)
    ag_ref[...] = scaled.astype(BF16)
    sums_ref[0:1, :] = col(scaled)
    sums_ref[1:2, :] = col(middle_grad * (acc_ref[...] + row(vec_ref, OUT_BIAS)))
    sums_ref[2:3, :] = col(second * normed)
    sums_ref[3:4, :] = col(second)
    sums_ref[4:5, :] = col(grad * row(vec_ref, MLP_SCALE))
    sums_ref[5:6, :] = col(grad * mlp_out)
    sums_ref[6:8, :] = jnp.zeros_like(sums_ref[6:8, :])


def attend_back_kernel(own, first, order, second, jobs, *refs):
    w_ref = refs[0]
    if own:
        qkv_mat, out_mat = refs[1:3]
        rest = refs[3:]
    else:
        local = refs[1].shape[0] // 4
        qkv_mat, out_mat = refs[1].at[: 3 * local, :], refs[1].at[3 * local :, :]
        rest = refs[2:]
    x_ref, ag_ref, qkv_ref, probs_ref, mixed_ref = rest[:5]
    rest = rest[5:]
    if not first:
        grad_in = rest[0]
        rest = rest[1:]
    if second:
        other_grad = rest[0]
        rest = rest[1:]
    n_jobs = len(jobs.arrays())
    jobs_in, rest = rest[:n_jobs], rest[n_jobs:]
    grad_ref, col_ref, grid_ref = rest[:3]
    if second:
        keep, send = rest[3:5]
        rest = rest[5:]
    else:
        mat_grad = rest[3]
        rest = rest[4:]
    n_jobs = len(jobs.outs())
    jobs_out, rest = rest[:n_jobs], rest[n_jobs:]
    if second:
        mat_grad, dqkv = rest
    else:
        (dqkv,) = rest
    jobs.add(jobs_in, jobs_out)
    local = out_mat.shape[0]
    heads = grid_ref.shape[0]
    size = local // heads
    ag = ag_ref[...]
    mixed_grad = mul(ag, out_mat[...], NT).astype(BF16)
    mat_grad[3 * local :, :] = mul(mixed_ref[...], ag, TN).astype(BF16)
    lane = lax.broadcasted_iota(jnp.int32, (PAD, local), 1)
    pages = x_ref.shape[0] // PAD
    zero = jnp.zeros((PAD, local), BF16)
    for page in range(pages):
        rows = slice(page * PAD, (page + 1) * PAD)
        q, v, dm = qkv_ref[0, rows, :], qkv_ref[2, rows, :], mixed_grad[rows]
        k = (qkv_ref[1, rows, :].astype(F32) * size ** (-0.5)).astype(BF16)
        dq = jnp.zeros((PAD, local), F32)
        dk = jnp.zeros((PAD, local), F32)
        dv = jnp.zeros((PAD, local), F32)
        for head in range(heads):
            own = (lane >= head * size) & (lane < (head + 1) * size)
            dmh = jnp.where(own, dm, zero)
            probs_low = probs_ref[page * heads + head]
            probs = probs_low.astype(F32)
            weighed = probs * mul(dmh, v, NT)
            score = weighed - probs * jnp.sum(weighed, axis=1, keepdims=True)
            low = score.astype(BF16)
            if page == 0:
                grid_ref[head] = low.astype(F32)
            else:
                grid_ref[head] = grid_ref[head] + low.astype(F32)
            dq = dq + mul(low, jnp.where(own, k, zero))
            dk = dk + mul(low, jnp.where(own, q, zero), TN)
            dv = dv + mul(probs_low, dmh, TN)
        dqkv[rows, :] = jnp.concatenate([dq, dk, dv], axis=1).astype(BF16)
    grads = dqkv[...]
    mat_grad[: 3 * local, :] = mul(grads, x_ref[...], TN).astype(BF16)
    col_ref[...] = col(grads.astype(F32))
    back = mul(grads, qkv_mat[...])
    grad_ref[...] = back if first else grad_in[...] + back
    if second:
        take_apart(w_ref, [other_grad, mat_grad], order, keep, send)


def last_kernel(tok_ref, mask_ref, mgrad_ref, first_ref, vec_ref, grad_ref, sums_ref):
    mask = mask_ref[...] > 0.0
    masked = jnp.where(mask, row(vec_ref, TOKEN), tok_ref[...].astype(F32))
    normed, inverse = norm_parts(masked)
    first = first_ref[...]
    in_grad = mgrad_ref[...] + norm_back(first, normed, inverse, row(vec_ref, FIRST_GAIN))
    grad_ref[...] = jnp.where(mask, 0.0, in_grad).astype(BF16)
    sums_ref[0:1, :] = col(jnp.where(mask, in_grad, 0.0))
    sums_ref[1:2, :] = col(first * normed)
    sums_ref[2:3, :] = col(first)
    sums_ref[3:8, :] = jnp.zeros_like(sums_ref[3:8, :])


def table_kernel(grid_count, begin, end, *refs):
    buckets_ref = refs[0]
    grids = refs[1 : 1 + grid_count]
    out_ref = refs[1 + grid_count]
    heads = grids[0].shape[0]
    highs = out_ref.shape[0] // (grid_count * heads)
    out_ref[...] = jnp.zeros_like(out_ref)

    def step(block, _):
        base = pl.multiple_of(block * 8, 8)
        index = buckets_ref[pl.ds(base, 8), :][:, :PAD]
        loads = [[g[h, pl.ds(base, 8), :] for h in range(heads)] for g in grids]
        total = None
        for row in range(8):
            one = index[row : row + 1]
            low = lax.bitwise_and(one, LOW - 1)
            high = lax.shift_right_logical(one, LOW.bit_length() - 1)
            right = (
                jnp.broadcast_to(low, (LOW, PAD)) == lax.broadcasted_iota(jnp.int32, (LOW, PAD), 0)
            ).astype(F32).astype(BF16)
            match = jnp.broadcast_to(high, (highs, PAD)) == lax.broadcasted_iota(
                jnp.int32, (highs, PAD), 0
            )
            left = jnp.concatenate(
                [
                    jnp.where(match, jnp.broadcast_to(loads[g][h][row : row + 1], (highs, PAD)), 0.0)
                    for g in range(grid_count)
                    for h in range(heads)
                ],
                axis=0,
            ).astype(BF16)
            part = mul(left, right, NT)
            total = part if total is None else total + part
        out_ref[...] += total
        return 0

    lax.fori_loop(begin, end, step, 0)


def sum_kernel(jobs, *refs):
    n_in, n_out = len(jobs.arrays()), len(jobs.outs())
    jobs.add(refs[:n_in], refs[n_in : n_in + n_out])


SHARED = 16
PART = 8
SENT = 16


def pack_kernel(count, w_ref, last_ref, mid_ref, table_ref, table_more_ref, *refs):
    qkv_cols, in_cols, out_ref = refs[:count], refs[count : 2 * count], refs[2 * count]
    out_ref[...] = jnp.zeros_like(out_ref)
    out_ref[0:3, :] = last_ref[0:3, :]
    out_ref[3:9, :] = mid_ref[0:6, :]
    tables = table_ref.shape[0] // count
    parts = out_ref.shape[1] // LOW
    for d in range(count):
        base = SHARED + d * PART
        out_ref[base : base + 1, : qkv_cols[d].shape[1]] = qkv_cols[d][...]
        out_ref[base + 1 : base + 2, :] = in_cols[d][...]
        for k in range(tables):
            at = d * tables + k
            lanes = slice(k % parts * LOW, (k % parts + 1) * LOW)
            out_ref[base + 2 + k // parts : base + 3 + k // parts, lanes] = row(table_ref, at) + row(table_more_ref, at)
    held = out_ref[SHARED:, :]
    for d in range(count):
        shard = lax.rem(w_ref[1] + d, count)
        out_ref[pl.ds(pl.multiple_of(SHARED + shard * PART, 8), PART), :] = held[d * PART : (d + 1) * PART]


def leave_kernel(count, w_ref, stay_a, came_a, stay_b, came_b, flat_ref, *outs):
    rows = stay_a.shape[2]
    pairs = [(stay_b, came_b, 1), (stay_a, came_a, 0), (stay_a, came_a, 1), (stay_b, came_b, 0)]
    for d in range(count):
        stay, came, slot = pairs[d]
        total = stay[0, slot].astype(F32) + came[0, slot].astype(F32)
        shard = lax.rem(w_ref[1] + d, count)
        part = flat_ref[pl.ds(pl.multiple_of(SHARED + shard * PART, 8), PART), :]
        small = jnp.concatenate(
            [flat_ref[:9, :], part[:5], jnp.zeros((SENT - 14, part.shape[1]), F32)], axis=0
        )
        outs[d][:rows, :] = total.astype(outs[d].dtype)
        outs[d][rows:, :] = small.astype(outs[d].dtype)


def home_kernel(own_ref, *refs):
    came, done_ref = refs[:-1], refs[-1]
    total = own_ref[...]
    for ref in came:
        total = total + ref[...].astype(F32)
    done_ref[0, 0] = total.astype(BF16)


def assemble(w_ref, pair, number, place_in):
    rows = place_in.shape[0] // PIECES
    for piece in range(PIECES):
        start = pl.multiple_of(lax.bitwise_xor(w_ref[0], piece) * rows, rows)
        place_in[pl.ds(start, rows), :] = pair[piece & CORE][piece >> 1, 0, number, :rows, :].astype(F32)


def mlp_final_kernel(w_ref, own_ref, other_ref, in_ref, down_ref):
    assemble(w_ref, (own_ref, other_ref), 0, in_ref)
    assemble(w_ref, (own_ref, other_ref), 1, down_ref)


def attend_final_kernel(w_ref, own_ref, other_ref, qkv_ref, out_ref, small_ref, whole):
    assemble(w_ref, (own_ref, other_ref), 0, whole)
    cut = qkv_ref.shape[0]
    qkv_ref[...] = whole[:cut, :]
    out_ref[...] = whole[cut:, :]
    rows = whole.shape[0] // PIECES
    total = jnp.zeros(small_ref.shape, F32)
    for ref in (own_ref, other_ref):
        for chip in range(ref.shape[0]):
            total = total + ref[chip, 0, 0, rows:, :].astype(F32)
    small_ref[...] = total


SIDE_FIRST = (0, 2, 1, 3)
DEEP_FIRST = (0, 1, 2, 3)


def body(
    tokens,
    page_mask,
    buckets,
    mask_token,
    first_gain,
    first_shift,
    qkv_weight,
    query_bias,
    value_bias,
    position_bias,
    out_weight,
    out_bias,
    attn_scale,
    second_gain,
    second_shift,
    in_weight,
    in_bias,
    down_weight,
    down_bias,
    mlp_scale,
    out_grad,
):
    pages, seq, width = tokens.shape
    count = lax.axis_size("narrow")
    local = qkv_weight.shape[2]
    heads, bucket_count = position_bias.shape
    rows = pages * PAD
    piece_rows = width // PIECES
    place = lax.bitwise_and(lax.axis_index("wide").astype(jnp.int32), PIECES - 1)
    place_ref = jnp.stack([place, lax.axis_index("narrow").astype(jnp.int32)])
    wide_shape = (rows, width)
    line = Line()

    def across(values, bit):
        others = lax.axis_size("wide")
        return lax.ppermute(values, "wide", [(i, i ^ bit) for i in range(others)])

    def along(values, step):
        return lax.ppermute(values, "narrow", [(i, (i + step) % count) for i in range(count)])

    def rest_of_wide(values):
        bit = PIECES
        while bit < lax.axis_size("wide"):
            values = (values.astype(F32) + across(values, bit).astype(F32)).astype(values.dtype)
            bit *= 2
        return values

    def plane(values):
        values = line.gate(values)
        return [values] + [across(values, bit) for bit in (SIDE, DEEP, SIDE | DEEP)]

    def stack(name, arrays, waits=()):
        return line.run(
            stack_kernel, name, [kept((len(arrays),) + arrays[0].shape, BF16)], list(arrays), waits=waits
        )[0]

    vecs = jnp.stack(
        [
            mask_token,
            first_gain,
            first_shift,
            out_bias,
            attn_scale,
            second_gain,
            second_shift,
            mlp_scale,
            down_bias,
        ]
    )
    tables = jnp.pad(position_bias, ((0, SMALL - 2 - heads), (0, width - bucket_count)))
    spare = width - LANES - local
    shifts = jnp.pad(query_bias, (0, width - local)) + jnp.pad(value_bias, (LANES, spare))
    small = jnp.concatenate([shifts[None], in_bias[None], tables], axis=0)
    qkv_own = qkv_weight.transpose(1, 2, 0).reshape(3 * local, width)
    piece = call(
        start_kernel,
        "start",
        [kept((piece_rows + 2 * SMALL, width), BF16)],
        [scalars(), vmem(), anywhere(), anywhere()],
        scratch=[pltpu.VMEM((piece_rows, width), BF16), pltpu.SemaphoreType.DMA],
    )(place_ref, small, qkv_own, out_weight)[0]
    attn_came = [along(piece, -step) for step in range(1, count)]
    smalls = [small]

    fill = ((0, 0), (0, PAD - seq), (0, 0))
    tok = jnp.pad(tokens, fill).reshape(rows, width)
    grad = jnp.pad(out_grad, fill).reshape(rows, width)
    flags = (page_mask > 0) & (jnp.arange(seq, dtype=jnp.int32) % SEQ != 0)
    mask = jnp.pad(flags.astype(F32), ((0, 0), (0, PAD - seq))).reshape(rows, 1)
    index = jnp.pad(buckets, ((0, PAD - seq), (0, LANES - seq)))

    four_mlp, *own_mlp = line.run(
        cut_kernel,
        "cut",
        [kept((4, 2 * piece_rows, width), BF16)] + [kept((2 * piece_rows, width), BF16)] * (count - 2),
        [in_weight, down_weight],
        scalar=place_ref,
    )
    x_one = line.run(
        first_kernel,
        "first",
        [kept(wide_shape, BF16)],
        [tok, mask, vecs],
    )[0]
    biases = []

    def make_bias(d, waits=()):
        biases.append(
            line.run(
                bias_kernel, f"bias{d}", [kept((heads, PAD, LANES), F32)], [index, smalls[d]], waits=waits
            )[0]
        )

    make_bias(0)
    zones = {}
    attn_zero, *others = line.run(
        functools.partial(arrive_kernel, count - 1),
        "arrive",
        [kept((count - 1, piece_rows, width), BF16)] + [kept((SMALL, width), F32)] * (count - 1),
        attn_came,
    )
    smalls += others
    attn_came = plane(attn_zero)
    for step in range(1, count - 1):
        zones[step] = along(line.gate(own_mlp[step - 1]), -step)

    held = []

    def attend(d, acc, weights, waits=()):
        own = d == 0
        made = line.run(
            functools.partial(attend_kernel, d - 1, own),
            f"attend{d}",
            [
                kept(wide_shape, F32),
                kept((3, rows, local), BF16),
                kept((pages * heads, PAD, PAD), BF16),
                kept((rows, local), BF16),
            ]
            + ([] if own else [kept((width, width), BF16)]),
            [*weights, x_one, smalls[d], biases[d]] + ([] if own else [acc]),
            scalar=place_ref,
            waits=waits,
        )
        held.append((weights if own else [made[4]], *made[1:4]))
        return made[0]

    acc = attend(0, None, [qkv_own, out_weight])
    for d in range(1, count - 1):
        make_bias(d)
    attn_four = stack("stack_attn", attn_came, [zones[step] for step in range(1, count - 1)])
    attn_other = across(attn_four, CORE)
    planes = {2: plane(zones[2][None])}
    zones[count - 1] = along(line.gate(four_mlp), -(count - 1))
    make_bias(count - 1)
    for d in range(1, count):
        acc = attend(d, acc, [attn_four, attn_other])

    middle, x_two, mlp_grad = line.run(
        middle_kernel,
        "middle",
        [kept(wide_shape, F32), kept(wide_shape, BF16), kept(wide_shape, BF16)],
        [
            acc,
            tok,
            mask,
            grad,
            vecs,
        ],
    )

    group, bits = {}, {}

    def run_jobs(plan):
        jobs = []
        for step, name in plan:
            counts = {"core": (2, 2), "hop": (1, 1), "fan": (1, 1, 1, 1), "end": (1,)}[step]
            jobs.append((group[name], counts, 2 if step == "end" and name[0] == "a" else 1))
        jobs = Jobs(jobs)

        def store(outs):
            for (step, name), made in zip(plan, jobs.split(outs), strict=True):
                group[name] = made
                hops[name] = hops.get(name, 0) + 1

        return jobs, store

    hops = {}

    def send(*names, after=()):
        leaves = [group[name][1] for name in names]
        if after:
            leaves = line.gate(*leaves, waits=[group[name][1] for name in after])
        for name, leave in zip(names, leaves, strict=True):
            group[name] = [group[name][0], across(leave, bits[name][hops[name] - 1])]

    def sums_of(*plan, flops=FLOPS):
        jobs, store = run_jobs(plan)
        outs = line.run(
            functools.partial(sum_kernel, jobs),
            "sum_" + "_".join(step + name for step, name in plan),
            jobs.outs(),
            jobs.arrays(),
            flops=flops,
        )
        store(outs)

    def pause(*waits):
        line.run(lambda *refs: None, "pause", [], [], waits=waits)

    mlp_sums = []
    in_cols = [None] * count
    mlp_order = []

    def feed(d, weights, *plan):
        own = d == 0
        name = f"m{len(mlp_order)}"
        side_first = len(mlp_order) % 2 == 0
        mlp_order.append(d)
        bits[name] = (SIDE, DEEP) if side_first else (DEEP, SIDE)
        jobs, store = run_jobs(plan)
        outs = line.run(
            functools.partial(mlp_kernel, own, SIDE_FIRST if side_first else DEEP_FIRST, jobs),
            f"mlp{d}",
            [
                kept(wide_shape, F32),
                kept(wide_shape, F32),
                kept((1, width), F32),
                kept((4, 2, piece_rows, width), BF16),
                kept((4, 2, piece_rows, width), BF16),
            ]
            + jobs.outs(),
            [*weights, x_two, mlp_grad, smalls[d], *mlp_sums, *jobs.arrays()],
            scalar=place_ref,
            scratch=[pltpu.VMEM((width, width), BF16)] * (2 if own else 4),
        )
        mlp_sums[:] = outs[:2]
        in_cols[d] = outs[2]
        store(outs[5:])
        group[name] = [outs[3], across(outs[4], CORE)]

    full = {}
    full[2] = stack("stack2", planes[2])
    full[2] = [full[2], across(full[2], CORE)]
    planes[1] = plane(zones[1][None])
    feed(0, [in_weight, down_weight])
    pause(full[2][1])
    feed(2, full[2], ("core", "m0"))
    last_zone = line.gate(zones[count - 1])
    full[1] = stack("stack1", planes[1], [last_zone])
    full[1] = [full[1], across(full[1], CORE)]
    last_zone = last_zone[:, None]
    full[count - 1] = [last_zone, across(last_zone, CORE)]
    send("m0")
    sums_of(("core", "m1"))
    send("m1")
    feed(1, full[1])
    feed(count - 1, full[count - 1])

    jobs, store = run_jobs([])
    layer, middle_grad, attn_grad, mid_sums, *outs = line.run(
        functools.partial(turn_kernel, jobs),
        "turn",
        [kept(wide_shape, BF16), kept(wide_shape, F32), kept(wide_shape, BF16), kept((8, width), F32)]
        + jobs.outs(),
        [
            middle,
            *mlp_sums,
            grad,
            acc,
            vecs,
            *jobs.arrays(),
        ],
    )
    store(outs)

    back_sum = []
    qkv_cols, grids = [None] * count, [None] * count
    back_order = []
    half = []

    def attend_back(d, *plan):
        second = len(half) == 1
        name = f"a{len(back_order) // 2}"
        side_first = name == "a0"
        first = not back_sum
        back_order.append(d)
        bits[name] = (SIDE, DEEP) if side_first else (DEEP, SIDE)
        jobs, store = run_jobs(plan)
        mats, *others = held[d]
        piece_arrays = [kept((4, 2, piece_rows, width), BF16)] * 2
        outs = line.run(
            functools.partial(attend_back_kernel, d == 0, first, SIDE_FIRST if side_first else DEEP_FIRST, second, jobs),
            f"attend_back{d}",
            [kept(wide_shape, F32), kept((1, 3 * local), F32), kept((heads, PAD, PAD), F32)]
            + (piece_arrays if second else [kept((width, width), BF16)])
            + jobs.outs(),
            [*mats, x_one, attn_grad, *others, *back_sum, *half, *jobs.arrays()],
            scalar=place_ref,
            scratch=[pltpu.VMEM((width, width), BF16)] * second + [pltpu.VMEM((rows, 3 * local), BF16)],
        )
        back_sum[:] = outs[:1]
        qkv_cols[d], grids[d] = outs[1:3]
        store(outs[5 if second else 4 :])
        if second:
            group[name] = [outs[3], across(outs[4], CORE)]
            half.clear()
        else:
            half.append(outs[3])

    pause(group["m0"][1], group["m1"][1])
    sums_of(("core", "m2"), ("core", "m3"))
    send("m2", "m3")
    attend_back(1, ("hop", "m0"), ("hop", "m1"))
    attend_back(2)
    attend_back(3)
    send("m0", "m1", after=("m2", "m3"))
    attend_back(0, ("hop", "m2"), ("hop", "m3"), ("core", "a0"))

    tok_grad, last_sums = line.run(
        last_kernel,
        "last",
        [kept(wide_shape, BF16), kept((8, width), F32)],
        [tok, mask, middle_grad, *back_sum, vecs],
    )
    send("m2", "m3", after=("m0", "m1"))

    highs = width // LOW
    blocks = -(-seq // 8)

    def make_table(begin, end):
        return line.run(
            functools.partial(table_kernel, count, begin, end),
            f"table{begin}",
            [kept((count * heads * highs, LOW), F32)],
            [index, *grids],
            flops=0,
        )[0]

    def come_home(name, pieces):
        jobs = Jobs([([pieces[d] for d in range(count)], (1,), 1)])
        done = line.run(functools.partial(sum_kernel, jobs), name, jobs.outs(), jobs.arrays())[0]
        return rest_of_wide(done)

    sums_of(("end", "m0"), ("end", "m1"), ("core", "a1"))
    group["a0"][1], group["a1"][1] = line.gate(group["a0"][1], group["a1"][1])
    send("a0", "a1")
    home = {0: group["m0"][0], 2: along(group["m1"][0], 2)}
    table = make_table(0, blocks // 2)
    more_table = make_table(blocks // 2, blocks)
    sums_of(("end", "m2"), ("end", "m3"), flops=0)
    home[1] = along(group["m2"][0], 1)
    home[3] = along(group["m3"][0], 3)
    flat = line.run(
        functools.partial(pack_kernel, count),
        "pack",
        [kept((SHARED + count * PART, width), F32)],
        [last_sums, mid_sums, table, more_table, *qkv_cols, *in_cols],
        scalar=place_ref,
        waits=[home[2]],
    )[0]
    sums_of(("hop", "a0"), ("hop", "a1"))
    send("a0", "a1")
    pause()
    mlp_home = come_home("home_mlp", home)
    mlp_side, mlp_deep = across(mlp_home, SIDE), across(mlp_home, DEEP)
    own_home, *leaving = line.run(
        functools.partial(leave_kernel, count),
        "leave",
        [kept((piece_rows + SENT, width), F32)] + [kept((piece_rows + SENT, width), BF16)] * (count - 1),
        [*group["a0"], *group["a1"], flat],
        scalar=place_ref,
    )
    came = [along(leaving[d - 1], d) for d in range(1, count)]

    def rows_first(values):
        values = line.gate(values)
        return values.reshape(pages, PAD, width)[:, :seq].transpose(1, 0, 2)

    layer_out, tokens_out = line.gate(rows_first(layer), rows_first(tok_grad), place=sent)
    pause(layer_out, tokens_out)
    mlp_side, mlp_deep = line.gate(mlp_side, mlp_deep)
    mlp_far = across(mlp_side, DEEP)
    pause()
    attn_home = line.run(
        home_kernel, "home_attn", [kept((1, 1, piece_rows + SENT, width), BF16)], [own_home, *came]
    )[0]
    attn_home = rest_of_wide(attn_home)
    attn_came = [attn_home] + [across(attn_home, bit) for bit in (SIDE, DEEP, SIDE | DEEP)]
    mlp_four = stack("stack_mlp", [mlp_home, mlp_side, mlp_deep, mlp_far])
    mlp_other = across(mlp_four, CORE)
    pause()
    in_w_grad, down_w_grad = line.run(
        mlp_final_kernel,
        "mlp_final",
        [sent((width, width), F32)] * 2,
        [mlp_four, mlp_other],
        scalar=place_ref,
    )
    attn_four = stack("stack_attn_home", attn_came)
    attn_other = across(attn_four, CORE)
    qkv_w_grad, out_w_grad, total = final_call(
        attend_final_kernel,
        "attend_final",
        [sent((3 * local, width), F32), sent((local, width), F32), kept((SENT, width), F32)],
        place_ref,
        [attn_four, attn_other],
        line.token,
        scratch=[pltpu.VMEM((width, width), F32)],
    )

    return (
        layer_out.transpose(1, 0, 2),
        tokens_out.transpose(1, 0, 2),
        total[0],
        total[1],
        total[2],
        qkv_w_grad.reshape(3, local, width).transpose(2, 0, 1),
        total[9, :local],
        total[9, 2 * local : 3 * local],
        total[11 : 11 + heads, :bucket_count],
        out_w_grad,
        total[3],
        total[4],
        total[5],
        total[6],
        in_w_grad,
        total[10],
        down_w_grad,
        total[7],
        total[8],
    )


def solution(mesh):
    placed = (
        P(None, ("wide", "narrow"), None),
        P(None, ("wide", "narrow")),
        P(),
        P(),
        P(),
        P(),
        P(None, None, "narrow"),
        P("narrow"),
        P("narrow"),
        P("narrow", None),
        P("narrow", None),
        P(),
        P(),
        P(),
        P(),
        P(None, "narrow"),
        P("narrow"),
        P("narrow", None),
        P(),
        P(),
        P(None, ("wide", "narrow"), None),
    )
    return jax.shard_map(
        body,
        mesh=mesh,
        in_specs=placed,
        out_specs=(
            P(None, ("wide", "narrow"), None),
            P(None, ("wide", "narrow"), None),
            P(),
            P(),
            P(),
            P(None, None, "narrow"),
            P("narrow"),
            P("narrow"),
            P("narrow", None),
            P("narrow", None),
            P(),
            P(),
            P(),
            P(),
            P(None, "narrow"),
            P("narrow"),
            P("narrow", None),
            P(),
            P(),
        ),
        check_vma=False,
    )
```

```python
import functools

import jax
import jax.numpy as jnp
from jax import lax
from jax.experimental import pallas as pl
from jax.experimental.pallas import tpu as pltpu
from jax.sharding import PartitionSpec as P


SEQ = 197
PAD = 208
LANES = 256
EPSILON = 1e-06
ROOT_HALF = 0.7071067811865476
DENSITY = 0.3989422804014327
CORE, SIDE, DEEP = 1, 2, 4
PIECES = 8
LOW = 128
NEGATIVE = -1e30
FLOPS = 2 * 10**10
F32 = jnp.float32
BF16 = jnp.bfloat16

NN = (((1,), (0,)), ((), ()))
NT = (((1,), (1,)), ((), ()))
TN = (((0,), (0,)), ((), ()))


def mul(left, right, dims=NN):
    return lax.dot_general(left, right, dims, preferred_element_type=F32)


def vmem():
    return pl.BlockSpec(memory_space=pltpu.VMEM)


def anywhere():
    return pl.BlockSpec(memory_space=pl.ANY)


def scalars():
    return pl.BlockSpec(memory_space=pltpu.SMEM)


def near(values):
    return pltpu.with_memory_space_constraint(values, pltpu.VMEM)


def kept(shape, dtype):
    return pltpu.VMEM(shape, dtype)


def sent(shape, dtype):
    return jax.ShapeDtypeStruct(shape, dtype)


def call(kernel, name, outs, in_specs, out_specs=None, scratch=(), flops=FLOPS, limit=12, aliases=None):
    made = pl.pallas_call(
        kernel,
        out_shape=outs,
        in_specs=in_specs,
        out_specs=out_specs or [vmem()] * len(outs),
        scratch_shapes=list(scratch),
        input_output_aliases=aliases or {},
        compiler_params=pltpu.CompilerParams(vmem_limit_bytes=limit * 1024 * 1024),
        cost_estimate=pl.CostEstimate(flops=flops, bytes_accessed=0, transcendentals=0),
        name=name,
    )
    return lambda *arrays: made(
        *[near(a) if spec.memory_space == pltpu.VMEM else a for spec, a in zip(in_specs, arrays, strict=True)]
    )


class Line:
    def __init__(self):
        self.token = None

    def run(self, kernel, name, outs, arrays, scalar=None, waits=(), scratch=(), flops=FLOPS, limit=12):
        before = list(waits) + ([] if self.token is None else [self.token])
        start, n_in = (0 if scalar is None else 1), len(arrays)

        def whole(*refs):
            inputs = refs[: start + n_in]
            rest = refs[start + n_in + len(before) :]
            rest[len(outs)][...] = jnp.zeros((8, 128), F32)
            kernel(*inputs, *rest[: len(outs)], *rest[len(outs) + 1 :])

        made = call(
            whole,
            name,
            outs + [kept((8, 128), F32)],
            [scalars()] * start + [vmem()] * n_in + [anywhere()] * len(before),
            scratch=scratch,
            flops=flops,
            limit=limit,
        )(*([] if scalar is None else [scalar]), *arrays, *before)
        self.token = made[-1]
        return made[:-1]

    def gate(self, *arrays, waits=(), place=kept):
        n = len(arrays)
        made = call(
            lambda *refs: None,
            "gate",
            [place(a.shape, a.dtype) for a in arrays],
            [anywhere()] * (n + 1 + len(waits)),
            out_specs=[anywhere()] * n,
            aliases={i: i for i in range(n)},
            flops=0,
        )(*[near(a) if place is kept else a for a in arrays], self.token, *waits)
        return made[0] if n == 1 else made


class Jobs:
    def __init__(self, jobs):
        self.jobs = jobs

    def arrays(self):
        return [a for arrays, _, _ in self.jobs for a in arrays]

    def outs(self):
        made = []
        for arrays, counts, parts in self.jobs:
            _, mats, *rest = arrays[0].shape
            made += [kept((count, mats // parts, *rest), BF16) for count in counts for _ in range(parts)]
        return made

    def add(self, refs_in, refs_out):
        at_in = at_out = 0
        for arrays, counts, parts in self.jobs:
            sources = refs_in[at_in : at_in + len(arrays)]
            at_in += len(arrays)
            mats = arrays[0].shape[1] // parts
            first = 0
            for count in counts:
                for part in range(parts):
                    for i in range(count):
                        for j in range(mats):
                            at = (first + i, part * mats + j)
                            total = sources[0][at].astype(F32)
                            for source in sources[1:]:
                                total = total + source[at].astype(F32)
                            refs_out[at_out][i, j] = total.astype(BF16)
                    at_out += 1
                first += count

    def split(self, outs):
        made, at = [], 0
        for _, counts, parts in self.jobs:
            made.append(list(outs[at : at + len(counts) * parts]))
            at += len(counts) * parts
        return made


def final_call(kernel, name, outs, scalar, arrays, token, scratch=()):
    n_in = 1 + len(arrays)
    return call(
        lambda *refs: kernel(*refs[:n_in], *refs[n_in + 1 :]),
        name,
        outs,
        [scalars()] + [vmem()] * len(arrays) + [anywhere()],
        scratch=scratch,
    )(scalar, *arrays, token)


def norm_parts(values):
    center = values - jnp.mean(values, axis=-1, keepdims=True)
    spread = jnp.mean(center * center, axis=-1, keepdims=True)
    inverse = lax.rsqrt(spread + EPSILON)
    return center * inverse, inverse


def norm_back(grad, normed, inverse, gain):
    scaled = grad * gain
    inner = jnp.mean(scaled, axis=-1, keepdims=True)
    cross = jnp.mean(scaled * normed, axis=-1, keepdims=True)
    return inverse * (scaled - inner - normed * cross)


def col(values):
    return jnp.sum(values, axis=0, keepdims=True)


SMALL = 8
VECTORS = 5


TOKEN, FIRST_GAIN, FIRST_SHIFT, OUT_BIAS, ATTN_SCALE, SECOND_GAIN, SECOND_SHIFT, MLP_SCALE, DOWN_BIAS = range(9)


def row(ref, number):
    return ref[number : number + 1, :]


def first_kernel(tok_ref, mask_ref, vec_ref, out_ref):
    masked = jnp.where(mask_ref[...] > 0.0, row(vec_ref, TOKEN), tok_ref[...].astype(F32))
    normed, _ = norm_parts(masked)
    out = normed * row(vec_ref, FIRST_GAIN) + row(vec_ref, FIRST_SHIFT)
    rows = lax.broadcasted_iota(jnp.int32, (tok_ref.shape[0], 1), 0)
    real = lax.rem(rows, PAD) < SEQ
    out_ref[...] = jnp.where(real, out, 0.0).astype(BF16)


def bias_kernel(buckets_ref, small_ref, out_ref):
    heads = out_ref.shape[0]
    parts = small_ref.shape[1] // 128
    for half in range(2):
        lanes = pl.ds(half * 128, 128)
        index = buckets_ref[:, lanes]
        low = lax.bitwise_and(index, 127)
        high = lax.shift_right_logical(index, 7)
        column = lax.broadcasted_iota(jnp.int32, index.shape, 1) + half * 128
        for head in range(heads):
            total = jnp.full(index.shape, NEGATIVE, F32)
            for part in range(parts):
                values = small_ref[2 + head : 3 + head, part * 128 : (part + 1) * 128]
                values = jnp.broadcast_to(values, index.shape)
                found = jnp.take_along_axis(values, low, axis=1, mode="promise_in_bounds")
                total = jnp.where(high == part, found, total)
            out_ref[head, :, lanes] = jnp.where(column < SEQ, total, NEGATIVE)


def stack_kernel(*refs):
    for i, ref in enumerate(refs[:-1]):
        refs[-1][i] = ref[...]


def start_kernel(w_ref, small_ref, qkv_ref, out_ref, piece_ref, own_ref, sem):
    place = w_ref[0]
    rows = piece_ref.shape[0] - 2 * SMALL
    cut = qkv_ref.shape[0] // rows

    def bring(ref, number):
        copy = pltpu.make_async_copy(
            ref.at[pl.ds(pl.multiple_of(number * rows, rows), rows), :], own_ref, sem
        )
        copy.start()
        copy.wait()

    @pl.when(place < cut)
    def _():
        bring(qkv_ref, place)

    @pl.when(place >= cut)
    def _():
        bring(out_ref, place - cut)

    piece_ref[:rows, :] = own_ref[...]
    small = small_ref[:VECTORS, :]
    upper = small.astype(BF16).astype(F32)
    middle = (small - upper).astype(BF16).astype(F32)
    lower = small - upper - middle
    terms = jnp.concatenate([upper, middle, lower, jnp.zeros((1, small.shape[1]), F32)], axis=0)
    piece_ref[rows:, :] = terms.astype(BF16)


def arrive_kernel(count, *refs):
    came, zero_ref, smalls = refs[:count], refs[count], refs[count + 1 :]
    rows = zero_ref.shape[1]
    for i, ref in enumerate(came):
        zero_ref[i] = ref[:rows, :]
        terms = ref[rows:, :].astype(F32)
        smalls[i][...] = jnp.zeros_like(smalls[i])
        smalls[i][:VECTORS, :] = (
            terms[:VECTORS] + terms[VECTORS : 2 * VECTORS] + terms[2 * VECTORS : 3 * VECTORS]
        )


def cut_kernel(w_ref, in_ref, down_ref, four_ref, *own_refs):
    rows = four_ref.shape[1] // 2
    for k in range(four_ref.shape[0]):
        start = pl.multiple_of(lax.bitwise_xor(w_ref[0], 2 * k) * rows, rows)
        for i, ref in enumerate((in_ref, down_ref)):
            part = ref[pl.ds(start, rows), :]
            four_ref[k, i * rows : (i + 1) * rows, :] = part
            for own_ref in own_refs if k == 0 else ():
                own_ref[i * rows : (i + 1) * rows, :] = part


def put_together(w_ref, pair, slot, cut, target):
    rows = target.shape[0] // PIECES
    for piece in range(PIECES):
        start = pl.multiple_of(lax.bitwise_xor(w_ref[0], piece) * rows, rows)
        target[pl.ds(start, rows), :] = pair[piece & CORE][piece >> 1, slot, cut : cut + rows, :]


def take_apart(w_ref, mats, order, keep, send):
    for number, mat in enumerate(mats):
        rows = mat.shape[0] // PIECES
        for piece in range(PIECES):
            start = pl.multiple_of(lax.bitwise_xor(w_ref[0], piece) * rows, rows)
            target = send if piece & CORE else keep
            target[order[piece >> 1], number] = mat[pl.ds(start, rows), :]


def attend_kernel(slot, first, *refs):
    w_ref = refs[0]
    weights = refs[1:3]
    rest = refs[3:]
    x_ref, small_ref, bias_ref = rest[:3]
    rest = rest[3:]
    if not first:
        acc_in = rest[0]
        rest = rest[1:]
    acc_ref, qkv_ref, probs_ref, mixed_ref = rest[:4]
    if first:
        qkv_mat, out_mat = weights
        width = qkv_mat.shape[1]
        local = width // 4
    else:
        mat = rest[4]
        put_together(w_ref, weights, slot, 0, mat)
        width = mat.shape[0]
        local = width // 4
        qkv_mat, out_mat = mat.at[: 3 * local, :], mat.at[3 * local :, :]
    heads = bias_ref.shape[0]
    size = local // heads
    qkv = mul(x_ref[...], qkv_mat[...], NT)
    queries = qkv[:, :local] + small_ref[0:1, :local]
    queries = (queries.astype(BF16).astype(F32) * size ** (-0.5)).astype(BF16)
    keys = qkv[:, local : 2 * local].astype(BF16)
    values = qkv[:, 2 * local :] + small_ref[0:1, LANES : LANES + local]
    values = values.astype(BF16)
    qkv_ref[0] = queries
    qkv_ref[1] = keys
    qkv_ref[2] = values
    lane = lax.broadcasted_iota(jnp.int32, (PAD, local), 1)
    pages = x_ref.shape[0] // PAD
    zero = jnp.zeros((PAD, local), BF16)
    for page in range(pages):
        rows = slice(page * PAD, (page + 1) * PAD)
        q, k, v = queries[rows], keys[rows], values[rows]
        mixed = jnp.zeros((PAD, local), F32)
        for head in range(heads):
            own = (lane >= head * size) & (lane < (head + 1) * size)
            scores = mul(jnp.where(own, q, zero), k, NT) + bias_ref[head][:, :PAD]
            top = jnp.max(scores, axis=1, keepdims=True)
            power = jnp.exp(scores - top)
            total = jnp.sum(power, axis=1, keepdims=True)
            probs = (power * (1.0 / total)).astype(BF16)
            probs_ref[page * heads + head] = probs
            mixed = mixed + mul(probs, jnp.where(own, v, zero))
        mixed_ref[rows, :] = mixed.astype(BF16)
    out = mul(mixed_ref[...], out_mat[...])
    acc_ref[...] = out if first else acc_in[...] + out


def middle_kernel(acc_ref, tok_ref, mask_ref, grad_ref, vec_ref, mid_ref, x_ref, mg_ref):
    masked = jnp.where(mask_ref[...] > 0.0, row(vec_ref, TOKEN), tok_ref[...].astype(F32))
    middle = masked + row(vec_ref, ATTN_SCALE) * (acc_ref[...] + row(vec_ref, OUT_BIAS))
    mid_ref[...] = middle
    normed, _ = norm_parts(middle)
    x_ref[...] = (normed * row(vec_ref, SECOND_GAIN) + row(vec_ref, SECOND_SHIFT)).astype(BF16)
    mg_ref[...] = (grad_ref[...].astype(F32) * row(vec_ref, MLP_SCALE)).astype(BF16)


def mlp_kernel(first, order, jobs, *refs):
    w_ref = refs[0]
    weights = refs[1:3]
    rest = refs[3:]
    x_ref, mg_ref, small_ref = rest[:3]
    rest = rest[3:]
    if not first:
        out_in, grad_in = rest[:2]
        rest = rest[2:]
    n_jobs = len(jobs.arrays())
    jobs_in, rest = rest[:n_jobs], rest[n_jobs:]
    out_ref, grad_ref, col_ref, keep, send = rest[:5]
    rest = rest[5:]
    n_jobs = len(jobs.outs())
    jobs_out, rest = rest[:n_jobs], rest[n_jobs:]
    in_grad, down_grad = rest[:2]
    if first:
        in_mat, down_mat = weights
    else:
        in_mat, down_mat = rest[2:]
        put_together(w_ref, weights, 0, 0, in_mat)
        put_together(w_ref, weights, 0, in_mat.shape[0] // PIECES, down_mat)
    jobs.add(jobs_in, jobs_out)
    width = in_mat.shape[0]
    x = x_ref[...]
    mg = mg_ref[...]
    out = None
    back = None
    for start in range(0, width, 256):
        units = slice(start, start + 256)
        weight_in = in_mat[:, units]
        weight_down = down_mat[units, :]
        pre = mul(x, weight_in) + small_ref[1:2, units]
        phi = 0.5 * (1.0 + lax.erf(pre * ROOT_HALF))
        hidden = (pre * phi).astype(BF16)
        slope = phi + pre * (DENSITY * jnp.exp(-0.5 * pre * pre))
        part = mul(hidden, weight_down)
        out = part if out is None else out + part
        hidden_grad = mul(mg, weight_down, NT)
        pre_grad = hidden_grad * slope
        low = pre_grad.astype(BF16)
        col_ref[:, units] = col(low.astype(F32))
        part = mul(low, weight_in, NT)
        back = part if back is None else back + part
        down_grad[units, :] = mul(hidden, mg, TN).astype(BF16)
        in_grad[:, units] = mul(x, low, TN).astype(BF16)
    out_ref[...] = out if first else out_in[...] + out
    grad_ref[...] = back if first else grad_in[...] + back
    take_apart(w_ref, [in_grad, down_grad], order, keep, send)


def turn_kernel(jobs, *refs):
    mid_ref, out_ref, back_ref, grad_ref, acc_ref, vec_ref = refs[:6]
    refs = refs[6:]
    n_jobs = len(jobs.arrays())
    jobs_in, refs = refs[:n_jobs], refs[n_jobs:]
    layer_ref, mgrad_ref, ag_ref, sums_ref = refs[:4]
    jobs.add(jobs_in, refs[4:])
    middle = mid_ref[...]
    grad = grad_ref[...].astype(F32)
    mlp_out = out_ref[...] + row(vec_ref, DOWN_BIAS)
    layer_ref[...] = (middle + row(vec_ref, MLP_SCALE) * mlp_out).astype(BF16)
    normed, inverse = norm_parts(middle)
    second = back_ref[...]
    middle_grad = grad + norm_back(second, normed, inverse, row(vec_ref, SECOND_GAIN))
    mgrad_ref[...] = middle_grad
    scaled = middle_grad * row(vec_ref, ATTN_SCALE)
    ag_ref[...] = scaled.astype(BF16)
    sums_ref[0:1, :] = col(scaled)
    sums_ref[1:2, :] = col(middle_grad * (acc_ref[...] + row(vec_ref, OUT_BIAS)))
    sums_ref[2:3, :] = col(second * normed)
    sums_ref[3:4, :] = col(second)
    sums_ref[4:5, :] = col(grad * row(vec_ref, MLP_SCALE))
    sums_ref[5:6, :] = col(grad * mlp_out)
    sums_ref[6:8, :] = jnp.zeros_like(sums_ref[6:8, :])


def attend_back_kernel(own, first, order, second, jobs, *refs):
    w_ref = refs[0]
    if own:
        qkv_mat, out_mat = refs[1:3]
        rest = refs[3:]
    else:
        local = refs[1].shape[0] // 4
        qkv_mat, out_mat = refs[1].at[: 3 * local, :], refs[1].at[3 * local :, :]
        rest = refs[2:]
    x_ref, ag_ref, qkv_ref, probs_ref, mixed_ref = rest[:5]
    rest = rest[5:]
    if not first:
        grad_in = rest[0]
        rest = rest[1:]
    if second:
        other_grad = rest[0]
        rest = rest[1:]
    n_jobs = len(jobs.arrays())
    jobs_in, rest = rest[:n_jobs], rest[n_jobs:]
    grad_ref, col_ref, grid_ref = rest[:3]
    if second:
        keep, send = rest[3:5]
        rest = rest[5:]
    else:
        mat_grad = rest[3]
        rest = rest[4:]
    n_jobs = len(jobs.outs())
    jobs_out, rest = rest[:n_jobs], rest[n_jobs:]
    if second:
        mat_grad, dqkv = rest
    else:
        (dqkv,) = rest
    jobs.add(jobs_in, jobs_out)
    local = out_mat.shape[0]
    heads = grid_ref.shape[0]
    size = local // heads
    ag = ag_ref[...]
    mixed_grad = mul(ag, out_mat[...], NT).astype(BF16)
    mat_grad[3 * local :, :] = mul(mixed_ref[...], ag, TN).astype(BF16)
    lane = lax.broadcasted_iota(jnp.int32, (PAD, local), 1)
    pages = x_ref.shape[0] // PAD
    zero = jnp.zeros((PAD, local), BF16)
    for page in range(pages):
        rows = slice(page * PAD, (page + 1) * PAD)
        q, v, dm = qkv_ref[0, rows, :], qkv_ref[2, rows, :], mixed_grad[rows]
        k = (qkv_ref[1, rows, :].astype(F32) * size ** (-0.5)).astype(BF16)
        dq = jnp.zeros((PAD, local), F32)
        dk = jnp.zeros((PAD, local), F32)
        dv = jnp.zeros((PAD, local), F32)
        for head in range(heads):
            own = (lane >= head * size) & (lane < (head + 1) * size)
            dmh = jnp.where(own, dm, zero)
            probs_low = probs_ref[page * heads + head]
            probs = probs_low.astype(F32)
            weighed = probs * mul(dmh, v, NT)
            score = weighed - probs * jnp.sum(weighed, axis=1, keepdims=True)
            low = score.astype(BF16)
            if page == 0:
                grid_ref[head] = low.astype(F32)
            else:
                grid_ref[head] = grid_ref[head] + low.astype(F32)
            dq = dq + mul(low, jnp.where(own, k, zero))
            dk = dk + mul(low, jnp.where(own, q, zero), TN)
            dv = dv + mul(probs_low, dmh, TN)
        dqkv[rows, :] = jnp.concatenate([dq, dk, dv], axis=1).astype(BF16)
    grads = dqkv[...]
    mat_grad[: 3 * local, :] = mul(grads, x_ref[...], TN).astype(BF16)
    col_ref[...] = col(grads.astype(F32))
    back = mul(grads, qkv_mat[...])
    grad_ref[...] = back if first else grad_in[...] + back
    if second:
        take_apart(w_ref, [other_grad, mat_grad], order, keep, send)


def last_kernel(tok_ref, mask_ref, mgrad_ref, first_ref, vec_ref, grad_ref, sums_ref):
    mask = mask_ref[...] > 0.0
    masked = jnp.where(mask, row(vec_ref, TOKEN), tok_ref[...].astype(F32))
    normed, inverse = norm_parts(masked)
    first = first_ref[...]
    in_grad = mgrad_ref[...] + norm_back(first, normed, inverse, row(vec_ref, FIRST_GAIN))
    grad_ref[...] = jnp.where(mask, 0.0, in_grad).astype(BF16)
    sums_ref[0:1, :] = col(jnp.where(mask, in_grad, 0.0))
    sums_ref[1:2, :] = col(first * normed)
    sums_ref[2:3, :] = col(first)
    sums_ref[3:8, :] = jnp.zeros_like(sums_ref[3:8, :])


def table_kernel(grid_count, begin, end, *refs):
    buckets_ref = refs[0]
    grids = refs[1 : 1 + grid_count]
    out_ref = refs[1 + grid_count]
    heads = grids[0].shape[0]
    highs = out_ref.shape[0] // (grid_count * heads)
    out_ref[...] = jnp.zeros_like(out_ref)

    def step(block, _):
        base = pl.multiple_of(block * 8, 8)
        index = buckets_ref[pl.ds(base, 8), :][:, :PAD]
        loads = [[g[h, pl.ds(base, 8), :] for h in range(heads)] for g in grids]
        total = None
        for row in range(8):
            one = index[row : row + 1]
            low = lax.bitwise_and(one, LOW - 1)
            high = lax.shift_right_logical(one, LOW.bit_length() - 1)
            right = (
                jnp.broadcast_to(low, (LOW, PAD)) == lax.broadcasted_iota(jnp.int32, (LOW, PAD), 0)
            ).astype(F32).astype(BF16)
            match = jnp.broadcast_to(high, (highs, PAD)) == lax.broadcasted_iota(
                jnp.int32, (highs, PAD), 0
            )
            left = jnp.concatenate(
                [
                    jnp.where(match, jnp.broadcast_to(loads[g][h][row : row + 1], (highs, PAD)), 0.0)
                    for g in range(grid_count)
                    for h in range(heads)
                ],
                axis=0,
            ).astype(BF16)
            part = mul(left, right, NT)
            total = part if total is None else total + part
        out_ref[...] += total
        return 0

    lax.fori_loop(begin, end, step, 0)


def sum_kernel(jobs, *refs):
    n_in, n_out = len(jobs.arrays()), len(jobs.outs())
    jobs.add(refs[:n_in], refs[n_in : n_in + n_out])


SHARED = 16
PART = 8
SENT = 16


def pack_kernel(count, w_ref, last_ref, mid_ref, table_ref, table_more_ref, *refs):
    qkv_cols, in_cols, out_ref = refs[:count], refs[count : 2 * count], refs[2 * count]
    out_ref[...] = jnp.zeros_like(out_ref)
    out_ref[0:3, :] = last_ref[0:3, :]
    out_ref[3:9, :] = mid_ref[0:6, :]
    tables = table_ref.shape[0] // count
    parts = out_ref.shape[1] // LOW
    for d in range(count):
        base = SHARED + d * PART
        out_ref[base : base + 1, : qkv_cols[d].shape[1]] = qkv_cols[d][...]
        out_ref[base + 1 : base + 2, :] = in_cols[d][...]
        for k in range(tables):
            at = d * tables + k
            lanes = slice(k % parts * LOW, (k % parts + 1) * LOW)
            out_ref[base + 2 + k // parts : base + 3 + k // parts, lanes] = row(table_ref, at) + row(table_more_ref, at)
    held = out_ref[SHARED:, :]
    for d in range(count):
        shard = lax.rem(w_ref[1] + d, count)
        out_ref[pl.ds(pl.multiple_of(SHARED + shard * PART, 8), PART), :] = held[d * PART : (d + 1) * PART]


def leave_kernel(count, w_ref, stay_a, came_a, stay_b, came_b, flat_ref, *outs):
    rows = stay_a.shape[2]
    pairs = [(stay_b, came_b, 1), (stay_a, came_a, 0), (stay_a, came_a, 1), (stay_b, came_b, 0)]
    for d in range(count):
        stay, came, slot = pairs[d]
        total = stay[0, slot].astype(F32) + came[0, slot].astype(F32)
        shard = lax.rem(w_ref[1] + d, count)
        part = flat_ref[pl.ds(pl.multiple_of(SHARED + shard * PART, 8), PART), :]
        small = jnp.concatenate(
            [flat_ref[:9, :], part[:5], jnp.zeros((SENT - 14, part.shape[1]), F32)], axis=0
        )
        outs[d][:rows, :] = total.astype(outs[d].dtype)
        outs[d][rows:, :] = small.astype(outs[d].dtype)


def home_kernel(own_ref, *refs):
    came, done_ref = refs[:-1], refs[-1]
    total = own_ref[...]
    for ref in came:
        total = total + ref[...].astype(F32)
    done_ref[0, 0] = total.astype(BF16)


def assemble(w_ref, pair, number, place_in):
    rows = place_in.shape[0] // PIECES
    for piece in range(PIECES):
        start = pl.multiple_of(lax.bitwise_xor(w_ref[0], piece) * rows, rows)
        place_in[pl.ds(start, rows), :] = pair[piece & CORE][piece >> 1, 0, number, :rows, :].astype(F32)


def mlp_final_kernel(w_ref, own_ref, other_ref, in_ref, down_ref):
    assemble(w_ref, (own_ref, other_ref), 0, in_ref)
    assemble(w_ref, (own_ref, other_ref), 1, down_ref)


def attend_final_kernel(w_ref, own_ref, other_ref, qkv_ref, out_ref, small_ref, whole):
    assemble(w_ref, (own_ref, other_ref), 0, whole)
    cut = qkv_ref.shape[0]
    qkv_ref[...] = whole[:cut, :]
    out_ref[...] = whole[cut:, :]
    rows = whole.shape[0] // PIECES
    total = jnp.zeros(small_ref.shape, F32)
    for ref in (own_ref, other_ref):
        for chip in range(ref.shape[0]):
            total = total + ref[chip, 0, 0, rows:, :].astype(F32)
    small_ref[...] = total


SIDE_FIRST = (0, 2, 1, 3)
DEEP_FIRST = (0, 1, 2, 3)


def body(
    tokens,
    page_mask,
    buckets,
    mask_token,
    first_gain,
    first_shift,
    qkv_weight,
    query_bias,
    value_bias,
    position_bias,
    out_weight,
    out_bias,
    attn_scale,
    second_gain,
    second_shift,
    in_weight,
    in_bias,
    down_weight,
    down_bias,
    mlp_scale,
    out_grad,
):
    pages, seq, width = tokens.shape
    count = lax.axis_size("narrow")
    local = qkv_weight.shape[2]
    heads, bucket_count = position_bias.shape
    rows = pages * PAD
    piece_rows = width // PIECES
    place = lax.bitwise_and(lax.axis_index("wide").astype(jnp.int32), PIECES - 1)
    place_ref = jnp.stack([place, lax.axis_index("narrow").astype(jnp.int32)])
    wide_shape = (rows, width)
    line = Line()

    def across(values, bit):
        others = lax.axis_size("wide")
        return lax.ppermute(values, "wide", [(i, i ^ bit) for i in range(others)])

    def along(values, step):
        return lax.ppermute(values, "narrow", [(i, (i + step) % count) for i in range(count)])

    def rest_of_wide(values):
        bit = PIECES
        while bit < lax.axis_size("wide"):
            values = (values.astype(F32) + across(values, bit).astype(F32)).astype(values.dtype)
            bit *= 2
        return values

    def plane(values):
        values = line.gate(values)
        return [values] + [across(values, bit) for bit in (SIDE, DEEP, SIDE | DEEP)]

    def stack(name, arrays, waits=()):
        return line.run(
            stack_kernel, name, [kept((len(arrays),) + arrays[0].shape, BF16)], list(arrays), waits=waits
        )[0]

    vecs = jnp.stack(
        [
            mask_token,
            first_gain,
            first_shift,
            out_bias,
            attn_scale,
            second_gain,
            second_shift,
            mlp_scale,
            down_bias,
        ]
    )
    tables = jnp.pad(position_bias, ((0, SMALL - 2 - heads), (0, width - bucket_count)))
    spare = width - LANES - local
    shifts = jnp.pad(query_bias, (0, width - local)) + jnp.pad(value_bias, (LANES, spare))
    small = jnp.concatenate([shifts[None], in_bias[None], tables], axis=0)
    qkv_own = qkv_weight.transpose(1, 2, 0).reshape(3 * local, width)
    piece = call(
        start_kernel,
        "start",
        [kept((piece_rows + 2 * SMALL, width), BF16)],
        [scalars(), vmem(), anywhere(), anywhere()],
        scratch=[pltpu.VMEM((piece_rows, width), BF16), pltpu.SemaphoreType.DMA],
    )(place_ref, small, qkv_own, out_weight)[0]
    attn_came = [along(piece, -step) for step in range(1, count)]
    smalls = [small]

    fill = ((0, 0), (0, PAD - seq), (0, 0))
    tok = jnp.pad(tokens, fill).reshape(rows, width)
    grad = jnp.pad(out_grad, fill).reshape(rows, width)
    flags = (page_mask > 0) & (jnp.arange(seq, dtype=jnp.int32) % SEQ != 0)
    mask = jnp.pad(flags.astype(F32), ((0, 0), (0, PAD - seq))).reshape(rows, 1)
    index = jnp.pad(buckets, ((0, PAD - seq), (0, LANES - seq)))

    four_mlp, *own_mlp = line.run(
        cut_kernel,
        "cut",
        [kept((4, 2 * piece_rows, width), BF16)] + [kept((2 * piece_rows, width), BF16)] * (count - 2),
        [in_weight, down_weight],
        scalar=place_ref,
    )
    x_one = line.run(
        first_kernel,
        "first",
        [kept(wide_shape, BF16)],
        [tok, mask, vecs],
    )[0]
    biases = []

    def make_bias(d, waits=()):
        biases.append(
            line.run(
                bias_kernel, f"bias{d}", [kept((heads, PAD, LANES), F32)], [index, smalls[d]], waits=waits
            )[0]
        )

    make_bias(0)
    zones = {}
    attn_zero, *others = line.run(
        functools.partial(arrive_kernel, count - 1),
        "arrive",
        [kept((count - 1, piece_rows, width), BF16)] + [kept((SMALL, width), F32)] * (count - 1),
        attn_came,
    )
    smalls += others
    attn_came = plane(attn_zero)
    for step in range(1, count - 1):
        zones[step] = along(line.gate(own_mlp[step - 1]), -step)

    held = []

    def attend(d, acc, weights, waits=()):
        own = d == 0
        made = line.run(
            functools.partial(attend_kernel, d - 1, own),
            f"attend{d}",
            [
                kept(wide_shape, F32),
                kept((3, rows, local), BF16),
                kept((pages * heads, PAD, PAD), BF16),
                kept((rows, local), BF16),
            ]
            + ([] if own else [kept((width, width), BF16)]),
            [*weights, x_one, smalls[d], biases[d]] + ([] if own else [acc]),
            scalar=place_ref,
            waits=waits,
        )
        held.append((weights if own else [made[4]], *made[1:4]))
        return made[0]

    acc = attend(0, None, [qkv_own, out_weight])
    for d in range(1, count - 1):
        make_bias(d)
    attn_four = stack("stack_attn", attn_came, [zones[step] for step in range(1, count - 1)])
    attn_other = across(attn_four, CORE)
    planes = {2: plane(zones[2][None])}
    zones[count - 1] = along(line.gate(four_mlp), -(count - 1))
    make_bias(count - 1)
    for d in range(1, count):
        acc = attend(d, acc, [attn_four, attn_other])

    middle, x_two, mlp_grad = line.run(
        middle_kernel,
        "middle",
        [kept(wide_shape, F32), kept(wide_shape, BF16), kept(wide_shape, BF16)],
        [
            acc,
            tok,
            mask,
            grad,
            vecs,
        ],
    )

    group, bits = {}, {}

    def run_jobs(plan):
        jobs = []
        for step, name in plan:
            counts = {"core": (2, 2), "hop": (1, 1), "fan": (1, 1, 1, 1), "end": (1,)}[step]
            jobs.append((group[name], counts, 2 if step == "end" and name[0] == "a" else 1))
        jobs = Jobs(jobs)

        def store(outs):
            for (step, name), made in zip(plan, jobs.split(outs), strict=True):
                group[name] = made
                hops[name] = hops.get(name, 0) + 1

        return jobs, store

    hops = {}

    def send(*names, after=()):
        leaves = [group[name][1] for name in names]
        if after:
            leaves = line.gate(*leaves, waits=[group[name][1] for name in after])
        for name, leave in zip(names, leaves, strict=True):
            group[name] = [group[name][0], across(leave, bits[name][hops[name] - 1])]

    def sums_of(*plan, flops=FLOPS):
        jobs, store = run_jobs(plan)
        outs = line.run(
            functools.partial(sum_kernel, jobs),
            "sum_" + "_".join(step + name for step, name in plan),
            jobs.outs(),
            jobs.arrays(),
            flops=flops,
        )
        store(outs)

    def pause(*waits):
        line.run(lambda *refs: None, "pause", [], [], waits=waits)

    mlp_sums = []
    in_cols = [None] * count
    mlp_order = []

    def feed(d, weights, *plan):
        own = d == 0
        name = f"m{len(mlp_order)}"
        side_first = len(mlp_order) % 2 == 0
        mlp_order.append(d)
        bits[name] = (SIDE, DEEP) if side_first else (DEEP, SIDE)
        jobs, store = run_jobs(plan)
        outs = line.run(
            functools.partial(mlp_kernel, own, SIDE_FIRST if side_first else DEEP_FIRST, jobs),
            f"mlp{d}",
            [
                kept(wide_shape, F32),
                kept(wide_shape, F32),
                kept((1, width), F32),
                kept((4, 2, piece_rows, width), BF16),
                kept((4, 2, piece_rows, width), BF16),
            ]
            + jobs.outs(),
            [*weights, x_two, mlp_grad, smalls[d], *mlp_sums, *jobs.arrays()],
            scalar=place_ref,
            scratch=[pltpu.VMEM((width, width), BF16)] * (2 if own else 4),
        )
        mlp_sums[:] = outs[:2]
        in_cols[d] = outs[2]
        store(outs[5:])
        group[name] = [outs[3], across(outs[4], CORE)]

    full = {}
    full[2] = stack("stack2", planes[2])
    full[2] = [full[2], across(full[2], CORE)]
    planes[1] = plane(zones[1][None])
    feed(0, [in_weight, down_weight])
    pause(full[2][1])
    feed(2, full[2], ("core", "m0"))
    full[1] = stack("stack1", planes[1])
    full[1] = [full[1], across(full[1], CORE)]
    send("m0")
    sums_of(("core", "m1"))
    send("m1")
    last_zone = line.gate(zones[count - 1])[:, None]
    full[count - 1] = [last_zone, across(last_zone, CORE)]
    feed(1, full[1])
    feed(count - 1, full[count - 1])

    jobs, store = run_jobs([])
    layer, middle_grad, attn_grad, mid_sums, *outs = line.run(
        functools.partial(turn_kernel, jobs),
        "turn",
        [kept(wide_shape, BF16), kept(wide_shape, F32), kept(wide_shape, BF16), kept((8, width), F32)]
        + jobs.outs(),
        [
            middle,
            *mlp_sums,
            grad,
            acc,
            vecs,
            *jobs.arrays(),
        ],
    )
    store(outs)

    back_sum = []
    qkv_cols, grids = [None] * count, [None] * count
    back_order = []
    half = []

    def attend_back(d, *plan):
        second = len(half) == 1
        name = f"a{len(back_order) // 2}"
        side_first = name == "a0"
        first = not back_sum
        back_order.append(d)
        bits[name] = (SIDE, DEEP) if side_first else (DEEP, SIDE)
        jobs, store = run_jobs(plan)
        mats, *others = held[d]
        piece_arrays = [kept((4, 2, piece_rows, width), BF16)] * 2
        outs = line.run(
            functools.partial(attend_back_kernel, d == 0, first, SIDE_FIRST if side_first else DEEP_FIRST, second, jobs),
            f"attend_back{d}",
            [kept(wide_shape, F32), kept((1, 3 * local), F32), kept((heads, PAD, PAD), F32)]
            + (piece_arrays if second else [kept((width, width), BF16)])
            + jobs.outs(),
            [*mats, x_one, attn_grad, *others, *back_sum, *half, *jobs.arrays()],
            scalar=place_ref,
            scratch=[pltpu.VMEM((width, width), BF16)] * second + [pltpu.VMEM((rows, 3 * local), BF16)],
        )
        back_sum[:] = outs[:1]
        qkv_cols[d], grids[d] = outs[1:3]
        store(outs[5 if second else 4 :])
        if second:
            group[name] = [outs[3], outs[4]]
            half.clear()
        else:
            half.append(outs[3])

    pause(group["m0"][1], group["m1"][1])
    sums_of(("hop", "m0"), ("hop", "m1"), ("core", "m2"), ("core", "m3"))
    send("m0", "m1")
    send("m2", "m3")
    attend_back(1)
    attend_back(2)
    attend_back(3, ("end", "m0"), ("end", "m1"))
    home = {0: group["m0"][0], 2: along(group["m1"][0], 2)}
    attend_back(0)

    tok_grad, last_sums = line.run(
        last_kernel,
        "last",
        [kept(wide_shape, BF16), kept((8, width), F32)],
        [tok, mask, middle_grad, *back_sum, vecs],
    )
    highs = width // LOW
    blocks = -(-seq // 8)

    def make_table(begin, end):
        return line.run(
            functools.partial(table_kernel, count, begin, end),
            f"table{begin}",
            [kept((count * heads * highs, LOW), F32)],
            [index, *grids],
            flops=0,
        )[0]

    def come_home(name, pieces):
        jobs = Jobs([([pieces[d] for d in range(count)], (1,), 1)])
        done = line.run(functools.partial(sum_kernel, jobs), name, jobs.outs(), jobs.arrays())[0]
        return rest_of_wide(done)

    sums_of(("hop", "m2"), ("hop", "m3"))
    send("m2", "m3")
    for name, leave in zip(("a0", "a1"), line.gate(group["a0"][1], group["a1"][1]), strict=True):
        group[name][1] = across(leave, CORE)
    table = make_table(0, blocks // 2)
    sums_of(("core", "a0"), ("core", "a1"))
    send("a0", "a1")
    more_table = make_table(blocks // 2, blocks)
    sums_of(("end", "m2"), ("end", "m3"), flops=0)
    home[1] = along(group["m2"][0], 1)
    home[3] = along(group["m3"][0], 3)
    flat = line.run(
        functools.partial(pack_kernel, count),
        "pack",
        [kept((SHARED + count * PART, width), F32)],
        [last_sums, mid_sums, table, more_table, *qkv_cols, *in_cols],
        scalar=place_ref,
        waits=[home[2]],
    )[0]
    sums_of(("hop", "a0"), ("hop", "a1"))
    send("a0", "a1")
    pause()
    mlp_home = come_home("home_mlp", home)
    mlp_side, mlp_deep = across(mlp_home, SIDE), across(mlp_home, DEEP)
    own_home, *leaving = line.run(
        functools.partial(leave_kernel, count),
        "leave",
        [kept((piece_rows + SENT, width), F32)] + [kept((piece_rows + SENT, width), BF16)] * (count - 1),
        [*group["a0"], *group["a1"], flat],
        scalar=place_ref,
    )
    came = [along(leaving[d - 1], d) for d in (2, 1, 3)]

    def rows_first(values):
        values = line.gate(values)
        return values.reshape(pages, PAD, width)[:, :seq].transpose(1, 0, 2)

    layer_out, tokens_out = line.gate(rows_first(layer), rows_first(tok_grad), place=sent)
    pause(layer_out, tokens_out)
    mlp_side, mlp_deep = line.gate(mlp_side, mlp_deep)
    mlp_far = across(mlp_side, DEEP)
    pause()
    attn_home = line.run(
        home_kernel, "home_attn", [kept((1, 1, piece_rows + SENT, width), BF16)], [own_home, *came]
    )[0]
    attn_home = rest_of_wide(attn_home)
    attn_came = [attn_home] + [across(attn_home, bit) for bit in (SIDE, DEEP, SIDE | DEEP)]
    mlp_four = stack("stack_mlp", [mlp_home, mlp_side, mlp_deep, mlp_far])
    mlp_other = across(mlp_four, CORE)
    pause()
    in_w_grad, down_w_grad = line.run(
        mlp_final_kernel,
        "mlp_final",
        [sent((width, width), F32)] * 2,
        [mlp_four, mlp_other],
        scalar=place_ref,
    )
    attn_four = stack("stack_attn_home", attn_came)
    attn_other = across(attn_four, CORE)
    qkv_w_grad, out_w_grad, total = final_call(
        attend_final_kernel,
        "attend_final",
        [sent((3 * local, width), F32), sent((local, width), F32), kept((SENT, width), F32)],
        place_ref,
        [attn_four, attn_other],
        line.token,
        scratch=[pltpu.VMEM((width, width), F32)],
    )

    return (
        layer_out.transpose(1, 0, 2),
        tokens_out.transpose(1, 0, 2),
        total[0],
        total[1],
        total[2],
        qkv_w_grad.reshape(3, local, width).transpose(2, 0, 1),
        total[9, :local],
        total[9, 2 * local : 3 * local],
        total[11 : 11 + heads, :bucket_count],
        out_w_grad,
        total[3],
        total[4],
        total[5],
        total[6],
        in_w_grad,
        total[10],
        down_w_grad,
        total[7],
        total[8],
    )


def solution(mesh):
    placed = (
        P(None, ("wide", "narrow"), None),
        P(None, ("wide", "narrow")),
        P(),
        P(),
        P(),
        P(),
        P(None, None, "narrow"),
        P("narrow"),
        P("narrow"),
        P("narrow", None),
        P("narrow", None),
        P(),
        P(),
        P(),
        P(),
        P(None, "narrow"),
        P("narrow"),
        P("narrow", None),
        P(),
        P(),
        P(None, ("wide", "narrow"), None),
    )
    return jax.shard_map(
        body,
        mesh=mesh,
        in_specs=placed,
        out_specs=(
            P(None, ("wide", "narrow"), None),
            P(None, ("wide", "narrow"), None),
            P(),
            P(),
            P(),
            P(None, None, "narrow"),
            P("narrow"),
            P("narrow"),
            P("narrow", None),
            P("narrow", None),
            P(),
            P(),
            P(),
            P(),
            P(None, "narrow"),
            P("narrow"),
            P("narrow", None),
            P(),
            P(),
        ),
        check_vma=False,
    )
```

```python
import functools

import jax
import jax.numpy as jnp
from jax import lax
from jax.experimental import pallas as pl
from jax.experimental.pallas import tpu as pltpu
from jax.sharding import PartitionSpec as P


SEQ = 197
PAD = 208
LANES = 256
EPSILON = 1e-06
ROOT_HALF = 0.7071067811865476
DENSITY = 0.3989422804014327
CORE, SIDE, DEEP = 1, 2, 4
PIECES = 8
LOW = 128
NEGATIVE = -1e30
FLOPS = 2 * 10**10
F32 = jnp.float32
BF16 = jnp.bfloat16

NN = (((1,), (0,)), ((), ()))
NT = (((1,), (1,)), ((), ()))
TN = (((0,), (0,)), ((), ()))


def mul(left, right, dims=NN):
    return lax.dot_general(left, right, dims, preferred_element_type=F32)


def vmem():
    return pl.BlockSpec(memory_space=pltpu.VMEM)


def anywhere():
    return pl.BlockSpec(memory_space=pl.ANY)


def scalars():
    return pl.BlockSpec(memory_space=pltpu.SMEM)


def near(values):
    return pltpu.with_memory_space_constraint(values, pltpu.VMEM)


def kept(shape, dtype):
    return pltpu.VMEM(shape, dtype)


def sent(shape, dtype):
    return jax.ShapeDtypeStruct(shape, dtype)


def call(kernel, name, outs, in_specs, out_specs=None, scratch=(), flops=FLOPS, limit=12, aliases=None):
    made = pl.pallas_call(
        kernel,
        out_shape=outs,
        in_specs=in_specs,
        out_specs=out_specs or [vmem()] * len(outs),
        scratch_shapes=list(scratch),
        input_output_aliases=aliases or {},
        compiler_params=pltpu.CompilerParams(vmem_limit_bytes=limit * 1024 * 1024),
        cost_estimate=pl.CostEstimate(flops=flops, bytes_accessed=0, transcendentals=0),
        name=name,
    )
    return lambda *arrays: made(
        *[near(a) if spec.memory_space == pltpu.VMEM else a for spec, a in zip(in_specs, arrays, strict=True)]
    )


class Line:
    def __init__(self):
        self.token = None

    def run(self, kernel, name, outs, arrays, scalar=None, waits=(), scratch=(), flops=FLOPS, limit=12):
        before = list(waits) + ([] if self.token is None else [self.token])
        start, n_in = (0 if scalar is None else 1), len(arrays)

        def whole(*refs):
            inputs = refs[: start + n_in]
            rest = refs[start + n_in + len(before) :]
            rest[len(outs)][...] = jnp.zeros((8, 128), F32)
            kernel(*inputs, *rest[: len(outs)], *rest[len(outs) + 1 :])

        made = call(
            whole,
            name,
            outs + [kept((8, 128), F32)],
            [scalars()] * start + [vmem()] * n_in + [anywhere()] * len(before),
            scratch=scratch,
            flops=flops,
            limit=limit,
        )(*([] if scalar is None else [scalar]), *arrays, *before)
        self.token = made[-1]
        return made[:-1]

    def gate(self, *arrays, waits=(), place=kept):
        n = len(arrays)
        made = call(
            lambda *refs: None,
            "gate",
            [place(a.shape, a.dtype) for a in arrays],
            [anywhere()] * (n + 1 + len(waits)),
            out_specs=[anywhere()] * n,
            aliases={i: i for i in range(n)},
            flops=0,
        )(*[near(a) if place is kept else a for a in arrays], self.token, *waits)
        return made[0] if n == 1 else made


class Jobs:
    def __init__(self, jobs):
        self.jobs = jobs

    def arrays(self):
        return [a for arrays, _, _ in self.jobs for a in arrays]

    def outs(self):
        made = []
        for arrays, counts, parts in self.jobs:
            _, mats, *rest = arrays[0].shape
            made += [kept((count, mats // parts, *rest), BF16) for count in counts for _ in range(parts)]
        return made

    def add(self, refs_in, refs_out):
        at_in = at_out = 0
        for arrays, counts, parts in self.jobs:
            sources = refs_in[at_in : at_in + len(arrays)]
            at_in += len(arrays)
            mats = arrays[0].shape[1] // parts
            first = 0
            for count in counts:
                for part in range(parts):
                    for i in range(count):
                        for j in range(mats):
                            at = (first + i, part * mats + j)
                            total = sources[0][at].astype(F32)
                            for source in sources[1:]:
                                total = total + source[at].astype(F32)
                            refs_out[at_out][i, j] = total.astype(BF16)
                    at_out += 1
                first += count

    def split(self, outs):
        made, at = [], 0
        for _, counts, parts in self.jobs:
            made.append(list(outs[at : at + len(counts) * parts]))
            at += len(counts) * parts
        return made


def final_call(kernel, name, outs, scalar, arrays, token, scratch=()):
    n_in = 1 + len(arrays)
    return call(
        lambda *refs: kernel(*refs[:n_in], *refs[n_in + 1 :]),
        name,
        outs,
        [scalars()] + [vmem()] * len(arrays) + [anywhere()],
        scratch=scratch,
    )(scalar, *arrays, token)


def norm_parts(values):
    center = values - jnp.mean(values, axis=-1, keepdims=True)
    spread = jnp.mean(center * center, axis=-1, keepdims=True)
    inverse = lax.rsqrt(spread + EPSILON)
    return center * inverse, inverse


def norm_back(grad, normed, inverse, gain):
    scaled = grad * gain
    inner = jnp.mean(scaled, axis=-1, keepdims=True)
    cross = jnp.mean(scaled * normed, axis=-1, keepdims=True)
    return inverse * (scaled - inner - normed * cross)


def col(values):
    return jnp.sum(values, axis=0, keepdims=True)


SMALL = 8
VECTORS = 5


TOKEN, FIRST_GAIN, FIRST_SHIFT, OUT_BIAS, ATTN_SCALE, SECOND_GAIN, SECOND_SHIFT, MLP_SCALE, DOWN_BIAS = range(9)


def row(ref, number):
    return ref[number : number + 1, :]


def first_kernel(tok_ref, mask_ref, vec_ref, out_ref):
    masked = jnp.where(mask_ref[...] > 0.0, row(vec_ref, TOKEN), tok_ref[...].astype(F32))
    normed, _ = norm_parts(masked)
    out = normed * row(vec_ref, FIRST_GAIN) + row(vec_ref, FIRST_SHIFT)
    rows = lax.broadcasted_iota(jnp.int32, (tok_ref.shape[0], 1), 0)
    real = lax.rem(rows, PAD) < SEQ
    out_ref[...] = jnp.where(real, out, 0.0).astype(BF16)


def bias_kernel(buckets_ref, small_ref, out_ref):
    heads = out_ref.shape[0]
    parts = small_ref.shape[1] // 128
    for half in range(2):
        lanes = pl.ds(half * 128, 128)
        index = buckets_ref[:, lanes]
        low = lax.bitwise_and(index, 127)
        high = lax.shift_right_logical(index, 7)
        column = lax.broadcasted_iota(jnp.int32, index.shape, 1) + half * 128
        for head in range(heads):
            total = jnp.full(index.shape, NEGATIVE, F32)
            for part in range(parts):
                values = small_ref[2 + head : 3 + head, part * 128 : (part + 1) * 128]
                values = jnp.broadcast_to(values, index.shape)
                found = jnp.take_along_axis(values, low, axis=1, mode="promise_in_bounds")
                total = jnp.where(high == part, found, total)
            out_ref[head, :, lanes] = jnp.where(column < SEQ, total, NEGATIVE)


def stack_kernel(*refs):
    for i, ref in enumerate(refs[:-1]):
        refs[-1][i] = ref[...]


def start_kernel(w_ref, small_ref, qkv_ref, out_ref, piece_ref, own_ref, sem):
    place = w_ref[0]
    rows = piece_ref.shape[0] - 2 * SMALL
    cut = qkv_ref.shape[0] // rows

    def bring(ref, number):
        copy = pltpu.make_async_copy(
            ref.at[pl.ds(pl.multiple_of(number * rows, rows), rows), :], own_ref, sem
        )
        copy.start()
        copy.wait()

    @pl.when(place < cut)
    def _():
        bring(qkv_ref, place)

    @pl.when(place >= cut)
    def _():
        bring(out_ref, place - cut)

    piece_ref[:rows, :] = own_ref[...]
    small = small_ref[:VECTORS, :]
    upper = small.astype(BF16).astype(F32)
    middle = (small - upper).astype(BF16).astype(F32)
    lower = small - upper - middle
    terms = jnp.concatenate([upper, middle, lower, jnp.zeros((1, small.shape[1]), F32)], axis=0)
    piece_ref[rows:, :] = terms.astype(BF16)


def arrive_kernel(count, *refs):
    came, zero_ref, smalls = refs[:count], refs[count], refs[count + 1 :]
    rows = zero_ref.shape[1]
    for i, ref in enumerate(came):
        zero_ref[i] = ref[:rows, :]
        terms = ref[rows:, :].astype(F32)
        smalls[i][...] = jnp.zeros_like(smalls[i])
        smalls[i][:VECTORS, :] = (
            terms[:VECTORS] + terms[VECTORS : 2 * VECTORS] + terms[2 * VECTORS : 3 * VECTORS]
        )


def cut_kernel(w_ref, in_ref, down_ref, four_ref, *own_refs):
    rows = four_ref.shape[1] // 2
    for k in range(four_ref.shape[0]):
        start = pl.multiple_of(lax.bitwise_xor(w_ref[0], 2 * k) * rows, rows)
        for i, ref in enumerate((in_ref, down_ref)):
            part = ref[pl.ds(start, rows), :]
            four_ref[k, i * rows : (i + 1) * rows, :] = part
            for own_ref in own_refs if k == 0 else ():
                own_ref[i * rows : (i + 1) * rows, :] = part


def put_together(w_ref, pair, slot, cut, target):
    rows = target.shape[0] // PIECES
    for piece in range(PIECES):
        start = pl.multiple_of(lax.bitwise_xor(w_ref[0], piece) * rows, rows)
        target[pl.ds(start, rows), :] = pair[piece & CORE][piece >> 1, slot, cut : cut + rows, :]


def take_apart(w_ref, mats, order, keep, send):
    for number, mat in enumerate(mats):
        rows = mat.shape[0] // PIECES
        for piece in range(PIECES):
            start = pl.multiple_of(lax.bitwise_xor(w_ref[0], piece) * rows, rows)
            target = send if piece & CORE else keep
            target[order[piece >> 1], number] = mat[pl.ds(start, rows), :]


def attend_kernel(slot, first, *refs):
    w_ref = refs[0]
    weights = refs[1:3]
    rest = refs[3:]
    x_ref, small_ref, bias_ref = rest[:3]
    rest = rest[3:]
    if not first:
        acc_in = rest[0]
        rest = rest[1:]
    acc_ref, qkv_ref, probs_ref, mixed_ref = rest[:4]
    if first:
        qkv_mat, out_mat = weights
        width = qkv_mat.shape[1]
        local = width // 4
    else:
        mat = rest[4]
        put_together(w_ref, weights, slot, 0, mat)
        width = mat.shape[0]
        local = width // 4
        qkv_mat, out_mat = mat.at[: 3 * local, :], mat.at[3 * local :, :]
    heads = bias_ref.shape[0]
    size = local // heads
    qkv = mul(x_ref[...], qkv_mat[...], NT)
    queries = qkv[:, :local] + small_ref[0:1, :local]
    queries = (queries.astype(BF16).astype(F32) * size ** (-0.5)).astype(BF16)
    keys = qkv[:, local : 2 * local].astype(BF16)
    values = qkv[:, 2 * local :] + small_ref[0:1, LANES : LANES + local]
    values = values.astype(BF16)
    qkv_ref[0] = queries
    qkv_ref[1] = keys
    qkv_ref[2] = values
    lane = lax.broadcasted_iota(jnp.int32, (PAD, local), 1)
    pages = x_ref.shape[0] // PAD
    zero = jnp.zeros((PAD, local), BF16)
    for page in range(pages):
        rows = slice(page * PAD, (page + 1) * PAD)
        q, k, v = queries[rows], keys[rows], values[rows]
        mixed = jnp.zeros((PAD, local), F32)
        for head in range(heads):
            own = (lane >= head * size) & (lane < (head + 1) * size)
            scores = mul(jnp.where(own, q, zero), k, NT) + bias_ref[head][:, :PAD]
            top = jnp.max(scores, axis=1, keepdims=True)
            power = jnp.exp(scores - top)
            total = jnp.sum(power, axis=1, keepdims=True)
            probs = (power * (1.0 / total)).astype(BF16)
            probs_ref[page * heads + head] = probs
            mixed = mixed + mul(probs, jnp.where(own, v, zero))
        mixed_ref[rows, :] = mixed.astype(BF16)
    out = mul(mixed_ref[...], out_mat[...])
    acc_ref[...] = out if first else acc_in[...] + out


def middle_kernel(acc_ref, tok_ref, mask_ref, grad_ref, vec_ref, mid_ref, x_ref, mg_ref):
    masked = jnp.where(mask_ref[...] > 0.0, row(vec_ref, TOKEN), tok_ref[...].astype(F32))
    middle = masked + row(vec_ref, ATTN_SCALE) * (acc_ref[...] + row(vec_ref, OUT_BIAS))
    mid_ref[...] = middle
    normed, _ = norm_parts(middle)
    x_ref[...] = (normed * row(vec_ref, SECOND_GAIN) + row(vec_ref, SECOND_SHIFT)).astype(BF16)
    mg_ref[...] = (grad_ref[...].astype(F32) * row(vec_ref, MLP_SCALE)).astype(BF16)


def mlp_kernel(first, order, jobs, *refs):
    w_ref = refs[0]
    weights = refs[1:3]
    rest = refs[3:]
    x_ref, mg_ref, small_ref = rest[:3]
    rest = rest[3:]
    if not first:
        out_in, grad_in = rest[:2]
        rest = rest[2:]
    n_jobs = len(jobs.arrays())
    jobs_in, rest = rest[:n_jobs], rest[n_jobs:]
    out_ref, grad_ref, col_ref, keep, send = rest[:5]
    rest = rest[5:]
    n_jobs = len(jobs.outs())
    jobs_out, rest = rest[:n_jobs], rest[n_jobs:]
    in_grad, down_grad = rest[:2]
    if first:
        in_mat, down_mat = weights
    else:
        in_mat, down_mat = rest[2:]
        put_together(w_ref, weights, 0, 0, in_mat)
        put_together(w_ref, weights, 0, in_mat.shape[0] // PIECES, down_mat)
    jobs.add(jobs_in, jobs_out)
    width = in_mat.shape[0]
    x = x_ref[...]
    mg = mg_ref[...]
    out = None
    back = None
    for start in range(0, width, 256):
        units = slice(start, start + 256)
        weight_in = in_mat[:, units]
        weight_down = down_mat[units, :]
        pre = mul(x, weight_in) + small_ref[1:2, units]
        phi = 0.5 * (1.0 + lax.erf(pre * ROOT_HALF))
        hidden = (pre * phi).astype(BF16)
        slope = phi + pre * (DENSITY * jnp.exp(-0.5 * pre * pre))
        part = mul(hidden, weight_down)
        out = part if out is None else out + part
        hidden_grad = mul(mg, weight_down, NT)
        pre_grad = hidden_grad * slope
        low = pre_grad.astype(BF16)
        col_ref[:, units] = col(low.astype(F32))
        part = mul(low, weight_in, NT)
        back = part if back is None else back + part
        down_grad[units, :] = mul(hidden, mg, TN).astype(BF16)
        in_grad[:, units] = mul(x, low, TN).astype(BF16)
    out_ref[...] = out if first else out_in[...] + out
    grad_ref[...] = back if first else grad_in[...] + back
    take_apart(w_ref, [in_grad, down_grad], order, keep, send)


def turn_kernel(jobs, *refs):
    mid_ref, out_ref, back_ref, grad_ref, acc_ref, vec_ref = refs[:6]
    refs = refs[6:]
    n_jobs = len(jobs.arrays())
    jobs_in, refs = refs[:n_jobs], refs[n_jobs:]
    layer_ref, mgrad_ref, ag_ref, sums_ref = refs[:4]
    jobs.add(jobs_in, refs[4:])
    middle = mid_ref[...]
    grad = grad_ref[...].astype(F32)
    mlp_out = out_ref[...] + row(vec_ref, DOWN_BIAS)
    layer_ref[...] = (middle + row(vec_ref, MLP_SCALE) * mlp_out).astype(BF16)
    normed, inverse = norm_parts(middle)
    second = back_ref[...]
    middle_grad = grad + norm_back(second, normed, inverse, row(vec_ref, SECOND_GAIN))
    mgrad_ref[...] = middle_grad
    scaled = middle_grad * row(vec_ref, ATTN_SCALE)
    ag_ref[...] = scaled.astype(BF16)
    sums_ref[0:1, :] = col(scaled)
    sums_ref[1:2, :] = col(middle_grad * (acc_ref[...] + row(vec_ref, OUT_BIAS)))
    sums_ref[2:3, :] = col(second * normed)
    sums_ref[3:4, :] = col(second)
    sums_ref[4:5, :] = col(grad * row(vec_ref, MLP_SCALE))
    sums_ref[5:6, :] = col(grad * mlp_out)
    sums_ref[6:8, :] = jnp.zeros_like(sums_ref[6:8, :])


def attend_back_kernel(own, first, order, second, jobs, *refs):
    w_ref = refs[0]
    if own:
        qkv_mat, out_mat = refs[1:3]
        rest = refs[3:]
    else:
        local = refs[1].shape[0] // 4
        qkv_mat, out_mat = refs[1].at[: 3 * local, :], refs[1].at[3 * local :, :]
        rest = refs[2:]
    x_ref, ag_ref, qkv_ref, probs_ref, mixed_ref = rest[:5]
    rest = rest[5:]
    if not first:
        grad_in = rest[0]
        rest = rest[1:]
    if second:
        other_grad = rest[0]
        rest = rest[1:]
    n_jobs = len(jobs.arrays())
    jobs_in, rest = rest[:n_jobs], rest[n_jobs:]
    grad_ref, col_ref, grid_ref = rest[:3]
    if second:
        keep, send = rest[3:5]
        rest = rest[5:]
    else:
        mat_grad = rest[3]
        rest = rest[4:]
    n_jobs = len(jobs.outs())
    jobs_out, rest = rest[:n_jobs], rest[n_jobs:]
    if second:
        mat_grad, dqkv = rest
    else:
        (dqkv,) = rest
    jobs.add(jobs_in, jobs_out)
    local = out_mat.shape[0]
    heads = grid_ref.shape[0]
    size = local // heads
    ag = ag_ref[...]
    mixed_grad = mul(ag, out_mat[...], NT).astype(BF16)
    mat_grad[3 * local :, :] = mul(mixed_ref[...], ag, TN).astype(BF16)
    lane = lax.broadcasted_iota(jnp.int32, (PAD, local), 1)
    pages = x_ref.shape[0] // PAD
    zero = jnp.zeros((PAD, local), BF16)
    for page in range(pages):
        rows = slice(page * PAD, (page + 1) * PAD)
        q, v, dm = qkv_ref[0, rows, :], qkv_ref[2, rows, :], mixed_grad[rows]
        k = (qkv_ref[1, rows, :].astype(F32) * size ** (-0.5)).astype(BF16)
        dq = jnp.zeros((PAD, local), F32)
        dk = jnp.zeros((PAD, local), F32)
        dv = jnp.zeros((PAD, local), F32)
        for head in range(heads):
            own = (lane >= head * size) & (lane < (head + 1) * size)
            dmh = jnp.where(own, dm, zero)
            probs_low = probs_ref[page * heads + head]
            probs = probs_low.astype(F32)
            weighed = probs * mul(dmh, v, NT)
            score = weighed - probs * jnp.sum(weighed, axis=1, keepdims=True)
            low = score.astype(BF16)
            if page == 0:
                grid_ref[head] = low.astype(F32)
            else:
                grid_ref[head] = grid_ref[head] + low.astype(F32)
            dq = dq + mul(low, jnp.where(own, k, zero))
            dk = dk + mul(low, jnp.where(own, q, zero), TN)
            dv = dv + mul(probs_low, dmh, TN)
        dqkv[rows, :] = jnp.concatenate([dq, dk, dv], axis=1).astype(BF16)
    grads = dqkv[...]
    mat_grad[: 3 * local, :] = mul(grads, x_ref[...], TN).astype(BF16)
    col_ref[...] = col(grads.astype(F32))
    back = mul(grads, qkv_mat[...])
    grad_ref[...] = back if first else grad_in[...] + back
    if second:
        take_apart(w_ref, [other_grad, mat_grad], order, keep, send)


def last_kernel(tok_ref, mask_ref, mgrad_ref, first_ref, vec_ref, grad_ref, sums_ref):
    mask = mask_ref[...] > 0.0
    masked = jnp.where(mask, row(vec_ref, TOKEN), tok_ref[...].astype(F32))
    normed, inverse = norm_parts(masked)
    first = first_ref[...]
    in_grad = mgrad_ref[...] + norm_back(first, normed, inverse, row(vec_ref, FIRST_GAIN))
    grad_ref[...] = jnp.where(mask, 0.0, in_grad).astype(BF16)
    sums_ref[0:1, :] = col(jnp.where(mask, in_grad, 0.0))
    sums_ref[1:2, :] = col(first * normed)
    sums_ref[2:3, :] = col(first)
    sums_ref[3:8, :] = jnp.zeros_like(sums_ref[3:8, :])


def table_kernel(grid_count, begin, end, *refs):
    buckets_ref = refs[0]
    grids = refs[1 : 1 + grid_count]
    out_ref = refs[1 + grid_count]
    heads = grids[0].shape[0]
    highs = out_ref.shape[0] // (grid_count * heads)
    out_ref[...] = jnp.zeros_like(out_ref)

    def step(block, _):
        base = pl.multiple_of(block * 8, 8)
        index = buckets_ref[pl.ds(base, 8), :][:, :PAD]
        loads = [[g[h, pl.ds(base, 8), :] for h in range(heads)] for g in grids]
        total = None
        for row in range(8):
            one = index[row : row + 1]
            low = lax.bitwise_and(one, LOW - 1)
            high = lax.shift_right_logical(one, LOW.bit_length() - 1)
            right = (
                jnp.broadcast_to(low, (LOW, PAD)) == lax.broadcasted_iota(jnp.int32, (LOW, PAD), 0)
            ).astype(F32).astype(BF16)
            match = jnp.broadcast_to(high, (highs, PAD)) == lax.broadcasted_iota(
                jnp.int32, (highs, PAD), 0
            )
            left = jnp.concatenate(
                [
                    jnp.where(match, jnp.broadcast_to(loads[g][h][row : row + 1], (highs, PAD)), 0.0)
                    for g in range(grid_count)
                    for h in range(heads)
                ],
                axis=0,
            ).astype(BF16)
            part = mul(left, right, NT)
            total = part if total is None else total + part
        out_ref[...] += total
        return 0

    lax.fori_loop(begin, end, step, 0)


def sum_kernel(jobs, *refs):
    n_in, n_out = len(jobs.arrays()), len(jobs.outs())
    jobs.add(refs[:n_in], refs[n_in : n_in + n_out])


SHARED = 16
PART = 8
SENT = 16


def pack_kernel(count, w_ref, last_ref, mid_ref, table_ref, table_more_ref, *refs):
    qkv_cols, in_cols, out_ref = refs[:count], refs[count : 2 * count], refs[2 * count]
    out_ref[...] = jnp.zeros_like(out_ref)
    out_ref[0:3, :] = last_ref[0:3, :]
    out_ref[3:9, :] = mid_ref[0:6, :]
    tables = table_ref.shape[0] // count
    parts = out_ref.shape[1] // LOW
    for d in range(count):
        base = SHARED + d * PART
        out_ref[base : base + 1, : qkv_cols[d].shape[1]] = qkv_cols[d][...]
        out_ref[base + 1 : base + 2, :] = in_cols[d][...]
        for k in range(tables):
            at = d * tables + k
            lanes = slice(k % parts * LOW, (k % parts + 1) * LOW)
            out_ref[base + 2 + k // parts : base + 3 + k // parts, lanes] = row(table_ref, at) + row(table_more_ref, at)
    held = out_ref[SHARED:, :]
    for d in range(count):
        shard = lax.rem(w_ref[1] + d, count)
        out_ref[pl.ds(pl.multiple_of(SHARED + shard * PART, 8), PART), :] = held[d * PART : (d + 1) * PART]


def leave_kernel(count, w_ref, stay_a, came_a, stay_b, came_b, flat_ref, *outs):
    rows = stay_a.shape[2]
    pairs = [(stay_b, came_b, 1), (stay_a, came_a, 0), (stay_a, came_a, 1), (stay_b, came_b, 0)]
    for d in range(count):
        stay, came, slot = pairs[d]
        total = stay[0, slot].astype(F32) + came[0, slot].astype(F32)
        shard = lax.rem(w_ref[1] + d, count)
        part = flat_ref[pl.ds(pl.multiple_of(SHARED + shard * PART, 8), PART), :]
        small = jnp.concatenate(
            [flat_ref[:9, :], part[:5], jnp.zeros((SENT - 14, part.shape[1]), F32)], axis=0
        )
        outs[d][:rows, :] = total.astype(outs[d].dtype)
        outs[d][rows:, :] = small.astype(outs[d].dtype)


def home_kernel(own_ref, *refs):
    came, done_ref = refs[:-1], refs[-1]
    total = own_ref[...]
    for ref in came:
        total = total + ref[...].astype(F32)
    done_ref[0, 0] = total.astype(BF16)


def assemble(w_ref, pair, number, place_in):
    rows = place_in.shape[0] // PIECES
    for piece in range(PIECES):
        start = pl.multiple_of(lax.bitwise_xor(w_ref[0], piece) * rows, rows)
        place_in[pl.ds(start, rows), :] = pair[piece & CORE][piece >> 1, 0, number, :rows, :].astype(F32)


def mlp_final_kernel(w_ref, own_ref, other_ref, in_ref, down_ref):
    assemble(w_ref, (own_ref, other_ref), 0, in_ref)
    assemble(w_ref, (own_ref, other_ref), 1, down_ref)


def attend_final_kernel(w_ref, own_ref, other_ref, qkv_ref, out_ref, small_ref, table_ref, whole):
    assemble(w_ref, (own_ref, other_ref), 0, whole)
    cut = qkv_ref.shape[0]
    qkv_ref[...] = whole[:cut, :]
    out_ref[...] = whole[cut:, :]
    rows = whole.shape[0] // PIECES
    total = jnp.zeros(small_ref.shape, F32)
    for ref in (own_ref, other_ref):
        for chip in range(ref.shape[0]):
            total = total + ref[chip, 0, 0, rows:, :].astype(F32)
    small_ref[...] = total
    table_ref[...] = total[11 : 11 + table_ref.shape[0], : table_ref.shape[1]]


SIDE_FIRST = (0, 2, 1, 3)
DEEP_FIRST = (0, 1, 2, 3)


def body(
    tokens,
    page_mask,
    buckets,
    mask_token,
    first_gain,
    first_shift,
    qkv_weight,
    query_bias,
    value_bias,
    position_bias,
    out_weight,
    out_bias,
    attn_scale,
    second_gain,
    second_shift,
    in_weight,
    in_bias,
    down_weight,
    down_bias,
    mlp_scale,
    out_grad,
):
    pages, seq, width = tokens.shape
    count = lax.axis_size("narrow")
    local = qkv_weight.shape[2]
    heads, bucket_count = position_bias.shape
    rows = pages * PAD
    piece_rows = width // PIECES
    place = lax.bitwise_and(lax.axis_index("wide").astype(jnp.int32), PIECES - 1)
    place_ref = jnp.stack([place, lax.axis_index("narrow").astype(jnp.int32)])
    wide_shape = (rows, width)
    line = Line()

    def across(values, bit):
        others = lax.axis_size("wide")
        return lax.ppermute(values, "wide", [(i, i ^ bit) for i in range(others)])

    def along(values, step):
        return lax.ppermute(values, "narrow", [(i, (i + step) % count) for i in range(count)])

    def rest_of_wide(values):
        bit = PIECES
        while bit < lax.axis_size("wide"):
            values = (values.astype(F32) + across(values, bit).astype(F32)).astype(values.dtype)
            bit *= 2
        return values

    def plane(values):
        values = line.gate(values)
        return [values] + [across(values, bit) for bit in (SIDE, DEEP, SIDE | DEEP)]

    def stack(name, arrays, waits=()):
        return line.run(
            stack_kernel, name, [kept((len(arrays),) + arrays[0].shape, BF16)], list(arrays), waits=waits
        )[0]

    vecs = jnp.stack(
        [
            mask_token,
            first_gain,
            first_shift,
            out_bias,
            attn_scale,
            second_gain,
            second_shift,
            mlp_scale,
            down_bias,
        ]
    )
    tables = jnp.pad(position_bias, ((0, SMALL - 2 - heads), (0, width - bucket_count)))
    spare = width - LANES - local
    shifts = jnp.pad(query_bias, (0, width - local)) + jnp.pad(value_bias, (LANES, spare))
    small = jnp.concatenate([shifts[None], in_bias[None], tables], axis=0)
    qkv_own = qkv_weight.transpose(1, 2, 0).reshape(3 * local, width)
    piece = call(
        start_kernel,
        "start",
        [kept((piece_rows + 2 * SMALL, width), BF16)],
        [scalars(), vmem(), anywhere(), anywhere()],
        scratch=[pltpu.VMEM((piece_rows, width), BF16), pltpu.SemaphoreType.DMA],
    )(place_ref, small, qkv_own, out_weight)[0]
    attn_came = [along(piece, -step) for step in range(1, count)]
    smalls = [small]

    fill = ((0, 0), (0, PAD - seq), (0, 0))
    tok = jnp.pad(tokens, fill).reshape(rows, width)
    grad = jnp.pad(out_grad, fill).reshape(rows, width)
    flags = (page_mask > 0) & (jnp.arange(seq, dtype=jnp.int32) % SEQ != 0)
    mask = jnp.pad(flags.astype(F32), ((0, 0), (0, PAD - seq))).reshape(rows, 1)
    index = jnp.pad(buckets, ((0, PAD - seq), (0, LANES - seq)))

    four_mlp, *own_mlp = line.run(
        cut_kernel,
        "cut",
        [kept((4, 2 * piece_rows, width), BF16)] + [kept((2 * piece_rows, width), BF16)] * (count - 2),
        [in_weight, down_weight],
        scalar=place_ref,
    )
    x_one = line.run(
        first_kernel,
        "first",
        [kept(wide_shape, BF16)],
        [tok, mask, vecs],
    )[0]
    biases = []

    def make_bias(d, waits=()):
        biases.append(
            line.run(
                bias_kernel, f"bias{d}", [kept((heads, PAD, LANES), F32)], [index, smalls[d]], waits=waits
            )[0]
        )

    make_bias(0)
    zones = {}
    attn_zero, *others = line.run(
        functools.partial(arrive_kernel, count - 1),
        "arrive",
        [kept((count - 1, piece_rows, width), BF16)] + [kept((SMALL, width), F32)] * (count - 1),
        attn_came,
    )
    smalls += others
    attn_came = plane(attn_zero)
    for step in range(1, count - 1):
        zones[step] = along(line.gate(own_mlp[step - 1]), -step)

    held = []

    def attend(d, acc, weights, waits=()):
        own = d == 0
        made = line.run(
            functools.partial(attend_kernel, d - 1, own),
            f"attend{d}",
            [
                kept(wide_shape, F32),
                kept((3, rows, local), BF16),
                kept((pages * heads, PAD, PAD), BF16),
                kept((rows, local), BF16),
            ]
            + ([] if own else [kept((width, width), BF16)]),
            [*weights, x_one, smalls[d], biases[d]] + ([] if own else [acc]),
            scalar=place_ref,
            waits=waits,
        )
        held.append((weights if own else [made[4]], *made[1:4]))
        return made[0]

    acc = attend(0, None, [qkv_own, out_weight])
    for d in range(1, count - 1):
        make_bias(d)
    attn_four = stack("stack_attn", attn_came, [zones[step] for step in range(1, count - 1)])
    attn_other = across(attn_four, CORE)
    planes = {2: plane(zones[2][None])}
    zones[count - 1] = along(line.gate(four_mlp), -(count - 1))
    make_bias(count - 1)
    for d in range(1, count):
        acc = attend(d, acc, [attn_four, attn_other])

    middle, x_two, mlp_grad = line.run(
        middle_kernel,
        "middle",
        [kept(wide_shape, F32), kept(wide_shape, BF16), kept(wide_shape, BF16)],
        [
            acc,
            tok,
            mask,
            grad,
            vecs,
        ],
    )

    group, bits = {}, {}

    def run_jobs(plan):
        jobs = []
        for step, name in plan:
            counts = {"core": (2, 2), "hop": (1, 1), "fan": (1, 1, 1, 1), "end": (1,)}[step]
            jobs.append((group[name], counts, 2 if step == "end" and name[0] == "a" else 1))
        jobs = Jobs(jobs)

        def store(outs):
            for (step, name), made in zip(plan, jobs.split(outs), strict=True):
                group[name] = made
                hops[name] = hops.get(name, 0) + 1

        return jobs, store

    hops = {}

    def send(*names, after=()):
        leaves = [group[name][1] for name in names]
        if after:
            leaves = line.gate(*leaves, waits=[group[name][1] for name in after])
        for name, leave in zip(names, leaves, strict=True):
            group[name] = [group[name][0], across(leave, bits[name][hops[name] - 1])]

    def sums_of(*plan, flops=FLOPS):
        jobs, store = run_jobs(plan)
        outs = line.run(
            functools.partial(sum_kernel, jobs),
            "sum_" + "_".join(step + name for step, name in plan),
            jobs.outs(),
            jobs.arrays(),
            flops=flops,
        )
        store(outs)

    def pause(*waits):
        line.run(lambda *refs: None, "pause", [], [], waits=waits)

    mlp_sums = []
    in_cols = [None] * count
    mlp_order = []

    def feed(d, weights, *plan):
        own = d == 0
        name = f"m{len(mlp_order)}"
        side_first = len(mlp_order) % 2 == 0
        mlp_order.append(d)
        bits[name] = (SIDE, DEEP) if side_first else (DEEP, SIDE)
        jobs, store = run_jobs(plan)
        outs = line.run(
            functools.partial(mlp_kernel, own, SIDE_FIRST if side_first else DEEP_FIRST, jobs),
            f"mlp{d}",
            [
                kept(wide_shape, F32),
                kept(wide_shape, F32),
                kept((1, width), F32),
                kept((4, 2, piece_rows, width), BF16),
                kept((4, 2, piece_rows, width), BF16),
            ]
            + jobs.outs(),
            [*weights, x_two, mlp_grad, smalls[d], *mlp_sums, *jobs.arrays()],
            scalar=place_ref,
            scratch=[pltpu.VMEM((width, width), BF16)] * (2 if own else 4),
        )
        mlp_sums[:] = outs[:2]
        in_cols[d] = outs[2]
        store(outs[5:])
        group[name] = [outs[3], across(outs[4], CORE)]

    full = {}
    full[2] = stack("stack2", planes[2])
    full[2] = [full[2], across(full[2], CORE)]
    planes[1] = plane(zones[1][None])
    feed(0, [in_weight, down_weight])
    pause(full[2][1])
    feed(2, full[2], ("core", "m0"))
    full[1] = stack("stack1", planes[1])
    full[1] = [full[1], across(full[1], CORE)]
    send("m0")
    sums_of(("core", "m1"))
    send("m1")
    last_zone = line.gate(zones[count - 1])[:, None]
    full[count - 1] = [last_zone, across(last_zone, CORE)]
    feed(1, full[1])
    feed(count - 1, full[count - 1])

    jobs, store = run_jobs([])
    layer, middle_grad, attn_grad, mid_sums, *outs = line.run(
        functools.partial(turn_kernel, jobs),
        "turn",
        [kept(wide_shape, BF16), kept(wide_shape, F32), kept(wide_shape, BF16), kept((8, width), F32)]
        + jobs.outs(),
        [
            middle,
            *mlp_sums,
            grad,
            acc,
            vecs,
            *jobs.arrays(),
        ],
    )
    store(outs)

    back_sum = []
    qkv_cols, grids = [None] * count, [None] * count
    back_order = []
    half = []

    def attend_back(d, *plan):
        second = len(half) == 1
        name = f"a{len(back_order) // 2}"
        side_first = name == "a0"
        first = not back_sum
        back_order.append(d)
        bits[name] = (SIDE, DEEP) if side_first else (DEEP, SIDE)
        jobs, store = run_jobs(plan)
        mats, *others = held[d]
        piece_arrays = [kept((4, 2, piece_rows, width), BF16)] * 2
        outs = line.run(
            functools.partial(attend_back_kernel, d == 0, first, SIDE_FIRST if side_first else DEEP_FIRST, second, jobs),
            f"attend_back{d}",
            [kept(wide_shape, F32), kept((1, 3 * local), F32), kept((heads, PAD, PAD), F32)]
            + (piece_arrays if second else [kept((width, width), BF16)])
            + jobs.outs(),
            [*mats, x_one, attn_grad, *others, *back_sum, *half, *jobs.arrays()],
            scalar=place_ref,
            scratch=[pltpu.VMEM((width, width), BF16)] * second + [pltpu.VMEM((rows, 3 * local), BF16)],
        )
        back_sum[:] = outs[:1]
        qkv_cols[d], grids[d] = outs[1:3]
        store(outs[5 if second else 4 :])
        if second:
            group[name] = [outs[3], outs[4]]
            half.clear()
        else:
            half.append(outs[3])

    pause(group["m0"][1], group["m1"][1])
    sums_of(("hop", "m0"), ("hop", "m1"), ("core", "m2"), ("core", "m3"))
    send("m0", "m1")
    send("m2", "m3")
    attend_back(1)
    attend_back(2)
    attend_back(3, ("end", "m0"), ("end", "m1"))
    home = {0: group["m0"][0], 2: along(group["m1"][0], 2)}
    attend_back(0)

    tok_grad, last_sums = line.run(
        last_kernel,
        "last",
        [kept(wide_shape, BF16), kept((8, width), F32)],
        [tok, mask, middle_grad, *back_sum, vecs],
    )
    highs = width // LOW
    blocks = -(-seq // 8)

    def make_table(begin, end):
        return line.run(
            functools.partial(table_kernel, count, begin, end),
            f"table{begin}",
            [kept((count * heads * highs, LOW), F32)],
            [index, *grids],
            flops=0,
        )[0]

    def come_home(name, pieces):
        jobs = Jobs([([pieces[d] for d in range(count)], (1,), 1)])
        done = line.run(functools.partial(sum_kernel, jobs), name, jobs.outs(), jobs.arrays())[0]
        return rest_of_wide(done)

    sums_of(("hop", "m2"), ("hop", "m3"))
    send("m2", "m3")
    for name, leave in zip(("a0", "a1"), line.gate(group["a0"][1], group["a1"][1]), strict=True):
        group[name][1] = across(leave, CORE)
    table = make_table(0, blocks // 2)
    sums_of(("core", "a0"), ("core", "a1"))
    send("a0", "a1")
    more_table = make_table(blocks // 2, blocks)
    sums_of(("end", "m2"), ("end", "m3"), flops=0)
    home[1] = along(group["m2"][0], 1)
    home[3] = along(group["m3"][0], 3)
    flat = line.run(
        functools.partial(pack_kernel, count),
        "pack",
        [kept((SHARED + count * PART, width), F32)],
        [last_sums, mid_sums, table, more_table, *qkv_cols, *in_cols],
        scalar=place_ref,
        waits=[home[2]],
    )[0]
    sums_of(("hop", "a0"), ("hop", "a1"))
    send("a0", "a1")
    pause()
    mlp_home = come_home("home_mlp", home)
    mlp_side, mlp_deep = across(mlp_home, SIDE), across(mlp_home, DEEP)
    own_home, *leaving = line.run(
        functools.partial(leave_kernel, count),
        "leave",
        [kept((piece_rows + SENT, width), F32)] + [kept((piece_rows + SENT, width), BF16)] * (count - 1),
        [*group["a0"], *group["a1"], flat],
        scalar=place_ref,
    )
    came = [along(leaving[d - 1], d) for d in (2, 1, 3)]

    pause()
    mlp_side, mlp_deep = line.gate(mlp_side, mlp_deep)
    mlp_far = across(mlp_side, DEEP)

    def rows_first(values):
        values = line.gate(values)
        return values.reshape(pages, PAD, width)[:, :seq].transpose(1, 0, 2)

    layer_out, tokens_out = line.gate(rows_first(layer), rows_first(tok_grad), place=sent)
    pause(layer_out, tokens_out)
    attn_home = line.run(
        home_kernel, "home_attn", [kept((1, 1, piece_rows + SENT, width), BF16)], [own_home, *came]
    )[0]
    attn_home = rest_of_wide(attn_home)
    attn_came = [attn_home] + [across(attn_home, bit) for bit in (SIDE, DEEP, SIDE | DEEP)]
    mlp_four = stack("stack_mlp", [mlp_home, mlp_side, mlp_deep, mlp_far])
    mlp_other = across(mlp_four, CORE)
    pause()
    in_w_grad, down_w_grad = line.run(
        mlp_final_kernel,
        "mlp_final",
        [sent((width, width), F32)] * 2,
        [mlp_four, mlp_other],
        scalar=place_ref,
    )
    attn_four = stack("stack_attn_home", attn_came)
    attn_other = across(attn_four, CORE)
    qkv_w_grad, out_w_grad, total, table_grad = final_call(
        attend_final_kernel,
        "attend_final",
        [sent((3 * local, width), F32), sent((local, width), F32), kept((SENT, width), F32), sent((heads, bucket_count), F32)],
        place_ref,
        [attn_four, attn_other],
        line.token,
        scratch=[pltpu.VMEM((width, width), F32)],
    )

    return (
        layer_out.transpose(1, 0, 2),
        tokens_out.transpose(1, 0, 2),
        total[0],
        total[1],
        total[2],
        qkv_w_grad.reshape(3, local, width).transpose(2, 0, 1),
        total[9, :local],
        total[9, 2 * local : 3 * local],
        table_grad,
        out_w_grad,
        total[3],
        total[4],
        total[5],
        total[6],
        in_w_grad,
        total[10],
        down_w_grad,
        total[7],
        total[8],
    )


def solution(mesh):
    placed = (
        P(None, ("wide", "narrow"), None),
        P(None, ("wide", "narrow")),
        P(),
        P(),
        P(),
        P(),
        P(None, None, "narrow"),
        P("narrow"),
        P("narrow"),
        P("narrow", None),
        P("narrow", None),
        P(),
        P(),
        P(),
        P(),
        P(None, "narrow"),
        P("narrow"),
        P("narrow", None),
        P(),
        P(),
        P(None, ("wide", "narrow"), None),
    )
    return jax.shard_map(
        body,
        mesh=mesh,
        in_specs=placed,
        out_specs=(
            P(None, ("wide", "narrow"), None),
            P(None, ("wide", "narrow"), None),
            P(),
            P(),
            P(),
            P(None, None, "narrow"),
            P("narrow"),
            P("narrow"),
            P("narrow", None),
            P("narrow", None),
            P(),
            P(),
            P(),
            P(),
            P(None, "narrow"),
            P("narrow"),
            P("narrow", None),
            P(),
            P(),
        ),
        check_vma=False,
    )
```

```python
import functools

import jax
import jax.numpy as jnp
from jax import lax
from jax.experimental import pallas as pl
from jax.experimental.pallas import tpu as pltpu
from jax.sharding import PartitionSpec as P


SEQ = 197
PAD = 208
LANES = 256
EPSILON = 1e-06
ROOT_HALF = 0.7071067811865476
DENSITY = 0.3989422804014327
CORE, SIDE, DEEP = 1, 2, 4
PIECES = 8
LOW = 128
NEGATIVE = -1e30
FLOPS = 2 * 10**10
F32 = jnp.float32
BF16 = jnp.bfloat16

NN = (((1,), (0,)), ((), ()))
NT = (((1,), (1,)), ((), ()))
TN = (((0,), (0,)), ((), ()))


def mul(left, right, dims=NN):
    return lax.dot_general(left, right, dims, preferred_element_type=F32)


def vmem():
    return pl.BlockSpec(memory_space=pltpu.VMEM)


def anywhere():
    return pl.BlockSpec(memory_space=pl.ANY)


def scalars():
    return pl.BlockSpec(memory_space=pltpu.SMEM)


def near(values):
    return pltpu.with_memory_space_constraint(values, pltpu.VMEM)


def kept(shape, dtype):
    return pltpu.VMEM(shape, dtype)


def sent(shape, dtype):
    return jax.ShapeDtypeStruct(shape, dtype)


def call(kernel, name, outs, in_specs, out_specs=None, scratch=(), flops=FLOPS, limit=12, aliases=None):
    made = pl.pallas_call(
        kernel,
        out_shape=outs,
        in_specs=in_specs,
        out_specs=out_specs or [vmem()] * len(outs),
        scratch_shapes=list(scratch),
        input_output_aliases=aliases or {},
        compiler_params=pltpu.CompilerParams(vmem_limit_bytes=limit * 1024 * 1024),
        cost_estimate=pl.CostEstimate(flops=flops, bytes_accessed=0, transcendentals=0),
        name=name,
    )
    return lambda *arrays: made(
        *[near(a) if spec.memory_space == pltpu.VMEM else a for spec, a in zip(in_specs, arrays, strict=True)]
    )


class Line:
    def __init__(self):
        self.token = None

    def run(self, kernel, name, outs, arrays, scalar=None, waits=(), scratch=(), flops=FLOPS, limit=12):
        before = list(waits) + ([] if self.token is None else [self.token])
        start, n_in = (0 if scalar is None else 1), len(arrays)

        def whole(*refs):
            inputs = refs[: start + n_in]
            rest = refs[start + n_in + len(before) :]
            rest[len(outs)][...] = jnp.zeros((8, 128), F32)
            kernel(*inputs, *rest[: len(outs)], *rest[len(outs) + 1 :])

        made = call(
            whole,
            name,
            outs + [kept((8, 128), F32)],
            [scalars()] * start + [vmem()] * n_in + [anywhere()] * len(before),
            scratch=scratch,
            flops=flops,
            limit=limit,
        )(*([] if scalar is None else [scalar]), *arrays, *before)
        self.token = made[-1]
        return made[:-1]

    def gate(self, *arrays, waits=(), place=kept):
        n = len(arrays)
        made = call(
            lambda *refs: None,
            "gate",
            [place(a.shape, a.dtype) for a in arrays],
            [anywhere()] * (n + 1 + len(waits)),
            out_specs=[anywhere()] * n,
            aliases={i: i for i in range(n)},
            flops=0,
        )(*[near(a) if place is kept else a for a in arrays], self.token, *waits)
        return made[0] if n == 1 else made


class Jobs:
    def __init__(self, jobs):
        self.jobs = jobs

    def arrays(self):
        return [a for arrays, _, _ in self.jobs for a in arrays]

    def outs(self):
        made = []
        for arrays, counts, parts in self.jobs:
            _, mats, *rest = arrays[0].shape
            made += [kept((count, mats // parts, *rest), BF16) for count in counts for _ in range(parts)]
        return made

    def add(self, refs_in, refs_out):
        at_in = at_out = 0
        for arrays, counts, parts in self.jobs:
            sources = refs_in[at_in : at_in + len(arrays)]
            at_in += len(arrays)
            mats = arrays[0].shape[1] // parts
            first = 0
            for count in counts:
                for part in range(parts):
                    for i in range(count):
                        for j in range(mats):
                            at = (first + i, part * mats + j)
                            total = sources[0][at].astype(F32)
                            for source in sources[1:]:
                                total = total + source[at].astype(F32)
                            refs_out[at_out][i, j] = total.astype(BF16)
                    at_out += 1
                first += count

    def split(self, outs):
        made, at = [], 0
        for _, counts, parts in self.jobs:
            made.append(list(outs[at : at + len(counts) * parts]))
            at += len(counts) * parts
        return made


def final_call(kernel, name, outs, scalar, arrays, token, scratch=()):
    n_in = 1 + len(arrays)
    return call(
        lambda *refs: kernel(*refs[:n_in], *refs[n_in + 1 :]),
        name,
        outs,
        [scalars()] + [vmem()] * len(arrays) + [anywhere()],
        scratch=scratch,
    )(scalar, *arrays, token)


def norm_parts(values):
    center = values - jnp.mean(values, axis=-1, keepdims=True)
    spread = jnp.mean(center * center, axis=-1, keepdims=True)
    inverse = lax.rsqrt(spread + EPSILON)
    return center * inverse, inverse


def norm_back(grad, normed, inverse, gain):
    scaled = grad * gain
    inner = jnp.mean(scaled, axis=-1, keepdims=True)
    cross = jnp.mean(scaled * normed, axis=-1, keepdims=True)
    return inverse * (scaled - inner - normed * cross)


def col(values):
    return jnp.sum(values, axis=0, keepdims=True)


SMALL = 8
VECTORS = 5


TOKEN, FIRST_GAIN, FIRST_SHIFT, OUT_BIAS, ATTN_SCALE, SECOND_GAIN, SECOND_SHIFT, MLP_SCALE, DOWN_BIAS = range(9)


def row(ref, number):
    return ref[number : number + 1, :]


def first_kernel(tok_ref, mask_ref, vec_ref, out_ref):
    masked = jnp.where(mask_ref[...] > 0.0, row(vec_ref, TOKEN), tok_ref[...].astype(F32))
    normed, _ = norm_parts(masked)
    out = normed * row(vec_ref, FIRST_GAIN) + row(vec_ref, FIRST_SHIFT)
    rows = lax.broadcasted_iota(jnp.int32, (tok_ref.shape[0], 1), 0)
    real = lax.rem(rows, PAD) < SEQ
    out_ref[...] = jnp.where(real, out, 0.0).astype(BF16)


def bias_kernel(buckets_ref, small_ref, out_ref):
    heads = out_ref.shape[0]
    parts = small_ref.shape[1] // 128
    for half in range(2):
        lanes = pl.ds(half * 128, 128)
        index = buckets_ref[:, lanes]
        low = lax.bitwise_and(index, 127)
        high = lax.shift_right_logical(index, 7)
        column = lax.broadcasted_iota(jnp.int32, index.shape, 1) + half * 128
        for head in range(heads):
            total = jnp.full(index.shape, NEGATIVE, F32)
            for part in range(parts):
                values = small_ref[2 + head : 3 + head, part * 128 : (part + 1) * 128]
                values = jnp.broadcast_to(values, index.shape)
                found = jnp.take_along_axis(values, low, axis=1, mode="promise_in_bounds")
                total = jnp.where(high == part, found, total)
            out_ref[head, :, lanes] = jnp.where(column < SEQ, total, NEGATIVE)


def stack_kernel(*refs):
    for i, ref in enumerate(refs[:-1]):
        refs[-1][i] = ref[...]


def start_kernel(w_ref, small_ref, qkv_ref, out_ref, piece_ref, own_ref, sem):
    place = w_ref[0]
    rows = piece_ref.shape[0] - 2 * SMALL
    cut = qkv_ref.shape[0] // rows

    def bring(ref, number):
        copy = pltpu.make_async_copy(
            ref.at[pl.ds(pl.multiple_of(number * rows, rows), rows), :], own_ref, sem
        )
        copy.start()
        copy.wait()

    @pl.when(place < cut)
    def _():
        bring(qkv_ref, place)

    @pl.when(place >= cut)
    def _():
        bring(out_ref, place - cut)

    piece_ref[:rows, :] = own_ref[...]
    small = small_ref[:VECTORS, :]
    upper = small.astype(BF16).astype(F32)
    middle = (small - upper).astype(BF16).astype(F32)
    lower = small - upper - middle
    terms = jnp.concatenate([upper, middle, lower, jnp.zeros((1, small.shape[1]), F32)], axis=0)
    piece_ref[rows:, :] = terms.astype(BF16)


def arrive_kernel(count, *refs):
    came, zero_ref, smalls = refs[:count], refs[count], refs[count + 1 :]
    rows = zero_ref.shape[1]
    for i, ref in enumerate(came):
        zero_ref[i] = ref[:rows, :]
        terms = ref[rows:, :].astype(F32)
        smalls[i][...] = jnp.zeros_like(smalls[i])
        smalls[i][:VECTORS, :] = (
            terms[:VECTORS] + terms[VECTORS : 2 * VECTORS] + terms[2 * VECTORS : 3 * VECTORS]
        )


def cut_kernel(w_ref, in_ref, down_ref, four_ref, *own_refs):
    rows = four_ref.shape[1] // 2
    for k in range(four_ref.shape[0]):
        start = pl.multiple_of(lax.bitwise_xor(w_ref[0], 2 * k) * rows, rows)
        for i, ref in enumerate((in_ref, down_ref)):
            part = ref[pl.ds(start, rows), :]
            four_ref[k, i * rows : (i + 1) * rows, :] = part
            for own_ref in own_refs if k == 0 else ():
                own_ref[i * rows : (i + 1) * rows, :] = part


def put_together(w_ref, pair, slot, cut, target):
    rows = target.shape[0] // PIECES
    for piece in range(PIECES):
        start = pl.multiple_of(lax.bitwise_xor(w_ref[0], piece) * rows, rows)
        target[pl.ds(start, rows), :] = pair[piece & CORE][piece >> 1, slot, cut : cut + rows, :]


def take_apart(w_ref, mats, order, keep, send):
    for number, mat in enumerate(mats):
        rows = mat.shape[0] // PIECES
        for piece in range(PIECES):
            start = pl.multiple_of(lax.bitwise_xor(w_ref[0], piece) * rows, rows)
            target = send if piece & CORE else keep
            target[order[piece >> 1], number] = mat[pl.ds(start, rows), :]


def attend_kernel(slot, first, *refs):
    w_ref = refs[0]
    weights = refs[1:3]
    rest = refs[3:]
    x_ref, small_ref, bias_ref = rest[:3]
    rest = rest[3:]
    if not first:
        acc_in = rest[0]
        rest = rest[1:]
    acc_ref, qkv_ref, probs_ref, mixed_ref = rest[:4]
    if first:
        qkv_mat, out_mat = weights
        width = qkv_mat.shape[1]
        local = width // 4
    else:
        mat = rest[4]
        put_together(w_ref, weights, slot, 0, mat)
        width = mat.shape[0]
        local = width // 4
        qkv_mat, out_mat = mat.at[: 3 * local, :], mat.at[3 * local :, :]
    heads = bias_ref.shape[0]
    size = local // heads
    qkv = mul(x_ref[...], qkv_mat[...], NT)
    queries = qkv[:, :local] + small_ref[0:1, :local]
    queries = (queries.astype(BF16).astype(F32) * size ** (-0.5)).astype(BF16)
    keys = qkv[:, local : 2 * local].astype(BF16)
    values = qkv[:, 2 * local :] + small_ref[0:1, LANES : LANES + local]
    values = values.astype(BF16)
    qkv_ref[0] = queries
    qkv_ref[1] = keys
    qkv_ref[2] = values
    lane = lax.broadcasted_iota(jnp.int32, (PAD, local), 1)
    pages = x_ref.shape[0] // PAD
    zero = jnp.zeros((PAD, local), BF16)
    for page in range(pages):
        rows = slice(page * PAD, (page + 1) * PAD)
        q, k, v = queries[rows], keys[rows], values[rows]
        mixed = jnp.zeros((PAD, local), F32)
        for head in range(heads):
            own = (lane >= head * size) & (lane < (head + 1) * size)
            scores = mul(jnp.where(own, q, zero), k, NT) + bias_ref[head][:, :PAD]
            top = jnp.max(scores, axis=1, keepdims=True)
            power = jnp.exp(scores - top)
            total = jnp.sum(power, axis=1, keepdims=True)
            probs = (power * (1.0 / total)).astype(BF16)
            probs_ref[page * heads + head] = probs
            mixed = mixed + mul(probs, jnp.where(own, v, zero))
        mixed_ref[rows, :] = mixed.astype(BF16)
    out = mul(mixed_ref[...], out_mat[...])
    acc_ref[...] = out if first else acc_in[...] + out


def middle_kernel(acc_ref, tok_ref, mask_ref, grad_ref, vec_ref, mid_ref, x_ref, mg_ref):
    masked = jnp.where(mask_ref[...] > 0.0, row(vec_ref, TOKEN), tok_ref[...].astype(F32))
    middle = masked + row(vec_ref, ATTN_SCALE) * (acc_ref[...] + row(vec_ref, OUT_BIAS))
    mid_ref[...] = middle
    normed, _ = norm_parts(middle)
    x_ref[...] = (normed * row(vec_ref, SECOND_GAIN) + row(vec_ref, SECOND_SHIFT)).astype(BF16)
    mg_ref[...] = (grad_ref[...].astype(F32) * row(vec_ref, MLP_SCALE)).astype(BF16)


def mlp_kernel(first, order, jobs, *refs):
    w_ref = refs[0]
    weights = refs[1:3]
    rest = refs[3:]
    x_ref, mg_ref, small_ref = rest[:3]
    rest = rest[3:]
    if not first:
        out_in, grad_in = rest[:2]
        rest = rest[2:]
    n_jobs = len(jobs.arrays())
    jobs_in, rest = rest[:n_jobs], rest[n_jobs:]
    out_ref, grad_ref, col_ref, keep, send = rest[:5]
    rest = rest[5:]
    n_jobs = len(jobs.outs())
    jobs_out, rest = rest[:n_jobs], rest[n_jobs:]
    in_grad, down_grad = rest[:2]
    if first:
        in_mat, down_mat = weights
    else:
        in_mat, down_mat = rest[2:]
        put_together(w_ref, weights, 0, 0, in_mat)
        put_together(w_ref, weights, 0, in_mat.shape[0] // PIECES, down_mat)
    jobs.add(jobs_in, jobs_out)
    width = in_mat.shape[0]
    x = x_ref[...]
    mg = mg_ref[...]
    out = None
    back = None
    for start in range(0, width, 256):
        units = slice(start, start + 256)
        weight_in = in_mat[:, units]
        weight_down = down_mat[units, :]
        pre = mul(x, weight_in) + small_ref[1:2, units]
        phi = 0.5 * (1.0 + lax.erf(pre * ROOT_HALF))
        hidden = (pre * phi).astype(BF16)
        slope = phi + pre * (DENSITY * jnp.exp(-0.5 * pre * pre))
        part = mul(hidden, weight_down)
        out = part if out is None else out + part
        hidden_grad = mul(mg, weight_down, NT)
        pre_grad = hidden_grad * slope
        low = pre_grad.astype(BF16)
        col_ref[:, units] = col(low.astype(F32))
        part = mul(low, weight_in, NT)
        back = part if back is None else back + part
        down_grad[units, :] = mul(hidden, mg, TN).astype(BF16)
        in_grad[:, units] = mul(x, low, TN).astype(BF16)
    out_ref[...] = out if first else out_in[...] + out
    grad_ref[...] = back if first else grad_in[...] + back
    take_apart(w_ref, [in_grad, down_grad], order, keep, send)


def turn_kernel(jobs, *refs):
    mid_ref, out_ref, back_ref, grad_ref, acc_ref, vec_ref = refs[:6]
    refs = refs[6:]
    n_jobs = len(jobs.arrays())
    jobs_in, refs = refs[:n_jobs], refs[n_jobs:]
    layer_ref, mgrad_ref, ag_ref, sums_ref = refs[:4]
    jobs.add(jobs_in, refs[4:])
    middle = mid_ref[...]
    grad = grad_ref[...].astype(F32)
    mlp_out = out_ref[...] + row(vec_ref, DOWN_BIAS)
    layer_ref[...] = (middle + row(vec_ref, MLP_SCALE) * mlp_out).astype(BF16)
    normed, inverse = norm_parts(middle)
    second = back_ref[...]
    middle_grad = grad + norm_back(second, normed, inverse, row(vec_ref, SECOND_GAIN))
    mgrad_ref[...] = middle_grad
    scaled = middle_grad * row(vec_ref, ATTN_SCALE)
    ag_ref[...] = scaled.astype(BF16)
    sums_ref[0:1, :] = col(scaled)
    sums_ref[1:2, :] = col(middle_grad * (acc_ref[...] + row(vec_ref, OUT_BIAS)))
    sums_ref[2:3, :] = col(second * normed)
    sums_ref[3:4, :] = col(second)
    sums_ref[4:5, :] = col(grad * row(vec_ref, MLP_SCALE))
    sums_ref[5:6, :] = col(grad * mlp_out)
    sums_ref[6:8, :] = jnp.zeros_like(sums_ref[6:8, :])


def attend_back_kernel(own, first, order, second, jobs, *refs):
    w_ref = refs[0]
    if own:
        qkv_mat, out_mat = refs[1:3]
        rest = refs[3:]
    else:
        local = refs[1].shape[0] // 4
        qkv_mat, out_mat = refs[1].at[: 3 * local, :], refs[1].at[3 * local :, :]
        rest = refs[2:]
    x_ref, ag_ref, qkv_ref, probs_ref, mixed_ref = rest[:5]
    rest = rest[5:]
    if not first:
        grad_in = rest[0]
        rest = rest[1:]
    if second:
        other_grad = rest[0]
        rest = rest[1:]
    n_jobs = len(jobs.arrays())
    jobs_in, rest = rest[:n_jobs], rest[n_jobs:]
    grad_ref, col_ref, grid_ref = rest[:3]
    if second:
        keep, send = rest[3:5]
        rest = rest[5:]
    else:
        mat_grad = rest[3]
        rest = rest[4:]
    n_jobs = len(jobs.outs())
    jobs_out, rest = rest[:n_jobs], rest[n_jobs:]
    if second:
        mat_grad, dqkv = rest
    else:
        (dqkv,) = rest
    jobs.add(jobs_in, jobs_out)
    local = out_mat.shape[0]
    heads = grid_ref.shape[0]
    size = local // heads
    ag = ag_ref[...]
    mixed_grad = mul(ag, out_mat[...], NT).astype(BF16)
    mat_grad[3 * local :, :] = mul(mixed_ref[...], ag, TN).astype(BF16)
    lane = lax.broadcasted_iota(jnp.int32, (PAD, local), 1)
    pages = x_ref.shape[0] // PAD
    zero = jnp.zeros((PAD, local), BF16)
    for page in range(pages):
        rows = slice(page * PAD, (page + 1) * PAD)
        q, v, dm = qkv_ref[0, rows, :], qkv_ref[2, rows, :], mixed_grad[rows]
        k = (qkv_ref[1, rows, :].astype(F32) * size ** (-0.5)).astype(BF16)
        dq = jnp.zeros((PAD, local), F32)
        dk = jnp.zeros((PAD, local), F32)
        dv = jnp.zeros((PAD, local), F32)
        for head in range(heads):
            own = (lane >= head * size) & (lane < (head + 1) * size)
            dmh = jnp.where(own, dm, zero)
            probs_low = probs_ref[page * heads + head]
            probs = probs_low.astype(F32)
            weighed = probs * mul(dmh, v, NT)
            score = weighed - probs * jnp.sum(weighed, axis=1, keepdims=True)
            low = score.astype(BF16)
            if page == 0:
                grid_ref[head] = low.astype(F32)
            else:
                grid_ref[head] = grid_ref[head] + low.astype(F32)
            dq = dq + mul(low, jnp.where(own, k, zero))
            dk = dk + mul(low, jnp.where(own, q, zero), TN)
            dv = dv + mul(probs_low, dmh, TN)
        dqkv[rows, :] = jnp.concatenate([dq, dk, dv], axis=1).astype(BF16)
    grads = dqkv[...]
    mat_grad[: 3 * local, :] = mul(grads, x_ref[...], TN).astype(BF16)
    col_ref[...] = col(grads.astype(F32))
    back = mul(grads, qkv_mat[...])
    grad_ref[...] = back if first else grad_in[...] + back
    if second:
        take_apart(w_ref, [other_grad, mat_grad], order, keep, send)


def last_kernel(tok_ref, mask_ref, mgrad_ref, first_ref, vec_ref, grad_ref, sums_ref):
    mask = mask_ref[...] > 0.0
    masked = jnp.where(mask, row(vec_ref, TOKEN), tok_ref[...].astype(F32))
    normed, inverse = norm_parts(masked)
    first = first_ref[...]
    in_grad = mgrad_ref[...] + norm_back(first, normed, inverse, row(vec_ref, FIRST_GAIN))
    grad_ref[...] = jnp.where(mask, 0.0, in_grad).astype(BF16)
    sums_ref[0:1, :] = col(jnp.where(mask, in_grad, 0.0))
    sums_ref[1:2, :] = col(first * normed)
    sums_ref[2:3, :] = col(first)
    sums_ref[3:8, :] = jnp.zeros_like(sums_ref[3:8, :])


def table_kernel(grid_count, begin, end, *refs):
    buckets_ref = refs[0]
    grids = refs[1 : 1 + grid_count]
    out_ref = refs[1 + grid_count]
    heads = grids[0].shape[0]
    highs = out_ref.shape[0] // (grid_count * heads)
    out_ref[...] = jnp.zeros_like(out_ref)

    def step(block, _):
        base = pl.multiple_of(block * 8, 8)
        index = buckets_ref[pl.ds(base, 8), :][:, :PAD]
        loads = [[g[h, pl.ds(base, 8), :] for h in range(heads)] for g in grids]
        total = None
        for row in range(8):
            one = index[row : row + 1]
            low = lax.bitwise_and(one, LOW - 1)
            high = lax.shift_right_logical(one, LOW.bit_length() - 1)
            right = (
                jnp.broadcast_to(low, (LOW, PAD)) == lax.broadcasted_iota(jnp.int32, (LOW, PAD), 0)
            ).astype(F32).astype(BF16)
            match = jnp.broadcast_to(high, (highs, PAD)) == lax.broadcasted_iota(
                jnp.int32, (highs, PAD), 0
            )
            left = jnp.concatenate(
                [
                    jnp.where(match, jnp.broadcast_to(loads[g][h][row : row + 1], (highs, PAD)), 0.0)
                    for g in range(grid_count)
                    for h in range(heads)
                ],
                axis=0,
            ).astype(BF16)
            part = mul(left, right, NT)
            total = part if total is None else total + part
        out_ref[...] += total
        return 0

    lax.fori_loop(begin, end, step, 0)


def sum_kernel(jobs, *refs):
    n_in, n_out = len(jobs.arrays()), len(jobs.outs())
    jobs.add(refs[:n_in], refs[n_in : n_in + n_out])


SHARED = 16
PART = 8
SENT = 16


def pack_kernel(count, w_ref, last_ref, mid_ref, table_ref, table_more_ref, *refs):
    qkv_cols, in_cols, out_ref = refs[:count], refs[count : 2 * count], refs[2 * count]
    out_ref[...] = jnp.zeros_like(out_ref)
    out_ref[0:3, :] = last_ref[0:3, :]
    out_ref[3:9, :] = mid_ref[0:6, :]
    tables = table_ref.shape[0] // count
    parts = out_ref.shape[1] // LOW
    for d in range(count):
        base = SHARED + d * PART
        out_ref[base : base + 1, : qkv_cols[d].shape[1]] = qkv_cols[d][...]
        out_ref[base + 1 : base + 2, :] = in_cols[d][...]
        for k in range(tables):
            at = d * tables + k
            lanes = slice(k % parts * LOW, (k % parts + 1) * LOW)
            out_ref[base + 2 + k // parts : base + 3 + k // parts, lanes] = row(table_ref, at) + row(table_more_ref, at)
    held = out_ref[SHARED:, :]
    for d in range(count):
        shard = lax.rem(w_ref[1] + d, count)
        out_ref[pl.ds(pl.multiple_of(SHARED + shard * PART, 8), PART), :] = held[d * PART : (d + 1) * PART]


def leave_kernel(count, w_ref, stay_a, came_a, stay_b, came_b, flat_ref, *outs):
    rows = stay_a.shape[2]
    pairs = [(stay_b, came_b, 1), (stay_a, came_a, 0), (stay_a, came_a, 1), (stay_b, came_b, 0)]
    for d in range(count):
        stay, came, slot = pairs[d]
        total = stay[0, slot].astype(F32) + came[0, slot].astype(F32)
        shard = lax.rem(w_ref[1] + d, count)
        part = flat_ref[pl.ds(pl.multiple_of(SHARED + shard * PART, 8), PART), :]
        small = jnp.concatenate(
            [flat_ref[:9, :], part[:5], jnp.zeros((SENT - 14, part.shape[1]), F32)], axis=0
        )
        outs[d][:rows, :] = total.astype(outs[d].dtype)
        outs[d][rows:, :] = small.astype(outs[d].dtype)


def home_kernel(own_ref, *refs):
    came, done_ref = refs[:-1], refs[-1]
    total = own_ref[...]
    for ref in came:
        total = total + ref[...].astype(F32)
    done_ref[0, 0] = total.astype(BF16)


def assemble(w_ref, pair, number, place_in):
    rows = place_in.shape[0] // PIECES
    for piece in range(PIECES):
        start = pl.multiple_of(lax.bitwise_xor(w_ref[0], piece) * rows, rows)
        place_in[pl.ds(start, rows), :] = pair[piece & CORE][piece >> 1, 0, number, :rows, :].astype(F32)


def mlp_final_kernel(w_ref, own_ref, other_ref, in_ref, down_ref):
    assemble(w_ref, (own_ref, other_ref), 0, in_ref)
    assemble(w_ref, (own_ref, other_ref), 1, down_ref)


def attend_final_kernel(w_ref, own_ref, other_ref, qkv_ref, out_ref, small_ref, table_ref, whole):
    assemble(w_ref, (own_ref, other_ref), 0, whole)
    cut = qkv_ref.shape[0]
    qkv_ref[...] = whole[:cut, :]
    out_ref[...] = whole[cut:, :]
    rows = whole.shape[0] // PIECES
    total = jnp.zeros(small_ref.shape, F32)
    for ref in (own_ref, other_ref):
        for chip in range(ref.shape[0]):
            total = total + ref[chip, 0, 0, rows:, :].astype(F32)
    small_ref[...] = total
    table_ref[...] = total[11 : 11 + table_ref.shape[0], : table_ref.shape[1]]


SIDE_FIRST = (0, 2, 1, 3)
DEEP_FIRST = (0, 1, 2, 3)


def body(
    tokens,
    page_mask,
    buckets,
    mask_token,
    first_gain,
    first_shift,
    qkv_weight,
    query_bias,
    value_bias,
    position_bias,
    out_weight,
    out_bias,
    attn_scale,
    second_gain,
    second_shift,
    in_weight,
    in_bias,
    down_weight,
    down_bias,
    mlp_scale,
    out_grad,
):
    pages, seq, width = tokens.shape
    count = lax.axis_size("narrow")
    local = qkv_weight.shape[2]
    heads, bucket_count = position_bias.shape
    rows = pages * PAD
    piece_rows = width // PIECES
    place = lax.bitwise_and(lax.axis_index("wide").astype(jnp.int32), PIECES - 1)
    place_ref = jnp.stack([place, lax.axis_index("narrow").astype(jnp.int32)])
    wide_shape = (rows, width)
    line = Line()

    def across(values, bit):
        others = lax.axis_size("wide")
        return lax.ppermute(values, "wide", [(i, i ^ bit) for i in range(others)])

    def along(values, step):
        return lax.ppermute(values, "narrow", [(i, (i + step) % count) for i in range(count)])

    def rest_of_wide(values):
        bit = PIECES
        while bit < lax.axis_size("wide"):
            values = (values.astype(F32) + across(values, bit).astype(F32)).astype(values.dtype)
            bit *= 2
        return values

    def plane(values):
        values = line.gate(values)
        return [values] + [across(values, bit) for bit in (SIDE, DEEP, SIDE | DEEP)]

    def stack(name, arrays, waits=()):
        return line.run(
            stack_kernel, name, [kept((len(arrays),) + arrays[0].shape, BF16)], list(arrays), waits=waits
        )[0]

    vecs = jnp.stack(
        [
            mask_token,
            first_gain,
            first_shift,
            out_bias,
            attn_scale,
            second_gain,
            second_shift,
            mlp_scale,
            down_bias,
        ]
    )
    tables = jnp.pad(position_bias, ((0, SMALL - 2 - heads), (0, width - bucket_count)))
    spare = width - LANES - local
    shifts = jnp.pad(query_bias, (0, width - local)) + jnp.pad(value_bias, (LANES, spare))
    small = jnp.concatenate([shifts[None], in_bias[None], tables], axis=0)
    qkv_own = qkv_weight.transpose(1, 2, 0).reshape(3 * local, width)
    piece = call(
        start_kernel,
        "start",
        [kept((piece_rows + 2 * SMALL, width), BF16)],
        [scalars(), vmem(), anywhere(), anywhere()],
        scratch=[pltpu.VMEM((piece_rows, width), BF16), pltpu.SemaphoreType.DMA],
    )(place_ref, small, qkv_own, out_weight)[0]
    attn_came = [along(piece, -step) for step in range(1, count)]
    smalls = [small]

    fill = ((0, 0), (0, PAD - seq), (0, 0))
    tok = jnp.pad(tokens, fill).reshape(rows, width)
    grad = jnp.pad(out_grad, fill).reshape(rows, width)
    flags = (page_mask > 0) & (jnp.arange(seq, dtype=jnp.int32) % SEQ != 0)
    mask = jnp.pad(flags.astype(F32), ((0, 0), (0, PAD - seq))).reshape(rows, 1)
    index = jnp.pad(buckets, ((0, PAD - seq), (0, LANES - seq)))

    four_mlp, *own_mlp = line.run(
        cut_kernel,
        "cut",
        [kept((4, 2 * piece_rows, width), BF16)] + [kept((2 * piece_rows, width), BF16)] * (count - 2),
        [in_weight, down_weight],
        scalar=place_ref,
    )
    x_one = line.run(
        first_kernel,
        "first",
        [kept(wide_shape, BF16)],
        [tok, mask, vecs],
    )[0]
    biases = []

    def make_bias(d, waits=()):
        biases.append(
            line.run(
                bias_kernel, f"bias{d}", [kept((heads, PAD, LANES), F32)], [index, smalls[d]], waits=waits
            )[0]
        )

    make_bias(0)
    zones = {}
    attn_zero, *others = line.run(
        functools.partial(arrive_kernel, count - 1),
        "arrive",
        [kept((count - 1, piece_rows, width), BF16)] + [kept((SMALL, width), F32)] * (count - 1),
        attn_came,
    )
    smalls += others
    attn_came = plane(attn_zero)
    for step in range(1, count - 1):
        zones[step] = along(line.gate(own_mlp[step - 1]), -step)

    held = []

    def attend(d, acc, weights, waits=()):
        own = d == 0
        made = line.run(
            functools.partial(attend_kernel, d - 1, own),
            f"attend{d}",
            [
                kept(wide_shape, F32),
                kept((3, rows, local), BF16),
                kept((pages * heads, PAD, PAD), BF16),
                kept((rows, local), BF16),
            ]
            + ([] if own else [kept((width, width), BF16)]),
            [*weights, x_one, smalls[d], biases[d]] + ([] if own else [acc]),
            scalar=place_ref,
            waits=waits,
        )
        held.append((weights if own else [made[4]], *made[1:4]))
        return made[0]

    acc = attend(0, None, [qkv_own, out_weight])
    for d in range(1, count):
        make_bias(d)
    attn_four = stack("stack_attn", attn_came, [zones[step] for step in range(1, count - 1)])
    attn_other = across(attn_four, CORE)
    planes = {2: plane(zones[2][None])}
    zones[count - 1] = along(line.gate(four_mlp), -(count - 1))
    line.run(lambda *refs: None, "pause", [], [])
    for d in range(1, count):
        acc = attend(d, acc, [attn_four, attn_other])

    middle, x_two, mlp_grad = line.run(
        middle_kernel,
        "middle",
        [kept(wide_shape, F32), kept(wide_shape, BF16), kept(wide_shape, BF16)],
        [
            acc,
            tok,
            mask,
            grad,
            vecs,
        ],
    )

    group, bits = {}, {}

    def run_jobs(plan):
        jobs = []
        for step, name in plan:
            counts = {"core": (2, 2), "hop": (1, 1), "fan": (1, 1, 1, 1), "end": (1,)}[step]
            jobs.append((group[name], counts, 2 if step == "end" and name[0] == "a" else 1))
        jobs = Jobs(jobs)

        def store(outs):
            for (step, name), made in zip(plan, jobs.split(outs), strict=True):
                group[name] = made
                hops[name] = hops.get(name, 0) + 1

        return jobs, store

    hops = {}

    def send(*names, after=()):
        leaves = [group[name][1] for name in names]
        if after:
            leaves = line.gate(*leaves, waits=[group[name][1] for name in after])
        for name, leave in zip(names, leaves, strict=True):
            group[name] = [group[name][0], across(leave, bits[name][hops[name] - 1])]

    def sums_of(*plan, flops=FLOPS):
        jobs, store = run_jobs(plan)
        outs = line.run(
            functools.partial(sum_kernel, jobs),
            "sum_" + "_".join(step + name for step, name in plan),
            jobs.outs(),
            jobs.arrays(),
            flops=flops,
        )
        store(outs)

    def pause(*waits):
        line.run(lambda *refs: None, "pause", [], [], waits=waits)

    mlp_sums = []
    in_cols = [None] * count
    mlp_order = []

    def feed(d, weights, *plan):
        own = d == 0
        name = f"m{len(mlp_order)}"
        side_first = len(mlp_order) % 2 == 0
        mlp_order.append(d)
        bits[name] = (SIDE, DEEP) if side_first else (DEEP, SIDE)
        jobs, store = run_jobs(plan)
        outs = line.run(
            functools.partial(mlp_kernel, own, SIDE_FIRST if side_first else DEEP_FIRST, jobs),
            f"mlp{d}",
            [
                kept(wide_shape, F32),
                kept(wide_shape, F32),
                kept((1, width), F32),
                kept((4, 2, piece_rows, width), BF16),
                kept((4, 2, piece_rows, width), BF16),
            ]
            + jobs.outs(),
            [*weights, x_two, mlp_grad, smalls[d], *mlp_sums, *jobs.arrays()],
            scalar=place_ref,
            scratch=[pltpu.VMEM((width, width), BF16)] * (2 if own else 4),
        )
        mlp_sums[:] = outs[:2]
        in_cols[d] = outs[2]
        store(outs[5:])
        group[name] = [outs[3], across(outs[4], CORE)]

    full = {}
    full[2] = stack("stack2", planes[2])
    full[2] = [full[2], across(full[2], CORE)]
    planes[1] = plane(zones[1][None])
    feed(0, [in_weight, down_weight])
    pause(full[2][1])
    feed(2, full[2], ("core", "m0"))
    full[1] = stack("stack1", planes[1])
    full[1] = [full[1], across(full[1], CORE)]
    send("m0")
    sums_of(("core", "m1"))
    send("m1")
    last_zone = line.gate(zones[count - 1])[:, None]
    full[count - 1] = [last_zone, across(last_zone, CORE)]
    feed(1, full[1])
    feed(count - 1, full[count - 1])

    jobs, store = run_jobs([])
    layer, middle_grad, attn_grad, mid_sums, *outs = line.run(
        functools.partial(turn_kernel, jobs),
        "turn",
        [kept(wide_shape, BF16), kept(wide_shape, F32), kept(wide_shape, BF16), kept((8, width), F32)]
        + jobs.outs(),
        [
            middle,
            *mlp_sums,
            grad,
            acc,
            vecs,
            *jobs.arrays(),
        ],
    )
    store(outs)

    back_sum = []
    qkv_cols, grids = [None] * count, [None] * count
    back_order = []
    half = []

    def attend_back(d, *plan):
        second = len(half) == 1
        name = f"a{len(back_order) // 2}"
        side_first = name == "a0"
        first = not back_sum
        back_order.append(d)
        bits[name] = (SIDE, DEEP) if side_first else (DEEP, SIDE)
        jobs, store = run_jobs(plan)
        mats, *others = held[d]
        piece_arrays = [kept((4, 2, piece_rows, width), BF16)] * 2
        outs = line.run(
            functools.partial(attend_back_kernel, d == 0, first, SIDE_FIRST if side_first else DEEP_FIRST, second, jobs),
            f"attend_back{d}",
            [kept(wide_shape, F32), kept((1, 3 * local), F32), kept((heads, PAD, PAD), F32)]
            + (piece_arrays if second else [kept((width, width), BF16)])
            + jobs.outs(),
            [*mats, x_one, attn_grad, *others, *back_sum, *half, *jobs.arrays()],
            scalar=place_ref,
            scratch=[pltpu.VMEM((width, width), BF16)] * second + [pltpu.VMEM((rows, 3 * local), BF16)],
        )
        back_sum[:] = outs[:1]
        qkv_cols[d], grids[d] = outs[1:3]
        store(outs[5 if second else 4 :])
        if second:
            group[name] = [outs[3], outs[4]]
            half.clear()
        else:
            half.append(outs[3])

    pause(group["m0"][1], group["m1"][1])
    sums_of(("hop", "m0"), ("hop", "m1"), ("core", "m2"), ("core", "m3"))
    send("m0", "m1")
    send("m2", "m3")
    attend_back(1)
    attend_back(2)
    attend_back(3, ("end", "m0"), ("end", "m1"))
    home = {0: group["m0"][0], 2: along(group["m1"][0], 2)}
    attend_back(0)

    tok_grad, last_sums = line.run(
        last_kernel,
        "last",
        [kept(wide_shape, BF16), kept((8, width), F32)],
        [tok, mask, middle_grad, *back_sum, vecs],
    )
    highs = width // LOW
    blocks = -(-seq // 8)

    def make_table(begin, end):
        return line.run(
            functools.partial(table_kernel, count, begin, end),
            f"table{begin}",
            [kept((count * heads * highs, LOW), F32)],
            [index, *grids],
            flops=0,
        )[0]

    def come_home(name, pieces):
        jobs = Jobs([([pieces[d] for d in range(count)], (1,), 1)])
        done = line.run(functools.partial(sum_kernel, jobs), name, jobs.outs(), jobs.arrays())[0]
        return rest_of_wide(done)

    sums_of(("hop", "m2"), ("hop", "m3"))
    send("m2", "m3")
    for name, leave in zip(("a0", "a1"), line.gate(group["a0"][1], group["a1"][1]), strict=True):
        group[name][1] = across(leave, CORE)
    table = make_table(0, blocks // 2)
    sums_of(("core", "a0"), ("core", "a1"))
    send("a0", "a1")
    more_table = make_table(blocks // 2, blocks)
    sums_of(("end", "m2"), ("end", "m3"), flops=0)
    home[1] = along(group["m2"][0], 1)
    home[3] = along(group["m3"][0], 3)
    flat = line.run(
        functools.partial(pack_kernel, count),
        "pack",
        [kept((SHARED + count * PART, width), F32)],
        [last_sums, mid_sums, table, more_table, *qkv_cols, *in_cols],
        scalar=place_ref,
        waits=[home[2]],
    )[0]
    sums_of(("hop", "a0"), ("hop", "a1"))
    send("a0", "a1")
    pause()
    mlp_home = come_home("home_mlp", home)
    mlp_side, mlp_deep = across(mlp_home, SIDE), across(mlp_home, DEEP)
    own_home, *leaving = line.run(
        functools.partial(leave_kernel, count),
        "leave",
        [kept((piece_rows + SENT, width), F32)] + [kept((piece_rows + SENT, width), BF16)] * (count - 1),
        [*group["a0"], *group["a1"], flat],
        scalar=place_ref,
    )
    came = [along(leaving[d - 1], d) for d in (2, 1, 3)]

    pause()
    mlp_side, mlp_deep = line.gate(mlp_side, mlp_deep)
    mlp_far = across(mlp_side, DEEP)

    def rows_first(values):
        values = line.gate(values)
        return values.reshape(pages, PAD, width)[:, :seq].transpose(1, 0, 2)

    layer_out, tokens_out = line.gate(rows_first(layer), rows_first(tok_grad), place=sent)
    pause(layer_out, tokens_out)
    attn_home = line.run(
        home_kernel, "home_attn", [kept((1, 1, piece_rows + SENT, width), BF16)], [own_home, *came]
    )[0]
    attn_home = rest_of_wide(attn_home)
    attn_came = [attn_home] + [across(attn_home, bit) for bit in (SIDE, DEEP, SIDE | DEEP)]
    mlp_four = stack("stack_mlp", [mlp_home, mlp_side, mlp_deep, mlp_far])
    mlp_other = across(mlp_four, CORE)
    pause()
    in_w_grad, down_w_grad = line.run(
        mlp_final_kernel,
        "mlp_final",
        [sent((width, width), F32)] * 2,
        [mlp_four, mlp_other],
        scalar=place_ref,
    )
    attn_four = stack("stack_attn_home", attn_came)
    attn_other = across(attn_four, CORE)
    qkv_w_grad, out_w_grad, total, table_grad = final_call(
        attend_final_kernel,
        "attend_final",
        [sent((3 * local, width), F32), sent((local, width), F32), kept((SENT, width), F32), sent((heads, bucket_count), F32)],
        place_ref,
        [attn_four, attn_other],
        line.token,
        scratch=[pltpu.VMEM((width, width), F32)],
    )

    return (
        layer_out.transpose(1, 0, 2),
        tokens_out.transpose(1, 0, 2),
        total[0],
        total[1],
        total[2],
        qkv_w_grad.reshape(3, local, width).transpose(2, 0, 1),
        total[9, :local],
        total[9, 2 * local : 3 * local],
        table_grad,
        out_w_grad,
        total[3],
        total[4],
        total[5],
        total[6],
        in_w_grad,
        total[10],
        down_w_grad,
        total[7],
        total[8],
    )


def solution(mesh):
    placed = (
        P(None, ("wide", "narrow"), None),
        P(None, ("wide", "narrow")),
        P(),
        P(),
        P(),
        P(),
        P(None, None, "narrow"),
        P("narrow"),
        P("narrow"),
        P("narrow", None),
        P("narrow", None),
        P(),
        P(),
        P(),
        P(),
        P(None, "narrow"),
        P("narrow"),
        P("narrow", None),
        P(),
        P(),
        P(None, ("wide", "narrow"), None),
    )
    return jax.shard_map(
        body,
        mesh=mesh,
        in_specs=placed,
        out_specs=(
            P(None, ("wide", "narrow"), None),
            P(None, ("wide", "narrow"), None),
            P(),
            P(),
            P(),
            P(None, None, "narrow"),
            P("narrow"),
            P("narrow"),
            P("narrow", None),
            P("narrow", None),
            P(),
            P(),
            P(),
            P(),
            P(None, "narrow"),
            P("narrow"),
            P("narrow", None),
            P(),
            P(),
        ),
        check_vma=False,
    )
```
